32 devices in a mesh: ctx: 4 (over y, core), cand: 4 (over z), tp: 2 (over x).
Axes of the slice: x: 2, y: 2, z: 4, core: 2. Of those that a mesh axis runs over, the one named last changes fastest.
Arguments:
- prompt_q: bfloat16 [1024, 4096], P(('ctx', 'cand'), 'tp'), may hold values from -9 to 9
- prompt_kv: bfloat16 [2, 1024, 512], P(None, ('ctx', 'cand'), 'tp'), may hold values from -48 to 48, as said below
- cand_q: bfloat16 [4, 256, 4096], P('cand', 'ctx', 'tp'), may hold values from -9 to 9
- cand_kv: bfloat16 [2, 4, 256, 512], P(None, 'cand', 'ctx', 'tp'), may hold values from -48 to 48, as said below
- cand_lengths: int32 [4], P('cand'), may hold values from 64 to 256, as said below
- step_ends: int32 [4, 8], P('cand'), may hold values from 0 to 255, as said below
- reward_head: float32 [4096], P('tp'), may hold values from -0.09375 to 0.09375
Outputs:
- prompt_out: bfloat16 [1024, 4096], P(('ctx', 'cand'), 'tp')
- cand_out: bfloat16 [4, 256, 4096], P('cand', 'ctx', 'tp')
- step_logits: float32 [4, 8], P('cand')
The draws below stay inside these ranges and needn't reach their ends.
Inputs may be any that keep to these rules, and one draw needn't show every extreme that they name: `prompt_kv`: keys lie within -7 to 7. `cand_kv`: keys lie within -7 to 7. `cand_lengths`: at least one candidate uses all 256 positions. `step_ends`: for each candidate, 8 strictly increasing positions below its length, the last one equal to its length minus one.
All inputs are finite; a program needn't handle non-finite values.
Results may differ from the reference program's by a relative error of at most 0.0099.
Values may be sent and summed in bfloat16 or wider, within the bound.
No kernel may reach another device: no remote copies, remote signals or barrier semaphores. Data moves between devices by JAX's collectives and lax.ppermute only.
A program may use at most 192 MiB of HBM per device.

```python
import math
import jax
import jax.numpy as jnp
from jax import lax

HEADDIM = 128
QHEADS = 32
KVHEADS = 4
GROUP = 8
STEPS = 8
PROMPT = 1024
CLEN = 256
CANDS = 4


def shared_lengths(key):
    length_key = jax.random.fold_in(key, 500)
    key_one, key_two = jax.random.split(length_key)
    drawn_lengths = jax.random.randint(key_one, (CANDS,), CLEN // 4, CLEN + 1)
    longest = jax.random.randint(key_two, (), 0, CANDS)
    return jnp.where(jnp.arange(CANDS) == longest, CLEN, drawn_lengths).astype(jnp.int32)


def draw_prompt_q(key, part):
    key = jax.random.fold_in(key, 1)
    width = QHEADS * HEADDIM
    key_one = jax.random.fold_in(key, 0)
    values = jnp.clip(jax.random.normal(key_one, (PROMPT, width), jnp.float32), -6.0, 6.0)
    return values.astype(jnp.bfloat16)


def draw_cand_q(key, part):
    key = jax.random.fold_in(key, 3)
    width = QHEADS * HEADDIM
    row_count = CANDS * CLEN
    key_one = jax.random.fold_in(key, 0)
    values = jnp.clip(jax.random.normal(key_one, (row_count, width), jnp.float32), -6.0, 6.0)
    return values.reshape(CANDS, CLEN, width).astype(jnp.bfloat16)


def draw_prompt_kv(key, part):
    key = jax.random.fold_in(key, 2)
    width = KVHEADS * HEADDIM
    key_one = jax.random.fold_in(key, 0)
    key_four = jax.random.fold_in(key, 3)
    key_part = jnp.clip(jax.random.normal(key_one, (PROMPT, width), jnp.float32), -6.0, 6.0)
    value_part = jnp.clip(8.0 * jax.random.normal(key_four, (PROMPT, width), jnp.float32), -48.0, 48.0)
    return jnp.stack([key_part, value_part]).astype(jnp.bfloat16)


def draw_cand_kv(key, part):
    key = jax.random.fold_in(key, 4)
    width = KVHEADS * HEADDIM
    row_count = CANDS * CLEN
    key_one = jax.random.fold_in(key, 0)
    key_four = jax.random.fold_in(key, 3)
    key_part = jnp.clip(jax.random.normal(key_one, (row_count, width), jnp.float32), -6.0, 6.0)
    value_part = jnp.clip(8.0 * jax.random.normal(key_four, (row_count, width), jnp.float32), -48.0, 48.0)
    stacked = jnp.stack([key_part, value_part])
    return stacked.reshape(2, CANDS, CLEN, width).astype(jnp.bfloat16)


def draw_cand_lengths(key, part):
    return shared_lengths(key)


def draw_step_ends(key, part):
    lengths = shared_lengths(key)
    key = jax.random.fold_in(key, 6)
    step_index = jnp.arange(STEPS, dtype=jnp.int32)[None, :]
    spread = jnp.maximum(lengths // (2 * STEPS), 1)[:, None]
    wobble = jax.random.randint(key, (CANDS, STEPS), 0, 1 << 20) % spread
    wobble = jnp.where(step_index == STEPS - 1, 0, wobble)
    positions = (step_index + 1) * lengths[:, None] // STEPS - 1 - wobble
    return positions.astype(jnp.int32)


def steps_of(own_key, dims, cuts, low, high):
    def one(position, parts):
        draws = jax.random.uniform(jax.random.fold_in(jax.random.fold_in(own_key, 6), position), (parts,), jnp.float32, low / len(cuts), high / len(cuts))
        return jnp.repeat(jnp.exp(draws), dims[position] // parts).reshape((-1,) + (1,) * (len(dims) - position - 1))

    factor_of = one(*cuts[0])
    for cut in cuts[1:]:
        factor_of = factor_of * one(*cut)
    return factor_of


def scatter_about(rng, shape, scale, reach, cuts=(), kind=jnp.bfloat16):
    values = jax.random.normal(rng, shape, jnp.float32) * scale
    if len(cuts) > 0:
        values = steps_of(rng, shape, cuts, -0.22, 0.18) * values
    return jnp.clip(values, min=-reach, max=reach).astype(kind)


def setup_inputs(seed: int = 0) -> dict:
    keys = jax.random.split(jax.random.key(seed), 8)
    return {
        "prompt_q": draw_prompt_q(jax.random.fold_in(keys[7], 71), 0),
        "prompt_kv": draw_prompt_kv(jax.random.fold_in(keys[7], 71), 0),
        "cand_q": draw_cand_q(jax.random.fold_in(keys[7], 71), 0),
        "cand_kv": draw_cand_kv(jax.random.fold_in(keys[7], 71), 0),
        "cand_lengths": draw_cand_lengths(jax.random.fold_in(keys[7], 71), 0),
        "step_ends": draw_step_ends(jax.random.fold_in(keys[7], 71), 0),
        "reward_head": scatter_about(keys[6], (QHEADS * HEADDIM,), (QHEADS * HEADDIM) ** -0.5, 0.09375, ((0, 2),), jnp.float32),
    }


NEG_FILL = -1e30


def by_heads(flat_rows):
    row_count = flat_rows.shape[0]
    return flat_rows.astype(jnp.float32).reshape(row_count, KVHEADS, GROUP, HEADDIM)


def head_scores(queries, key_rows):
    key_heads = key_rows.astype(jnp.float32).reshape(key_rows.shape[0], KVHEADS, HEADDIM)
    return jnp.einsum('rhgd,nhd->hgrn', by_heads(queries), key_heads) * (HEADDIM ** -0.5)


def softmax_mix(sources):
    old_peak = None
    for scores, allowed, value_rows in sources:
        row_peak = jnp.max(jnp.where(allowed, scores, NEG_FILL), axis=-1)
        old_peak = row_peak if old_peak is None else jnp.maximum(old_peak, row_peak)
    totals = jnp.zeros(old_peak.shape, jnp.float32)
    blended = None
    for scores, allowed, value_rows in sources:
        weights = jnp.where(allowed, jnp.exp(scores - old_peak[..., None]), 0.0)
        totals = totals + jnp.sum(weights, axis=-1)
        rounded = lax.optimization_barrier(weights.astype(jnp.bfloat16)).astype(jnp.float32)
        value_heads = value_rows.astype(jnp.float32).reshape(value_rows.shape[0], KVHEADS, HEADDIM)
        contribution = jnp.einsum('hgrn,nhd->hgrd', rounded, value_heads)
        blended = contribution if blended is None else blended + contribution
    result = blended / totals[..., None]
    row_count = result.shape[2]
    return jnp.transpose(result, (2, 0, 1, 3)).reshape(row_count, QHEADS * HEADDIM)


def reference(prompt_q, prompt_kv, cand_q, cand_kv, cand_lengths, step_ends, reward_head):
    prompt_rows = math.gcd(PROMPT, 128)
    prompt_pos = jnp.arange(PROMPT, dtype=jnp.int32)

    def prompt_part(block_index):
        first_row = block_index * prompt_rows
        queries = lax.dynamic_slice_in_dim(prompt_q, first_row, prompt_rows, 0)
        query_pos = first_row + jnp.arange(prompt_rows, dtype=jnp.int32)
        allowed = prompt_pos[None, :] <= query_pos[:, None]
        scores = head_scores(queries, prompt_kv[0])
        return softmax_mix([(scores, allowed, prompt_kv[1])]).astype(jnp.bfloat16)

    prompt_out = lax.map(prompt_part, jnp.arange(PROMPT // prompt_rows, dtype=jnp.int32))
    prompt_out = prompt_out.reshape(PROMPT, QHEADS * HEADDIM)

    cand_rows = math.gcd(CLEN, 128)
    per_cand = CLEN // cand_rows
    flat_queries = cand_q.reshape(CANDS * CLEN, QHEADS * HEADDIM)
    own_pos = jnp.arange(CLEN, dtype=jnp.int32)
    every_key = jnp.ones((cand_rows, PROMPT), dtype=jnp.bool_)

    def cand_part(block_index):
        cand_index = block_index // per_cand
        first_row = (block_index % per_cand) * cand_rows
        queries = lax.dynamic_slice_in_dim(flat_queries, block_index * cand_rows, cand_rows, 0)
        row_pos = first_row + jnp.arange(cand_rows, dtype=jnp.int32)
        own_kv = lax.dynamic_index_in_dim(cand_kv, cand_index, 1, keepdims=False)
        sources = [(head_scores(queries, prompt_kv[0]), every_key, prompt_kv[1]),
                   (head_scores(queries, own_kv[0]), own_pos[None, :] <= row_pos[:, None], own_kv[1])]
        blended = softmax_mix(sources)
        alive_rows = row_pos < cand_lengths[cand_index]
        return jnp.where(alive_rows[:, None], blended, 0.0).astype(jnp.bfloat16)

    cand_out = lax.map(cand_part, jnp.arange(CANDS * per_cand, dtype=jnp.int32))
    cand_out = cand_out.reshape(CANDS, CLEN, QHEADS * HEADDIM)
    token_logit = jnp.dot(cand_out.reshape(CANDS * CLEN, QHEADS * HEADDIM).astype(jnp.float32), reward_head,
                          precision=lax.Precision.HIGHEST).reshape(CANDS, CLEN)
    step_logits = jnp.take_along_axis(token_logit, step_ends, axis=1)
    return prompt_out, cand_out, step_logits
```

```python
import functools
import math

import jax
import jax.numpy as jnp
from jax import lax
from jax.experimental import pallas as pl
from jax.experimental.pallas import tpu as pltpu
from jax.sharding import PartitionSpec as P

HEADDIM = 128
GROUP = 8
CORES = 2
NEG_FILL = -1e30
SCALE = HEADDIM ** -0.5 * math.log2(math.e)
ROW_TILE = 256
VMEM_LIMIT = 48 * 1024 * 1024


def shifted(block, axis, size, step):
    return lax.ppermute(block, axis, [(i, (i + step) % size) for i in range(size)])


def partner(block, axis, size):
    return lax.ppermute(block, axis, [(i, i ^ 1) for i in range(size)])


def gather_prompt(own, ctx_size, cand_size):
    along = [(own, 0)] + [(shifted(own, "cand", cand_size, k), k) for k in range(1, cand_size)]
    plane = [(b, 0, k) for b, k in along]
    for j in range(CORES, ctx_size, CORES):
        plane += [(shifted(b, "ctx", ctx_size, j), j, k) for b, k in along]
    blocks = [(b, j, 0, k) for b, j, k in plane]
    blocks += [(partner(b, "ctx", ctx_size), j, 1, k) for b, j, k in plane]
    return blocks


def gather_cand(own, ctx_size):
    blocks = [(own, 0, 0)]
    for j in range(CORES, ctx_size, CORES):
        blocks.append((shifted(own, "ctx", ctx_size, j), j, 0))
    return blocks + [(partner(b, "ctx", ctx_size), j, 1) for b, j, _ in blocks]


def owner_ctx(ctx_index, ctx_size, step, flip):
    side = ctx_index + flip - 2 * flip * lax.rem(ctx_index, 2)
    return lax.rem(side + ctx_size - step, ctx_size)


def key_positions(owners, rows):
    lane = lax.broadcasted_iota(jnp.int32, (1, len(owners) * rows), 1)
    positions = lane
    for index, owner in enumerate(owners):
        inside = (lane >= index * rows) & (lane < (index + 1) * rows)
        positions = jnp.where(inside, lane + (owner - index) * rows, positions)
    return positions


def mix(q_ref, sources, head, first_row):
    rows = q_ref.shape[0]
    columns = slice(head * HEADDIM, (head + 1) * HEADDIM)
    key_rows = jnp.concatenate([ref[0, :, columns] for refs, _ in sources for ref in refs], axis=0)
    value_rows = jnp.concatenate([ref[1, :, columns] for refs, _ in sources for ref in refs], axis=0)
    widened = jnp.concatenate([value_rows, jnp.ones_like(value_rows)], axis=1)
    fan = max(1, ROW_TILE // rows)
    for start in range(head * GROUP, (head + 1) * GROUP, fan):
        heads = range(start, start + fan)
        queries = jnp.concatenate([q_ref[:, h * HEADDIM : (h + 1) * HEADDIM] for h in heads], axis=0)
        scores = lax.dot_general(
            queries, key_rows, (((1,), (1,)), ((), ())), preferred_element_type=jnp.float32
        )
        row_pos = first_row + lax.rem(
            lax.broadcasted_iota(jnp.int32, (fan * rows, 1), 0), jnp.int32(rows)
        )
        parts = []
        offset = 0
        for refs, positions in sources:
            width = sum(ref.shape[1] for ref in refs)
            part = scores[:, offset : offset + width]
            if positions is not None:
                part = jnp.where(positions <= row_pos, part, NEG_FILL)
            parts.append(part)
            offset += width
        scores = jnp.concatenate(parts, axis=1)
        peak = jnp.max(scores, axis=1, keepdims=True)
        weights = jnp.exp2((scores - peak) * SCALE).astype(jnp.bfloat16)
        blended = jnp.dot(weights, widened, preferred_element_type=jnp.float32)
        result = blended[:, :HEADDIM] / blended[:, HEADDIM:]
        yield heads, result


def prompt_kernel(shifts, ctx_size, cand_size, q_ref, *refs):
    blocks, out_ref = refs[:-1], refs[-1]
    rows = q_ref.shape[0]
    ctx_index = lax.axis_index("ctx")
    cand_index = lax.axis_index("cand")
    owners = [
        owner_ctx(ctx_index, ctx_size, j, flip) * cand_size
        + lax.rem(cand_index + cand_size - k, cand_size)
        for j, flip, k in shifts
    ]
    positions = key_positions(owners, rows)
    first_row = (ctx_index * cand_size + cand_index) * rows
    for head in range(blocks[0].shape[2] // HEADDIM):
        for heads, result in mix(q_ref, [(blocks, positions)], head, first_row):
            for index, h in enumerate(heads):
                out_ref[:, h * HEADDIM : (h + 1) * HEADDIM] = result[
                    index * rows : (index + 1) * rows
                ].astype(jnp.bfloat16)


def cand_kernel(shifts, ctx_size, length_ref, q_ref, ends_ref, head_ref, *refs):
    own_count = len(shifts)
    own, prompt = refs[:own_count], refs[own_count:-2]
    out_ref, logit_ref = refs[-2:]
    rows = q_ref.shape[0]
    ctx_index = lax.axis_index("ctx")
    owners = [owner_ctx(ctx_index, ctx_size, j, flip) for j, flip in shifts]
    positions = key_positions(owners, rows)
    first_row = ctx_index * rows
    row_pos = first_row + lax.broadcasted_iota(jnp.int32, (rows, 1), 0)
    alive = row_pos < length_ref[0]
    total = jnp.zeros((rows, HEADDIM), jnp.float32)
    for head in range(own[0].shape[2] // HEADDIM):
        for heads, result in mix(q_ref, [(prompt, None), (own, positions)], head, first_row):
            for index, h in enumerate(heads):
                columns = slice(h * HEADDIM, (h + 1) * HEADDIM)
                kept = jnp.where(alive, result[index * rows : (index + 1) * rows], 0.0)
                kept = kept.astype(jnp.bfloat16)
                out_ref[:, columns] = kept
                total += kept.astype(jnp.float32) * head_ref[:, columns]
    logits = jnp.sum(total, axis=1, keepdims=True)
    hits = jnp.where(row_pos == ends_ref[...], logits, 0.0)
    logit_ref[...] = jnp.sum(hits, axis=0, keepdims=True)


def vmem(count):
    return [pl.BlockSpec(memory_space=pltpu.VMEM)] * count


def per_device(ctx_size, cand_size, prompt_q, prompt_kv, cand_q, cand_kv, cand_lengths, step_ends, reward_head):
    params = pltpu.CompilerParams(vmem_limit_bytes=VMEM_LIMIT)
    gathered = gather_prompt(prompt_kv, ctx_size, cand_size)
    own = gather_cand(cand_kv[:, 0], ctx_size)
    prompt_blocks = [b for b, *_ in gathered]
    own_blocks = [b for b, *_ in own]
    cand_out, partial = pl.pallas_call(
        functools.partial(cand_kernel, [s for _, *s in own], ctx_size),
        out_shape=(
            jax.ShapeDtypeStruct(cand_q.shape[1:], jnp.bfloat16),
            jax.ShapeDtypeStruct(step_ends.shape, jnp.float32),
        ),
        in_specs=[pl.BlockSpec(memory_space=pltpu.SMEM)] + vmem(3 + len(own_blocks) + len(prompt_blocks)),
        out_specs=tuple(vmem(2)),
        compiler_params=params,
        name="cand_attention",
    )(cand_lengths, cand_q[0], step_ends, reward_head[None], *own_blocks, *prompt_blocks)
    step_logits = lax.psum(partial, ("ctx", "tp"))
    prompt_out = pl.pallas_call(
        functools.partial(prompt_kernel, [s for _, *s in gathered], ctx_size, cand_size),
        out_shape=jax.ShapeDtypeStruct(prompt_q.shape, jnp.bfloat16),
        in_specs=vmem(1 + len(prompt_blocks)),
        out_specs=vmem(1)[0],
        compiler_params=params,
        name="prompt_attention",
    )(prompt_q, *prompt_blocks)
    return (prompt_out, cand_out[None], step_logits)


def solution(mesh):
    placed = (
        P(("ctx", "cand"), "tp"),
        P(None, ("ctx", "cand"), "tp"),
        P("cand", "ctx", "tp"),
        P(None, "cand", "ctx", "tp"),
        P("cand"),
        P("cand", None),
        P("tp"),
    )
    return jax.shard_map(
        functools.partial(per_device, mesh.shape["ctx"], mesh.shape["cand"]),
        mesh=mesh,
        in_specs=placed,
        out_specs=(P(("ctx", "cand"), "tp"), P("cand", "ctx", "tp"), P("cand", None)),
        check_vma=False,
    )
```

```python
import functools
import math

import jax
import jax.numpy as jnp
from jax import lax
from jax.experimental import pallas as pl
from jax.experimental.pallas import tpu as pltpu
from jax.sharding import PartitionSpec as P

HEADDIM = 128
GROUP = 8
NEG_FILL = -1e30
SCALE = HEADDIM ** -0.5 * math.log2(math.e)
ROW_TILE = 256
VMEM_LIMIT = 48 * 1024 * 1024


def flipped(block, axis, size, bit):
    return lax.ppermute(block, axis, [(i, i ^ bit) for i in range(size)])


def bits_of(size):
    return [1 << b for b in reversed(range(size.bit_length() - 1))]


def gather(own, axes, first=None):
    blocks = [(own, 0)]
    below = math.prod(size for _, size in axes)
    steps = []
    for axis, size in axes:
        below //= size
        steps.append([(axis, size, bit, bit * below) for bit in bits_of(size)])
    for axis, size, bit, mask in sum(reversed(steps), []):
        sent = blocks
        if first is not None:
            sent, first = [(first, 0)], None
        blocks += [(flipped(b, axis, size, bit), m | mask) for b, m in sent]
    return blocks


def key_positions(owners, rows):
    lane = lax.broadcasted_iota(jnp.int32, (1, len(owners) * rows), 1)
    positions = lane
    for index, owner in enumerate(owners):
        inside = (lane >= index * rows) & (lane < (index + 1) * rows)
        positions = jnp.where(inside, lane + (owner - index) * rows, positions)
    return positions


def mix(q_ref, sources, head, first_row):
    rows = q_ref.shape[0]
    columns = slice(head * HEADDIM, (head + 1) * HEADDIM)
    key_rows = jnp.concatenate([ref[0, :, columns] for refs, _ in sources for ref in refs], axis=0)
    value_rows = jnp.concatenate([ref[1, :, columns] for refs, _ in sources for ref in refs], axis=0)
    widened = jnp.concatenate([value_rows, jnp.ones_like(value_rows)], axis=1)
    fan = max(1, ROW_TILE // rows)
    for start in range(head * GROUP, (head + 1) * GROUP, fan):
        heads = range(start, start + fan)
        queries = jnp.concatenate([q_ref[:, h * HEADDIM : (h + 1) * HEADDIM] for h in heads], axis=0)
        scores = lax.dot_general(
            queries, key_rows, (((1,), (1,)), ((), ())), preferred_element_type=jnp.float32
        )
        row_pos = first_row + lax.rem(
            lax.broadcasted_iota(jnp.int32, (fan * rows, 1), 0), jnp.int32(rows)
        )
        parts = []
        offset = 0
        for refs, positions in sources:
            width = sum(ref.shape[1] for ref in refs)
            part = scores[:, offset : offset + width]
            if positions is not None:
                part = jnp.where(positions <= row_pos, part, NEG_FILL)
            parts.append(part)
            offset += width
        scores = jnp.concatenate(parts, axis=1)
        peak = jnp.max(scores, axis=1, keepdims=True)
        weights = jnp.exp2((scores - peak) * SCALE).astype(jnp.bfloat16)
        blended = jnp.dot(weights, widened, preferred_element_type=jnp.float32)
        result = blended[:, :HEADDIM] / blended[:, HEADDIM:]
        yield heads, result


def prompt_kernel(masks, cand_size, q_ref, *refs):
    blocks, out_ref = refs[:-1], refs[-1]
    rows = q_ref.shape[0]
    place = lax.axis_index("ctx") * cand_size + lax.axis_index("cand")
    positions = key_positions([place ^ mask for mask in masks], rows)
    first_row = place * rows
    for head in range(blocks[0].shape[2] // HEADDIM):
        for heads, result in mix(q_ref, [(blocks, positions)], head, first_row):
            for index, h in enumerate(heads):
                out_ref[:, h * HEADDIM : (h + 1) * HEADDIM] = result[
                    index * rows : (index + 1) * rows
                ].astype(jnp.bfloat16)


def cand_kernel(masks, lengths_ref, q_ref, ends_ref, head_ref, *refs):
    own_count = len(masks)
    own, prompt = refs[:own_count], refs[own_count:-2]
    out_ref, logit_ref = refs[-2:]
    rows = q_ref.shape[0]
    place = lax.axis_index("ctx")
    positions = key_positions([place ^ mask for mask in masks], rows)
    first_row = place * rows
    row_pos = first_row + lax.broadcasted_iota(jnp.int32, (rows, 1), 0)
    alive = row_pos < lengths_ref[:, :1]
    total = jnp.zeros((rows, HEADDIM), jnp.float32)
    for head in range(own[0].shape[2] // HEADDIM):
        for heads, result in mix(q_ref, [(prompt, None), (own, positions)], head, first_row):
            for index, h in enumerate(heads):
                columns = slice(h * HEADDIM, (h + 1) * HEADDIM)
                kept = jnp.where(alive, result[index * rows : (index + 1) * rows], 0.0)
                kept = kept.astype(jnp.bfloat16)
                out_ref[:, columns] = kept
                total += kept.astype(jnp.float32) * head_ref[:, columns]
    logits = jnp.sum(total, axis=1, keepdims=True)
    hits = jnp.where(row_pos == ends_ref[...], logits, 0.0)
    logit_ref[...] = jnp.sum(hits, axis=0, keepdims=True)


def vmem(count):
    return [pl.BlockSpec(memory_space=pltpu.VMEM)] * count


def stage_kernel(count, length_ref, *refs):
    sources, targets, lengths_ref, sems = refs[:count], refs[count : 2 * count], refs[-2], refs[-1]
    copies = [pltpu.make_async_copy(sources[i], targets[i], sems.at[i]) for i in range(count)]
    for copy in copies:
        copy.start()
    lengths_ref[...] = jnp.full(lengths_ref.shape, length_ref[0], jnp.int32)
    for copy in copies:
        copy.wait()


def staged(length, arrays, params):
    count = len(arrays)
    shapes = [jax.ShapeDtypeStruct(a.shape, a.dtype) for a in arrays]
    return pl.pallas_call(
        functools.partial(stage_kernel, count),
        out_shape=tuple(shapes) + (jax.ShapeDtypeStruct((1, HEADDIM), jnp.int32),),
        in_specs=[pl.BlockSpec(memory_space=pltpu.SMEM)] + [pl.BlockSpec(memory_space=pltpu.HBM)] * count,
        out_specs=tuple(vmem(count + 1)),
        scratch_shapes=[pltpu.SemaphoreType.DMA((count,))],
        compiler_params=params,
        name="stage_operands",
    )(length, *(pltpu.with_memory_space_constraint(a, pltpu.HBM) for a in arrays))


def per_device(ctx_size, cand_size, prompt_q, prompt_kv, cand_q, cand_kv, cand_lengths, step_ends, reward_head):
    params = pltpu.CompilerParams(vmem_limit_bytes=VMEM_LIMIT)
    prompt_rows, cand_rows, prompt_own, cand_own, ends, head, lengths = staged(
        cand_lengths,
        (prompt_q, cand_q[0], prompt_kv, cand_kv[:, 0], step_ends, reward_head[None]),
        params,
    )
    gathered = gather(prompt_own, [("ctx", ctx_size), ("cand", cand_size)], first=prompt_kv)
    own = gather(cand_own, [("ctx", ctx_size)])
    prompt_blocks = [b for b, _ in gathered]
    own_blocks = [b for b, _ in own]
    cand_out, partial = pl.pallas_call(
        functools.partial(cand_kernel, [mask for _, mask in own]),
        out_shape=(
            jax.ShapeDtypeStruct(cand_q.shape[1:], jnp.bfloat16),
            jax.ShapeDtypeStruct(step_ends.shape, jnp.float32),
        ),
        in_specs=vmem(4 + len(own_blocks) + len(prompt_blocks)),
        out_specs=tuple(vmem(2)),
        compiler_params=params,
        name="cand_attention",
    )(lengths, cand_rows, ends, head, *own_blocks, *prompt_blocks)
    sharers = ("ctx", "tp")
    share_count = lax.axis_size(sharers)
    shares = jnp.broadcast_to(partial[None], (share_count,) + partial.shape)
    step_logits = jnp.sum(lax.all_to_all(shares, sharers, 0, 0), axis=0)
    prompt_out = pl.pallas_call(
        functools.partial(prompt_kernel, [mask for _, mask in gathered], cand_size),
        out_shape=jax.ShapeDtypeStruct(prompt_q.shape, jnp.bfloat16),
        in_specs=vmem(1 + len(prompt_blocks)),
        out_specs=vmem(1)[0],
        compiler_params=params,
        name="prompt_attention",
    )(prompt_rows, *prompt_blocks)
    return (prompt_out, cand_out[None], step_logits)


def solution(mesh):
    placed = (
        P(("ctx", "cand"), "tp"),
        P(None, ("ctx", "cand"), "tp"),
        P("cand", "ctx", "tp"),
        P(None, "cand", "ctx", "tp"),
        P("cand"),
        P("cand", None),
        P("tp"),
    )
    return jax.shard_map(
        functools.partial(per_device, mesh.shape["ctx"], mesh.shape["cand"]),
        mesh=mesh,
        in_specs=placed,
        out_specs=(P(("ctx", "cand"), "tp"), P("cand", "ctx", "tp"), P("cand", None)),
        check_vma=False,
    )
```

```python
import functools
import math

import jax
import jax.numpy as jnp
from jax import lax
from jax.experimental import pallas as pl
from jax.experimental.pallas import tpu as pltpu
from jax.sharding import PartitionSpec as P

HEADDIM = 128
GROUP = 8
SUBLANES = 8
NEG_FILL = -1e30
SCALE = HEADDIM ** -0.5 * math.log2(math.e)
ROW_TILE = 256
VMEM_LIMIT = 48 * 1024 * 1024
PARAMS = pltpu.CompilerParams(vmem_limit_bytes=VMEM_LIMIT)
PROMPT_AXES = ("ctx", "cand")


def vmem(count):
    return [pl.BlockSpec(memory_space=pltpu.VMEM)] * count


def like(array):
    return jax.ShapeDtypeStruct(array.shape, array.dtype)


def high_bits(size, lowest):
    return [1 << b for b in reversed(range(size.bit_length() - 1)) if 1 << b >= lowest]


def flipped(block, axes, size, bit):
    return lax.ppermute(block, axes, [(i, i ^ bit) for i in range(size)])


def pack_kernel(*refs):
    sources, out_ref = refs[:-1], refs[-1]
    start = 0
    for ref in sources:
        out_ref[start : start + ref.shape[0]] = ref[...]
        start += ref.shape[0]


def packed(*arrays):
    count = sum(a.shape[0] for a in arrays)
    return pl.pallas_call(
        pack_kernel,
        out_shape=jax.ShapeDtypeStruct((count,) + arrays[0].shape[1:], arrays[0].dtype),
        in_specs=vmem(len(arrays)),
        out_specs=vmem(1)[0],
        compiler_params=PARAMS,
        name="pack_blocks",
    )(*arrays)


def prompt_bits(ctx_size, cand_size):
    core, along, across = cand_size, 1, 2 * cand_size
    early = high_bits(cand_size, 2) + [bit * cand_size for bit in high_bits(ctx_size, 4)]
    return early, along, across, core


def gather_prompt(first, own, ctx_size, cand_size):
    size = ctx_size * cand_size
    early, along, across, core = prompt_bits(ctx_size, cand_size)
    held = own[None]
    for bit in early:
        sent = held if first is None else first[None]
        first = None
        held = packed(held, flipped(sent, PROMPT_AXES, size, bit))

    def shared_out(block, even, odd):
        return lax.ppermute(
            block, PROMPT_AXES, [(i, i ^ (odd if i & core else even)) for i in range(size)]
        )

    second = shared_out(held, along, across)
    third = shared_out(held, across, along)
    fourth = shared_out(second, across, along)
    rail = [held, second, third, fourth]
    return rail + [flipped(block, PROMPT_AXES, size, core) for block in rail]


def prompt_owners(ctx_size, cand_size):
    early, along, across, core = prompt_bits(ctx_size, cand_size)
    place = lax.axis_index("ctx") * cand_size + lax.axis_index("cand")
    odd = lax.rem(lax.axis_index("ctx"), 2)
    near = along + odd * (across - along)
    far = along + across - near
    masks = [0]
    for bit in early:
        masks += [mask ^ bit for mask in masks]
    shifts = [0, near, far, along + across, core, core + far, core + near, core + along + across]
    return [[place ^ mask ^ shift for mask in masks] for shift in shifts]


def gather_cand(own, ctx_size):
    blocks = [(own, 0)]
    for bit in high_bits(ctx_size, 2) + [1]:
        blocks += [(flipped(b, "ctx", ctx_size, bit), mask | bit) for b, mask in blocks]
    return blocks


def stage_kernel(length_ref, prompt_q, cand_q, prompt_kv, cand_kv, ends, head, *refs):
    q_out, cand_out, kv_out, pay_out, ends_out, head_out, length_out, sems = refs
    steps = ends.shape[1]
    pairs = [
        (cand_q, cand_out),
        (ends, ends_out),
        (cand_kv, pay_out.at[0:2]),
        (prompt_kv, kv_out),
        (prompt_q, q_out),
        (head, head_out),
    ]
    copies = [pltpu.make_async_copy(a, b, sems.at[i]) for i, (a, b) in enumerate(pairs)]
    for copy in copies:
        copy.start()
    length_out[...] = jnp.full(length_out.shape, length_ref[0], jnp.int32)
    copies[0].wait()
    copies[1].wait()
    rows = cand_out.shape[0]
    ends_column = column_of(ends_out[...])
    row_pos = lax.axis_index("ctx") * rows + lax.broadcasted_iota(jnp.int32, (steps, rows), 1)
    chosen = (row_pos == ends_column).astype(jnp.bfloat16)
    picked = jnp.dot(chosen, cand_out[...], preferred_element_type=jnp.float32)
    width = pay_out.shape[2]
    pieces = [picked[:, at : at + width] for at in range(0, picked.shape[1], width)]
    pay_out[2] = jnp.concatenate(pieces, axis=0).astype(jnp.bfloat16)
    for copy in copies[2:]:
        copy.wait()


def column_of(row):
    count = row.shape[1]
    down = lax.broadcasted_iota(jnp.int32, (count, count), 0)
    right = lax.broadcasted_iota(jnp.int32, (count, count), 1)
    return jnp.sum(jnp.where(down == right, row, 0), axis=1, keepdims=True)


def staged(length, prompt_q, cand_q, prompt_kv, cand_kv, ends, head):
    arrays = (prompt_q, cand_q, prompt_kv, cand_kv, ends, head)
    payload = jax.ShapeDtypeStruct((3,) + cand_kv.shape[1:], cand_kv.dtype)
    lengths = jax.ShapeDtypeStruct((1, HEADDIM), jnp.int32)
    return pl.pallas_call(
        stage_kernel,
        out_shape=(like(prompt_q), like(cand_q), like(prompt_kv), payload, like(ends), like(head), lengths),
        in_specs=[pl.BlockSpec(memory_space=pltpu.SMEM)]
        + [pl.BlockSpec(memory_space=pltpu.HBM)] * len(arrays),
        out_specs=tuple(vmem(7)),
        scratch_shapes=[pltpu.SemaphoreType.DMA((len(arrays),))],
        compiler_params=PARAMS,
        name="stage_operands",
    )(length, *(pltpu.with_memory_space_constraint(a, pltpu.HBM) for a in arrays))


def blend(queries, key_rows, widened, key_pos, row_pos, free):
    scores = lax.dot_general(
        queries, key_rows, (((1,), (1,)), ((), ())), preferred_element_type=jnp.float32
    )
    bound = jnp.where(key_pos <= row_pos, scores[:, free:], NEG_FILL)
    scores = bound if free == 0 else jnp.concatenate([scores[:, :free], bound], axis=1)
    peak = jnp.max(scores, axis=1, keepdims=True)
    weights = jnp.exp2((scores - peak) * SCALE).astype(jnp.bfloat16)
    blended = jnp.dot(weights, widened, preferred_element_type=jnp.float32)
    return blended[:, :HEADDIM] / blended[:, HEADDIM:]


def head_operands(kv_ref, count, head):
    columns = slice(head * HEADDIM, (head + 1) * HEADDIM)
    key_rows = kv_ref[0, :count, columns]
    value_rows = kv_ref[1, :count, columns]
    return key_rows, jnp.concatenate([value_rows, jnp.ones_like(value_rows)], axis=1)


def tiles(q_ref, head):
    fan = max(1, ROW_TILE // q_ref.shape[0])
    for start in range(head * GROUP, (head + 1) * GROUP, fan):
        heads = range(start, start + fan)
        yield heads, jnp.concatenate([q_ref[:, h * HEADDIM : (h + 1) * HEADDIM] for h in heads], axis=0)


def stacked_rows(first_row, rows, count):
    return first_row + lax.rem(lax.broadcasted_iota(jnp.int32, (count, 1), 0), jnp.int32(rows))


def prompt_kernel(cand_size, q_ref, kv_ref, out_ref):
    rows = q_ref.shape[0]
    count = rows * lax.axis_size(PROMPT_AXES)
    first_row = (lax.axis_index("ctx") * cand_size + lax.axis_index("cand")) * rows
    key_pos = lax.broadcasted_iota(jnp.int32, (1, count), 1)
    for head in range(kv_ref.shape[2] // HEADDIM):
        key_rows, widened = head_operands(kv_ref, count, head)
        for heads, queries in tiles(q_ref, head):
            row_pos = stacked_rows(first_row, rows, queries.shape[0])
            result = blend(queries, key_rows, widened, key_pos, row_pos, 0)
            for index, h in enumerate(heads):
                out_ref[:, h * HEADDIM : (h + 1) * HEADDIM] = result[
                    index * rows : (index + 1) * rows
                ].astype(jnp.bfloat16)


def cand_kernel(masks, ctx_size, cand_size, q_ref, ends_ref, head_ref, lengths_ref, *refs):
    pays, blocks = refs[: len(masks)], refs[len(masks) : -3]
    out_ref, logit_ref, kv_ref = refs[-3:]
    rows = q_ref.shape[0]
    free = rows * ctx_size * cand_size
    place = lax.axis_index("ctx")
    for ref, owners in zip(blocks, prompt_owners(ctx_size, cand_size)):
        for index, owner in enumerate(owners):
            at = pl.ds(pl.multiple_of(owner * rows, rows), rows)
            kv_ref[0, at, :] = ref[index, 0]
            kv_ref[1, at, :] = ref[index, 1]
    picked = jnp.zeros(pays[0].shape[1:], jnp.float32)
    for ref, mask in zip(pays, masks):
        at = pl.ds(pl.multiple_of(free + (place ^ mask) * rows, rows), rows)
        kv_ref[0, at, :] = ref[0]
        kv_ref[1, at, :] = ref[1]
        picked += ref[2].astype(jnp.float32)
    steps = ends_ref.shape[1]
    width = picked.shape[1]
    step_rows = [picked[at : at + steps] for at in range(0, steps * q_ref.shape[1] // width, steps)]

    count = free + rows * len(masks)
    key_pos = lax.broadcasted_iota(jnp.int32, (1, rows * len(masks)), 1)
    first_row = place * rows
    length = lengths_ref[:, :1]
    alive = stacked_rows(first_row, rows, rows) < length
    ends = column_of(ends_ref[...])
    total = jnp.zeros((steps, HEADDIM), jnp.float32)
    for head in range(kv_ref.shape[2] // HEADDIM):
        key_rows, widened = head_operands(kv_ref, count, head)
        for heads, queries in tiles(q_ref, head):
            row_pos = stacked_rows(first_row, rows, queries.shape[0])
            result = blend(queries, key_rows, widened, key_pos, row_pos, free)
            for index, h in enumerate(heads):
                kept = jnp.where(alive, result[index * rows : (index + 1) * rows], 0.0)
                out_ref[:, h * HEADDIM : (h + 1) * HEADDIM] = kept.astype(jnp.bfloat16)
        heads = range(head * GROUP, (head + 1) * GROUP)
        offsets = [divmod(h * HEADDIM, width) for h in heads]
        queries = jnp.concatenate([step_rows[a][:, b : b + HEADDIM] for a, b in offsets], axis=0)
        row_pos = jnp.concatenate([ends] * GROUP, axis=0)
        result = blend(queries.astype(jnp.bfloat16), key_rows, widened, key_pos, row_pos, free)
        for index, h in enumerate(heads):
            kept = jnp.where(ends < length, result[index * steps : (index + 1) * steps], 0.0)
            kept = kept.astype(jnp.bfloat16).astype(jnp.float32)
            total += kept * head_ref[:, h * HEADDIM : (h + 1) * HEADDIM]
    logits = jnp.sum(total, axis=1, keepdims=True)
    down = lax.broadcasted_iota(jnp.int32, (steps, steps), 0)
    right = lax.broadcasted_iota(jnp.int32, (steps, steps), 1)
    logit_ref[...] = jnp.sum(jnp.where(down == right, logits, 0.0), axis=0, keepdims=True)


def per_device(ctx_size, cand_size, prompt_q, prompt_kv, cand_q, cand_kv, cand_lengths, step_ends, reward_head):
    q_rows, cand_rows, own, payload, ends, head, lengths = staged(
        cand_lengths, prompt_q, cand_q[0], prompt_kv, cand_kv[:, 0], step_ends, reward_head[None]
    )
    blocks = gather_prompt(prompt_kv, own, ctx_size, cand_size)
    pays = gather_cand(payload, ctx_size)
    key_count = q_rows.shape[0] * ctx_size * cand_size + cand_rows.shape[0] * ctx_size
    cand_out, partial, arranged = pl.pallas_call(
        functools.partial(cand_kernel, [mask for _, mask in pays], ctx_size, cand_size),
        out_shape=(
            like(cand_rows),
            jax.ShapeDtypeStruct(step_ends.shape, jnp.float32),
            jax.ShapeDtypeStruct((2, key_count, own.shape[2]), own.dtype),
        ),
        in_specs=vmem(4 + len(pays) + len(blocks)),
        out_specs=tuple(vmem(3)),
        compiler_params=PARAMS,
        name="cand_attention",
    )(cand_rows, ends, head, lengths, *(b for b, _ in pays), *blocks)
    step_logits = partial
    tp_size = lax.axis_size("tp")
    for bit in high_bits(tp_size, 1):
        step_logits = step_logits + flipped(step_logits, "tp", tp_size, bit)
    prompt_out = pl.pallas_call(
        functools.partial(prompt_kernel, cand_size),
        out_shape=like(prompt_q),
        in_specs=vmem(2),
        out_specs=vmem(1)[0],
        compiler_params=PARAMS,
        name="prompt_attention",
    )(q_rows, arranged)
    return (prompt_out, cand_out[None], step_logits)


def solution(mesh):
    placed = (
        P(("ctx", "cand"), "tp"),
        P(None, ("ctx", "cand"), "tp"),
        P("cand", "ctx", "tp"),
        P(None, "cand", "ctx", "tp"),
        P("cand"),
        P("cand", None),
        P("tp"),
    )
    return jax.shard_map(
        functools.partial(per_device, mesh.shape["ctx"], mesh.shape["cand"]),
        mesh=mesh,
        in_specs=placed,
        out_specs=(P(("ctx", "cand"), "tp"), P("cand", "ctx", "tp"), P("cand", None)),
        check_vma=False,
    )
```

```python
import functools
import math

import jax
import jax.numpy as jnp
from jax import lax
from jax.experimental import pallas as pl
from jax.experimental.pallas import tpu as pltpu
from jax.sharding import PartitionSpec as P

HEADDIM = 128
GROUP = 8
SUBLANES = 8
NEG_FILL = -1e30
SCALE = HEADDIM ** -0.5 * math.log2(math.e)
ROW_TILE = 256
VMEM_LIMIT = 48 * 1024 * 1024
PARAMS = pltpu.CompilerParams(vmem_limit_bytes=VMEM_LIMIT)
PROMPT_AXES = ("ctx", "cand")


def vmem(count):
    return [pl.BlockSpec(memory_space=pltpu.VMEM)] * count


def like(array):
    return jax.ShapeDtypeStruct(array.shape, array.dtype)


def high_bits(size, lowest):
    return [1 << b for b in reversed(range(size.bit_length() - 1)) if 1 << b >= lowest]


def flipped(block, axes, size, bit):
    return lax.ppermute(block, axes, [(i, i ^ bit) for i in range(size)])


def pack_kernel(count, *refs):
    sources, out_ref = refs[:count], refs[-1]
    start = 0
    for ref in sources:
        out_ref[start : start + ref.shape[0]] = ref[...]
        start += ref.shape[0]


def packed(*arrays, after=()):
    count = sum(a.shape[0] for a in arrays)
    return pl.pallas_call(
        functools.partial(pack_kernel, len(arrays)),
        out_shape=jax.ShapeDtypeStruct((count,) + arrays[0].shape[1:], arrays[0].dtype),
        in_specs=vmem(len(arrays)) + [pl.BlockSpec(memory_space=pl.ANY)] * len(after),
        out_specs=vmem(1)[0],
        compiler_params=PARAMS,
        name="pack_blocks",
    )(*arrays, *after)


def prompt_bits(ctx_size, cand_size):
    core, along, across = cand_size, 1, 2 * cand_size
    early = high_bits(cand_size, 2) + [bit * cand_size for bit in high_bits(ctx_size, 4)]
    return early, along, across, core


def gather_prompt(first, own, pays, ctx_size, cand_size):
    size = ctx_size * cand_size
    early, along, across, core = prompt_bits(ctx_size, cand_size)
    held = own[None]
    for bit in early:
        sent = held if first is None else first[None]
        first = None
        parts = held, flipped(sent, PROMPT_AXES, size, bit)
        held = packed(*parts)

    def shared_out(block, even, odd):
        return lax.ppermute(
            block, PROMPT_AXES, [(i, i ^ (odd if i & core else even)) for i in range(size)]
        )

    second = shared_out(held, along, across)
    third = shared_out(held, across, along)
    fourth = shared_out(packed(second, after=pays[1:4]), across, along)
    rail = [held, second, third, fourth]
    return rail + [flipped(block, PROMPT_AXES, size, core) for block in rail]


def prompt_owners(ctx_size, cand_size):
    early, along, across, core = prompt_bits(ctx_size, cand_size)
    place = lax.axis_index("ctx") * cand_size + lax.axis_index("cand")
    odd = lax.rem(lax.axis_index("ctx"), 2)
    near = along + odd * (across - along)
    far = along + across - near
    masks = [0]
    for bit in early:
        masks += [mask ^ bit for mask in masks]
    shifts = [0, near, far, along + across, core, core + far, core + near, core + along + across]
    return [[place ^ mask ^ shift for mask in masks] for shift in shifts]


def gather_cand(own, ctx_size):
    blocks = [(own, 0), (flipped(own, "ctx", ctx_size, 1), 1)]
    for bit in reversed(high_bits(ctx_size, 2)):
        rail = [(flipped(b, "ctx", ctx_size, bit), mask | bit) for b, mask in blocks if not mask & 1]
        blocks += rail + [(flipped(b, "ctx", ctx_size, 1), mask | 1) for b, mask in rail]
    return blocks


def stage_kernel(length_ref, prompt_q, cand_q, prompt_kv, cand_kv, ends, head, *refs):
    q_out, cand_out, kv_out, pay_out, ends_out, head_out, length_out, length_here, sems = refs
    steps = ends.shape[1]
    pairs = [
        (cand_q, cand_out),
        (ends, ends_out),
        (cand_kv, pay_out.at[0:2]),
        (prompt_kv, kv_out),
        (prompt_q, q_out),
        (head, head_out),
        (length_ref, length_here),
    ]
    copies = [pltpu.make_async_copy(a, b, sems.at[i]) for i, (a, b) in enumerate(pairs)]
    for copy in copies:
        copy.start()
    copies[0].wait()
    copies[1].wait()
    rows = cand_out.shape[0]
    ends_column = column_of(ends_out[...])
    row_pos = lax.axis_index("ctx") * rows + lax.broadcasted_iota(jnp.int32, (steps, rows), 1)
    chosen = (row_pos == ends_column).astype(jnp.bfloat16)
    picked = jnp.dot(chosen, cand_out[...], preferred_element_type=jnp.float32)
    width = pay_out.shape[2]
    pieces = [picked[:, at : at + width] for at in range(0, picked.shape[1], width)]
    pay_out[2] = jnp.concatenate(pieces, axis=0).astype(jnp.bfloat16)
    for copy in copies[2:]:
        copy.wait()
    length_out[...] = jnp.full(length_out.shape, length_here[0], jnp.int32)


def column_of(row):
    count = row.shape[1]
    down = lax.broadcasted_iota(jnp.int32, (count, count), 0)
    right = lax.broadcasted_iota(jnp.int32, (count, count), 1)
    return jnp.sum(jnp.where(down == right, row, 0), axis=1, keepdims=True)


def staged(length, prompt_q, cand_q, prompt_kv, cand_kv, ends, head):
    arrays = (prompt_q, cand_q, prompt_kv, cand_kv, ends, head)
    payload = jax.ShapeDtypeStruct((3,) + cand_kv.shape[1:], cand_kv.dtype)
    lengths = jax.ShapeDtypeStruct((1, HEADDIM), jnp.int32)
    return pl.pallas_call(
        stage_kernel,
        out_shape=(like(prompt_q), like(cand_q), like(prompt_kv), payload, like(ends), like(head), lengths),
        in_specs=[pl.BlockSpec(memory_space=pl.ANY)]
        + [pl.BlockSpec(memory_space=pltpu.HBM)] * len(arrays),
        out_specs=tuple(vmem(7)),
        scratch_shapes=[pltpu.SMEM((1,), jnp.int32), pltpu.SemaphoreType.DMA((len(arrays) + 1,))],
        compiler_params=PARAMS,
        name="stage_operands",
    )(length, *(pltpu.with_memory_space_constraint(a, pltpu.HBM) for a in arrays))


def blend(queries, key_rows, widened, key_pos, row_pos, free):
    scores = lax.dot_general(
        queries, key_rows, (((1,), (1,)), ((), ())), preferred_element_type=jnp.float32
    )
    bound = jnp.where(key_pos <= row_pos, scores[:, free:], NEG_FILL)
    scores = bound if free == 0 else jnp.concatenate([scores[:, :free], bound], axis=1)
    peak = jnp.max(scores, axis=1, keepdims=True)
    weights = jnp.exp2((scores - peak) * SCALE).astype(jnp.bfloat16)
    blended = jnp.dot(weights, widened, preferred_element_type=jnp.float32)
    return blended[:, :HEADDIM] / blended[:, HEADDIM:]


def head_operands(kv_ref, count, head):
    columns = slice(head * HEADDIM, (head + 1) * HEADDIM)
    key_rows = kv_ref[0, :count, columns]
    value_rows = kv_ref[1, :count, columns]
    return key_rows, jnp.concatenate([value_rows, jnp.ones_like(value_rows)], axis=1)


def tiles(q_ref, head):
    fan = max(1, ROW_TILE // q_ref.shape[0])
    for start in range(head * GROUP, (head + 1) * GROUP, fan):
        heads = range(start, start + fan)
        yield heads, jnp.concatenate([q_ref[:, h * HEADDIM : (h + 1) * HEADDIM] for h in heads], axis=0)


def stacked_rows(first_row, rows, count):
    return first_row + lax.rem(lax.broadcasted_iota(jnp.int32, (count, 1), 0), jnp.int32(rows))


def prompt_kernel(cand_size, q_ref, kv_ref, out_ref):
    rows = q_ref.shape[0]
    count = rows * lax.axis_size(PROMPT_AXES)
    first_row = (lax.axis_index("ctx") * cand_size + lax.axis_index("cand")) * rows
    key_pos = lax.broadcasted_iota(jnp.int32, (1, count), 1)
    for head in range(kv_ref.shape[2] // HEADDIM):
        key_rows, widened = head_operands(kv_ref, count, head)
        for heads, queries in tiles(q_ref, head):
            row_pos = stacked_rows(first_row, rows, queries.shape[0])
            result = blend(queries, key_rows, widened, key_pos, row_pos, 0)
            for index, h in enumerate(heads):
                out_ref[:, h * HEADDIM : (h + 1) * HEADDIM] = result[
                    index * rows : (index + 1) * rows
                ].astype(jnp.bfloat16)


def cand_kernel(masks, ctx_size, cand_size, q_ref, ends_ref, head_ref, lengths_ref, *refs):
    pays, blocks = refs[: len(masks)], refs[len(masks) : -3]
    out_ref, logit_ref, kv_ref = refs[-3:]
    rows = q_ref.shape[0]
    free = rows * ctx_size * cand_size
    place = lax.axis_index("ctx")
    for ref, owners in zip(blocks, prompt_owners(ctx_size, cand_size)):
        for index, owner in enumerate(owners):
            at = pl.ds(pl.multiple_of(owner * rows, rows), rows)
            kv_ref[0, at, :] = ref[index, 0]
            kv_ref[1, at, :] = ref[index, 1]
    picked = jnp.zeros(pays[0].shape[1:], jnp.float32)
    for ref, mask in zip(pays, masks):
        at = pl.ds(pl.multiple_of(free + (place ^ mask) * rows, rows), rows)
        kv_ref[0, at, :] = ref[0]
        kv_ref[1, at, :] = ref[1]
        picked += ref[2].astype(jnp.float32)
    steps = ends_ref.shape[1]
    width = picked.shape[1]
    step_rows = [picked[at : at + steps] for at in range(0, steps * q_ref.shape[1] // width, steps)]

    count = free + rows * len(masks)
    key_pos = lax.broadcasted_iota(jnp.int32, (1, rows * len(masks)), 1)
    first_row = place * rows
    length = lengths_ref[:, :1]
    alive = stacked_rows(first_row, rows, rows) < length
    ends = column_of(ends_ref[...])
    total = jnp.zeros((steps, HEADDIM), jnp.float32)
    for head in range(kv_ref.shape[2] // HEADDIM):
        key_rows, widened = head_operands(kv_ref, count, head)
        for heads, queries in tiles(q_ref, head):
            own_rows = queries.shape[0]
            places = [divmod(h * HEADDIM, width) for h in heads]
            picks = jnp.concatenate([step_rows[a][:, b : b + HEADDIM] for a, b in places], axis=0)
            queries = jnp.concatenate([queries, picks.astype(jnp.bfloat16)], axis=0)
            row_pos = jnp.concatenate(
                [stacked_rows(first_row, rows, own_rows)] + [ends] * len(heads), axis=0
            )
            result = blend(queries, key_rows, widened, key_pos, row_pos, free)
            for index, h in enumerate(heads):
                kept = jnp.where(alive, result[index * rows : (index + 1) * rows], 0.0)
                out_ref[:, h * HEADDIM : (h + 1) * HEADDIM] = kept.astype(jnp.bfloat16)
                start = own_rows + index * steps
                kept = jnp.where(ends < length, result[start : start + steps], 0.0)
                kept = kept.astype(jnp.bfloat16).astype(jnp.float32)
                total += kept * head_ref[:, h * HEADDIM : (h + 1) * HEADDIM]
    logits = jnp.sum(total, axis=1, keepdims=True)
    down = lax.broadcasted_iota(jnp.int32, (steps, steps), 0)
    right = lax.broadcasted_iota(jnp.int32, (steps, steps), 1)
    logit_ref[...] = jnp.sum(jnp.where(down == right, logits, 0.0), axis=0, keepdims=True)


def per_device(ctx_size, cand_size, prompt_q, prompt_kv, cand_q, cand_kv, cand_lengths, step_ends, reward_head):
    q_rows, cand_rows, own, payload, ends, head, lengths = staged(
        cand_lengths, prompt_q, cand_q[0], prompt_kv, cand_kv[:, 0], step_ends, reward_head[None]
    )
    pays = gather_cand(payload, ctx_size)
    blocks = gather_prompt(prompt_kv, own, [b for b, _ in pays], ctx_size, cand_size)
    key_count = q_rows.shape[0] * ctx_size * cand_size + cand_rows.shape[0] * ctx_size
    cand_out, partial, arranged = pl.pallas_call(
        functools.partial(cand_kernel, [mask for _, mask in pays], ctx_size, cand_size),
        out_shape=(
            like(cand_rows),
            jax.ShapeDtypeStruct(step_ends.shape, jnp.float32),
            jax.ShapeDtypeStruct((2, key_count, own.shape[2]), own.dtype),
        ),
        in_specs=vmem(4 + len(pays) + len(blocks)),
        out_specs=tuple(vmem(3)),
        compiler_params=PARAMS,
        name="cand_attention",
    )(cand_rows, ends, head, lengths, *(b for b, _ in pays), *blocks)
    step_logits = partial
    tp_size = lax.axis_size("tp")
    for bit in high_bits(tp_size, 1):
        step_logits = step_logits + flipped(step_logits, "tp", tp_size, bit)
    prompt_out = pl.pallas_call(
        functools.partial(prompt_kernel, cand_size),
        out_shape=like(prompt_q),
        in_specs=vmem(2),
        out_specs=vmem(1)[0],
        compiler_params=PARAMS,
        name="prompt_attention",
    )(q_rows, arranged)
    return (prompt_out, cand_out[None], step_logits)


def solution(mesh):
    placed = (
        P(("ctx", "cand"), "tp"),
        P(None, ("ctx", "cand"), "tp"),
        P("cand", "ctx", "tp"),
        P(None, "cand", "ctx", "tp"),
        P("cand"),
        P("cand", None),
        P("tp"),
    )
    return jax.shard_map(
        functools.partial(per_device, mesh.shape["ctx"], mesh.shape["cand"]),
        mesh=mesh,
        in_specs=placed,
        out_specs=(P(("ctx", "cand"), "tp"), P("cand", "ctx", "tp"), P("cand", None)),
        check_vma=False,
    )
```

```python
import functools
import math

import jax
import jax.numpy as jnp
from jax import lax
from jax.experimental import pallas as pl
from jax.experimental.pallas import tpu as pltpu
from jax.sharding import PartitionSpec as P

HEADDIM = 128
GROUP = 8
SUBLANES = 8
NEG_FILL = -1e30
SCALE = HEADDIM ** -0.5 * math.log2(math.e)
ROW_TILE = 256
VMEM_LIMIT = 28 * 1024 * 1024
PARAMS = pltpu.CompilerParams(vmem_limit_bytes=VMEM_LIMIT)
PROMPT_AXES = ("ctx", "cand")


def vmem(count):
    return [pl.BlockSpec(memory_space=pltpu.VMEM)] * count


def like(array):
    return jax.ShapeDtypeStruct(array.shape, array.dtype)


def high_bits(size, lowest):
    return [1 << b for b in reversed(range(size.bit_length() - 1)) if 1 << b >= lowest]


def flipped(block, axes, size, bit):
    return lax.ppermute(block, axes, [(i, i ^ bit) for i in range(size)])


def pack_kernel(count, *refs):
    sources, out_ref = refs[:count], refs[-1]
    start = 0
    for ref in sources:
        out_ref[start : start + ref.shape[0]] = ref[...]
        start += ref.shape[0]


def packed(*arrays, after=()):
    count = sum(a.shape[0] for a in arrays)
    return pl.pallas_call(
        functools.partial(pack_kernel, len(arrays)),
        out_shape=jax.ShapeDtypeStruct((count,) + arrays[0].shape[1:], arrays[0].dtype),
        in_specs=vmem(len(arrays)) + [pl.BlockSpec(memory_space=pl.ANY)] * len(after),
        out_specs=vmem(1)[0],
        compiler_params=PARAMS,
        name="pack_blocks",
    )(*arrays, *after)


def prompt_bits(ctx_size, cand_size):
    core, along, across = cand_size, 1, 2 * cand_size
    early = high_bits(cand_size, 2) + [bit * cand_size for bit in high_bits(ctx_size, 4)]
    return early, along, across, core


def prompt_owners(ctx_size, cand_size):
    early, along, across, core = prompt_bits(ctx_size, cand_size)
    place = lax.axis_index("ctx") * cand_size + lax.axis_index("cand")
    odd = lax.rem(lax.axis_index("ctx"), 2)
    near = along + odd * (across - along)
    far = along + across - near
    masks = [0]
    for bit in early:
        masks += [mask ^ bit for mask in masks]
    shifts = [0, near, far, along + across, core, core + far, core + near, core + along + across]
    return [[place ^ mask ^ shift for mask in masks] for shift in shifts]


def gather_cand(own, ctx_size):
    blocks = [(own, 0), (flipped(own, "ctx", ctx_size, 1), 1)]
    for bit in reversed(high_bits(ctx_size, 2)):
        rail = [(flipped(b, "ctx", ctx_size, bit), mask | bit) for b, mask in blocks if not mask & 1]
        blocks += rail + [(flipped(b, "ctx", ctx_size, 1), mask | 1) for b, mask in rail]
    return blocks


def stage_kernel(length_ref, prompt_q, cand_q, prompt_kv, cand_kv, ends, head, *refs):
    q_out, cand_out, kv_out, pay_out, ends_out, head_out, length_out, length_here, sems = refs
    steps = ends.shape[1]
    pairs = [
        (cand_q, cand_out),
        (ends, ends_out),
        (cand_kv, pay_out.at[0:2]),
        (prompt_kv, kv_out),
        (prompt_q, q_out),
        (head, head_out),
        (length_ref, length_here),
    ]
    copies = [pltpu.make_async_copy(a, b, sems.at[i]) for i, (a, b) in enumerate(pairs)]
    for copy in copies:
        copy.start()
    copies[0].wait()
    copies[1].wait()
    rows = cand_out.shape[0]
    ends_column = column_of(ends_out[...])
    row_pos = lax.axis_index("ctx") * rows + lax.broadcasted_iota(jnp.int32, (steps, rows), 1)
    chosen = (row_pos == ends_column).astype(jnp.bfloat16)
    picked = jnp.dot(chosen, cand_out[...], preferred_element_type=jnp.float32)
    width = pay_out.shape[2]
    pieces = [picked[:, at : at + width] for at in range(0, picked.shape[1], width)]
    pay_out[2] = jnp.concatenate(pieces, axis=0).astype(jnp.bfloat16)
    for copy in copies[2:]:
        copy.wait()
    length_out[...] = jnp.full(length_out.shape, length_here[0], jnp.int32)


def column_of(row):
    count = row.shape[1]
    down = lax.broadcasted_iota(jnp.int32, (count, count), 0)
    right = lax.broadcasted_iota(jnp.int32, (count, count), 1)
    return jnp.sum(jnp.where(down == right, row, 0), axis=1, keepdims=True)


def staged(length, prompt_q, cand_q, prompt_kv, cand_kv, ends, head):
    arrays = (prompt_q, cand_q, prompt_kv, cand_kv, ends, head)
    payload = jax.ShapeDtypeStruct((3,) + cand_kv.shape[1:], cand_kv.dtype)
    lengths = jax.ShapeDtypeStruct((1, HEADDIM), jnp.int32)
    return pl.pallas_call(
        stage_kernel,
        out_shape=(like(prompt_q), like(cand_q), like(prompt_kv), payload, like(ends), like(head), lengths),
        in_specs=[pl.BlockSpec(memory_space=pl.ANY)]
        + [pl.BlockSpec(memory_space=pltpu.HBM)] * len(arrays),
        out_specs=tuple(vmem(7)),
        scratch_shapes=[pltpu.SMEM((1,), jnp.int32), pltpu.SemaphoreType.DMA((len(arrays) + 1,))],
        compiler_params=PARAMS,
        name="stage_operands",
    )(length, *(pltpu.with_memory_space_constraint(a, pltpu.HBM) for a in arrays))


def tiles(q_ref, head):
    rows = q_ref.shape[0]
    fan = max(1, ROW_TILE // rows)
    for start in range(head * GROUP, (head + 1) * GROUP, fan):
        heads = range(start, start + fan)
        queries = jnp.concatenate([q_ref[:, h * HEADDIM : (h + 1) * HEADDIM] for h in heads], axis=0)
        yield heads, slice(start * rows, (start + fan) * rows), queries


def stacked_rows(first_row, rows, count):
    return first_row + lax.rem(lax.broadcasted_iota(jnp.int32, (count, 1), 0), jnp.int32(rows))


def product(queries, key_rows):
    return lax.dot_general(
        queries, key_rows, (((1,), (1,)), ((), ())), preferred_element_type=jnp.float32
    )


def with_ones(value_rows):
    return jnp.concatenate([value_rows, jnp.ones_like(value_rows)], axis=1)


def head_rows(blocks, which, head):
    columns = slice(head * HEADDIM, (head + 1) * HEADDIM)
    return jnp.concatenate([ref[lead + (which,)][:, columns] for ref, lead in blocks], axis=0)


def key_positions(owners, rows):
    lane = lax.broadcasted_iota(jnp.int32, (1, len(owners) * rows), 1)
    positions = lane
    for index, owner in enumerate(owners):
        inside = (lane >= index * rows) & (lane < (index + 1) * rows)
        positions = jnp.where(inside, lane + (owner - index) * rows, positions)
    return positions


def spread(column, count):
    return jnp.concatenate([column] * (count // column.shape[1]), axis=1)


def absorb(queries, key_rows, widened, allowed, old):
    scores = product(queries, key_rows)
    if allowed is not None:
        scores = jnp.where(allowed, scores, NEG_FILL)
    count = scores.shape[1]
    peak = jnp.broadcast_to(jnp.max(scores, axis=1, keepdims=True), (scores.shape[0], HEADDIM))
    if old is not None:
        peak = jnp.maximum(peak, old[0])
    weights = jnp.exp2((scores - spread(peak, count)) * SCALE).astype(jnp.bfloat16)
    blended = jnp.dot(weights, widened, preferred_element_type=jnp.float32)
    if old is not None:
        blended += old[1] * spread(jnp.exp2((old[0] - peak) * SCALE), old[1].shape[1])
    return peak, blended


def prompt_place(cand_size):
    return lax.axis_index("ctx") * cand_size + lax.axis_index("cand")


def pairs_of(refs):
    return [(ref, (index,)) for ref in refs for index in range(ref.shape[0])]


def phase_kernel(sizes, arrays, masks, first, last, *refs):
    ctx_size, cand_size = sizes
    take = iter(refs)
    prompt_q, cand_q = next(take), next(take)
    block_refs = [next(take) for _ in arrays]
    pays = [next(take) for _ in masks]
    lengths = next(take) if last else None
    old = None if first else [(next(take), next(take)) for _ in range(2)]
    outs = refs[-2:] if last else refs[-4:]
    rows = prompt_q.shape[0]
    cand_rows = cand_q.shape[0]
    owners = prompt_owners(ctx_size, cand_size)
    key_pos = key_positions([place for index in arrays for place in owners[index]], rows)
    blocks = pairs_of(block_refs)
    own = [(ref, ()) for ref in pays]
    ctx = lax.axis_index("ctx")
    own_pos = key_positions([ctx ^ mask for mask in masks], cand_rows) if masks else None
    alive = stacked_rows(ctx * cand_rows, cand_rows, cand_rows) < lengths[:, :1] if last else None

    for head in range(block_refs[0].shape[3] // HEADDIM):
        key_rows = head_rows(blocks, 0, head)
        widened = with_ones(head_rows(blocks, 1, head))
        if masks:
            all_keys = jnp.concatenate([key_rows, head_rows(own, 0, head)], axis=0)
            all_widened = jnp.concatenate([widened, with_ones(head_rows(own, 1, head))], axis=0)
            free = jnp.full((1, key_rows.shape[0]), -1, jnp.int32)
            all_pos = jnp.concatenate([free, own_pos], axis=1)
        for kind, q_ref in enumerate((cand_q, prompt_q)):
            for heads, at, queries in tiles(q_ref, head):
                count = queries.shape[0]
                state = None if first else (old[kind][0][at], old[kind][1][at])
                if kind == 1:
                    first_row = prompt_place(cand_size) * rows
                    allowed = key_pos <= stacked_rows(first_row, rows, count)
                    state = absorb(queries, key_rows, widened, allowed, state)
                elif masks:
                    allowed = all_pos <= stacked_rows(ctx * cand_rows, cand_rows, count)
                    state = absorb(queries, all_keys, all_widened, allowed, state)
                else:
                    state = absorb(queries, key_rows, widened, None, state)
                if not last:
                    outs[2 * kind][at] = state[0]
                    outs[2 * kind + 1][at] = state[1]
                    continue
                result = state[1][:, :HEADDIM] / state[1][:, HEADDIM:]
                each = q_ref.shape[0]
                for index, h in enumerate(heads):
                    kept = result[index * each : (index + 1) * each]
                    if kind == 0:
                        kept = jnp.where(alive, kept, 0.0)
                    outs[kind][:, h * HEADDIM : (h + 1) * HEADDIM] = kept.astype(jnp.bfloat16)


def phase(sizes, arrays, q_rows, blocks, pays=(), state=None, lengths=None, after=()):
    prompt_q, cand_q = q_rows
    first, last = state is None, lengths is not None
    operands = [prompt_q, cand_q] + [blocks[index] for index in arrays]
    operands += [b for b, _ in pays]
    if last:
        operands.append(lengths)
    if not first:
        operands += state
    heads = prompt_q.shape[1] // HEADDIM
    if last:
        shapes = [like(cand_q), like(prompt_q)]
    else:
        shapes = []
        for q in (cand_q, prompt_q):
            count = heads * q.shape[0]
            shapes.append(jax.ShapeDtypeStruct((count, HEADDIM), jnp.float32))
            shapes.append(jax.ShapeDtypeStruct((count, 2 * HEADDIM), jnp.float32))
    key_count = sum(blocks[i].shape[0] * blocks[i].shape[2] for i in arrays)
    scores = heads * (prompt_q.shape[0] + cand_q.shape[0]) * key_count
    masks = [mask for _, mask in pays]
    return pl.pallas_call(
        functools.partial(phase_kernel, sizes, arrays, masks, first, last),
        out_shape=tuple(shapes),
        in_specs=vmem(len(operands)) + [pl.BlockSpec(memory_space=pl.ANY)] * len(after),
        out_specs=tuple(vmem(len(shapes))),
        compiler_params=PARAMS,
        cost_estimate=pl.CostEstimate(
            flops=6 * scores * HEADDIM, bytes_accessed=scores, transcendentals=scores
        ),
        name="attend_" + "_".join(str(i) for i in arrays),
    )(*operands, *after)


def step_kernel(sizes, masks, ends_ref, head_ref, lengths_ref, *refs):
    ctx_size, cand_size = sizes
    pays, blocks = refs[: len(masks)], refs[len(masks) : -2]
    logit_ref, kv_ref = refs[-2:]
    rows = blocks[0].shape[2]
    own_rows = pays[0].shape[1]
    free = rows * ctx_size * cand_size
    place = lax.axis_index("ctx")
    for ref, owners in zip(blocks, prompt_owners(ctx_size, cand_size)):
        for index, owner in enumerate(owners):
            at = pl.ds(pl.multiple_of(owner * rows, rows), rows)
            kv_ref[0, at, :] = ref[index, 0]
            kv_ref[1, at, :] = ref[index, 1]
    picked = jnp.zeros(pays[0].shape[1:], jnp.float32)
    for ref, mask in zip(pays, masks):
        at = pl.ds(pl.multiple_of(free + (place ^ mask) * own_rows, own_rows), own_rows)
        kv_ref[0, at, :] = ref[0]
        kv_ref[1, at, :] = ref[1]
        picked += ref[2].astype(jnp.float32)
    steps = ends_ref.shape[1]
    width = picked.shape[1]
    step_rows = [picked[at : at + steps] for at in range(0, steps * head_ref.shape[1] // width, steps)]

    ends = column_of(ends_ref[...])
    own_pos = lax.broadcasted_iota(jnp.int32, (1, own_rows * len(masks)), 1)
    row_pos = jnp.concatenate([ends] * GROUP, axis=0)
    total = jnp.zeros((steps, HEADDIM), jnp.float32)
    for head in range(width // HEADDIM):
        columns = slice(head * HEADDIM, (head + 1) * HEADDIM)
        heads = range(head * GROUP, (head + 1) * GROUP)
        places = [divmod(h * HEADDIM, width) for h in heads]
        queries = jnp.concatenate([step_rows[a][:, b : b + HEADDIM] for a, b in places], axis=0)
        scores = product(queries.astype(jnp.bfloat16), kv_ref[0, :, columns])
        bound = jnp.where(own_pos <= row_pos, scores[:, free:], NEG_FILL)
        scores = jnp.concatenate([scores[:, :free], bound], axis=1)
        peak = jnp.max(scores, axis=1, keepdims=True)
        weights = jnp.exp2((scores - peak) * SCALE).astype(jnp.bfloat16)
        blended = jnp.dot(weights, with_ones(kv_ref[1, :, columns]), preferred_element_type=jnp.float32)
        result = blended[:, :HEADDIM] / blended[:, HEADDIM:]
        for index, h in enumerate(heads):
            kept = jnp.where(ends < lengths_ref[:, :1], result[index * steps : (index + 1) * steps], 0.0)
            kept = kept.astype(jnp.bfloat16).astype(jnp.float32)
            total += kept * head_ref[:, h * HEADDIM : (h + 1) * HEADDIM]
    logits = jnp.sum(total, axis=1, keepdims=True)
    down = lax.broadcasted_iota(jnp.int32, (steps, steps), 0)
    right = lax.broadcasted_iota(jnp.int32, (steps, steps), 1)
    logit_ref[...] = jnp.sum(jnp.where(down == right, logits, 0.0), axis=0, keepdims=True)


def step_shares(sizes, ends, head, lengths, pays, blocks):
    ctx_size, cand_size = sizes
    rows, width = blocks[0].shape[2:]
    count = rows * ctx_size * cand_size + pays[0][0].shape[1] * ctx_size
    scores = ends.shape[1] * head.shape[1] // HEADDIM * count
    return pl.pallas_call(
        functools.partial(step_kernel, sizes, [mask for _, mask in pays]),
        out_shape=jax.ShapeDtypeStruct(ends.shape, jnp.float32),
        in_specs=vmem(3 + len(pays) + len(blocks)),
        out_specs=vmem(1)[0],
        scratch_shapes=[pltpu.VMEM((2, count, width), blocks[0].dtype)],
        compiler_params=PARAMS,
        cost_estimate=pl.CostEstimate(
            flops=6 * scores * HEADDIM, bytes_accessed=scores, transcendentals=scores
        ),
        name="step_logits",
    )(ends, head, lengths, *(b for b, _ in pays), *blocks)


def per_device(ctx_size, cand_size, prompt_q, prompt_kv, cand_q, cand_kv, cand_lengths, step_ends, reward_head):
    sizes = ctx_size, cand_size
    size = ctx_size * cand_size
    prompt_rows, cand_rows, own, payload, ends, head, lengths = staged(
        cand_lengths, prompt_q, cand_q[0], prompt_kv, cand_kv[:, 0], step_ends, reward_head[None]
    )
    q_rows = prompt_rows, cand_rows
    pays = gather_cand(payload, ctx_size)
    early, along, across, core = prompt_bits(ctx_size, cand_size)

    def across_cores(block):
        return flipped(block, PROMPT_AXES, size, core)

    def shared_out(block, even, odd):
        return lax.ppermute(
            block, PROMPT_AXES, [(i, i ^ (odd if i & core else even)) for i in range(size)]
        )

    held = own[None]
    sent = prompt_kv[None]
    for bit in early:
        held = packed(held, flipped(sent, PROMPT_AXES, size, bit))
        sent = held
    second = shared_out(held, along, across)
    third = shared_out(held, across, along)
    blocks = [held, second, third, None, across_cores(held), None, None, None]
    state = phase(sizes, [0, 4], q_rows, blocks)
    fourth = shared_out(packed(second, after=state[:1] + tuple(b for b, _ in pays[1:4])), across, along)
    blocks[3] = fourth
    blocks[5:7] = across_cores(second), across_cores(third)
    state = phase(sizes, [1, 2], q_rows, blocks, pays=pays, state=state)
    blocks[7] = across_cores(packed(fourth, after=state[:1]))
    state = phase(sizes, [5, 6], q_rows, blocks, state=state)
    step_logits = step_shares(sizes, ends, head, lengths, pays, blocks)
    cand_out, prompt_out = phase(sizes, [3, 7], q_rows, blocks, state=state, lengths=lengths)
    tp_size = lax.axis_size("tp")
    for bit in high_bits(tp_size, 1):
        step_logits = step_logits + flipped(step_logits, "tp", tp_size, bit)
    return (prompt_out, cand_out[None], step_logits)


def solution(mesh):
    placed = (
        P(("ctx", "cand"), "tp"),
        P(None, ("ctx", "cand"), "tp"),
        P("cand", "ctx", "tp"),
        P(None, "cand", "ctx", "tp"),
        P("cand"),
        P("cand", None),
        P("tp"),
    )
    return jax.shard_map(
        functools.partial(per_device, mesh.shape["ctx"], mesh.shape["cand"]),
        mesh=mesh,
        in_specs=placed,
        out_specs=(P(("ctx", "cand"), "tp"), P("cand", "ctx", "tp"), P("cand", None)),
        check_vma=False,
    )
```

```python
import functools
import math

import jax
import jax.numpy as jnp
from jax import lax
from jax.experimental import pallas as pl
from jax.experimental.pallas import tpu as pltpu
from jax.sharding import PartitionSpec as P

HEADDIM = 128
GROUP = 8
SUBLANES = 8
NEG_FILL = -1e30
SCALE = HEADDIM ** -0.5 * math.log2(math.e)
ROW_TILE = 256
VMEM_LIMIT = 28 * 1024 * 1024
PARAMS = pltpu.CompilerParams(vmem_limit_bytes=VMEM_LIMIT)
PROMPT_AXES = ("ctx", "cand")


def vmem(count):
    return [pl.BlockSpec(memory_space=pltpu.VMEM)] * count


def like(array):
    return jax.ShapeDtypeStruct(array.shape, array.dtype)


def high_bits(size, lowest):
    return [1 << b for b in reversed(range(size.bit_length() - 1)) if 1 << b >= lowest]


def flipped(block, axes, size, bit):
    return lax.ppermute(block, axes, [(i, i ^ bit) for i in range(size)])


def pack_kernel(count, *refs):
    sources, out_ref = refs[:count], refs[-1]
    start = 0
    for ref in sources:
        out_ref[start : start + ref.shape[0]] = ref[...]
        start += ref.shape[0]


def packed(*arrays, after=()):
    count = sum(a.shape[0] for a in arrays)
    return pl.pallas_call(
        functools.partial(pack_kernel, len(arrays)),
        out_shape=jax.ShapeDtypeStruct((count,) + arrays[0].shape[1:], arrays[0].dtype),
        in_specs=vmem(len(arrays)) + [pl.BlockSpec(memory_space=pl.ANY)] * len(after),
        out_specs=vmem(1)[0],
        compiler_params=PARAMS,
        name="pack_blocks",
    )(*arrays, *after)


def pack_side_kernel(even_ref, odd_ref, last_ref, _, out_ref):
    count = last_ref.shape[0]
    out_ref[count:] = last_ref[...]
    odd = lax.rem(lax.axis_index("ctx"), 2)

    @pl.when(odd == 0)
    def _():
        out_ref[:count] = even_ref[...]

    @pl.when(odd == 1)
    def _():
        out_ref[:count] = odd_ref[...]


def packed_side(even, odd, last, after):
    return pl.pallas_call(
        pack_side_kernel,
        out_shape=jax.ShapeDtypeStruct((2 * last.shape[0],) + last.shape[1:], last.dtype),
        in_specs=vmem(3) + [pl.BlockSpec(memory_space=pl.ANY)],
        out_specs=vmem(1)[0],
        compiler_params=PARAMS,
        name="pack_side",
    )(even, odd, last, after)


def prompt_bits(ctx_size, cand_size):
    core, along, across = cand_size, 1, 2 * cand_size
    early = high_bits(cand_size, 2) + [bit * cand_size for bit in high_bits(ctx_size, 4)]
    return early, along, across, core


def prompt_owners(ctx_size, cand_size):
    early, along, across, core = prompt_bits(ctx_size, cand_size)
    place = prompt_place(cand_size)
    near = along + lax.rem(lax.axis_index("ctx"), 2) * (across - along)
    far = along + across - near
    masks = [0]
    for bit in early[:-1]:
        masks += [mask ^ bit for mask in masks]
    last = early[-1]
    both = along + across
    shifts = [[0], [core], [across], [across + core]]
    shifts += [[last, along], [core + last, core + along]]
    shifts += [[last + near, last + far], [core + last + far, core + last + near]]
    shifts += [[both, both + last], [core + both, core + both + last]]
    return [[place ^ mask ^ shift for shift in array for mask in masks] for array in shifts]


def stage_kernel(prompt_q, cand_q, prompt_kv, cand_kv, ends, head, *refs):
    q_out, cand_out, own_out, pay_out, ends_out, head_out, sems = refs
    steps = ends.shape[1]
    pairs = [
        (cand_q, cand_out),
        (ends, ends_out),
        (prompt_kv, own_out),
        (cand_kv, pay_out.at[0:2]),
        (prompt_q, q_out),
        (head, head_out),
    ]
    copies = [pltpu.make_async_copy(a, b, sems.at[i]) for i, (a, b) in enumerate(pairs)]
    for copy in copies:
        copy.start()
    copies[0].wait()
    copies[1].wait()
    rows = cand_out.shape[0]
    ends_column = column_of(ends_out[...])
    row_pos = lax.axis_index("ctx") * rows + lax.broadcasted_iota(jnp.int32, (steps, rows), 1)
    chosen = (row_pos == ends_column).astype(jnp.bfloat16)
    picked = jnp.dot(chosen, cand_out[...], preferred_element_type=jnp.float32)
    width = pay_out.shape[2]
    pieces = [picked[:, at : at + width] for at in range(0, picked.shape[1], width)]
    pay_out[2] = jnp.concatenate(pieces, axis=0).astype(jnp.bfloat16)
    for copy in copies[2:]:
        copy.wait()


def column_of(row):
    count = row.shape[1]
    down = lax.broadcasted_iota(jnp.int32, (count, count), 0)
    right = lax.broadcasted_iota(jnp.int32, (count, count), 1)
    return jnp.sum(jnp.where(down == right, row, 0), axis=1, keepdims=True)


def staged(prompt_q, cand_q, prompt_kv, cand_kv, ends, head):
    arrays = (prompt_q, cand_q, prompt_kv, cand_kv, ends, head)
    pay = jax.ShapeDtypeStruct((3,) + cand_kv.shape[1:], cand_kv.dtype)
    return pl.pallas_call(
        stage_kernel,
        out_shape=(like(prompt_q), like(cand_q), like(prompt_kv), pay, like(ends), like(head)),
        in_specs=[pl.BlockSpec(memory_space=pltpu.HBM)] * len(arrays),
        out_specs=tuple(vmem(6)),
        scratch_shapes=[pltpu.SemaphoreType.DMA((len(arrays),))],
        compiler_params=PARAMS,
        name="stage_operands",
    )(*(pltpu.with_memory_space_constraint(a, pltpu.HBM) for a in arrays))


def tiles(q_ref, head):
    rows = q_ref.shape[0]
    fan = max(1, ROW_TILE // rows)
    for start in range(head * GROUP, (head + 1) * GROUP, fan):
        heads = range(start, start + fan)
        queries = jnp.concatenate([q_ref[:, h * HEADDIM : (h + 1) * HEADDIM] for h in heads], axis=0)
        yield heads, slice(start * rows, (start + fan) * rows), queries


def stacked_rows(first_row, rows, count):
    return first_row + lax.rem(lax.broadcasted_iota(jnp.int32, (count, 1), 0), jnp.int32(rows))


def product(queries, key_rows):
    return lax.dot_general(
        queries, key_rows, (((1,), (1,)), ((), ())), preferred_element_type=jnp.float32
    )


def with_ones(value_rows):
    return jnp.concatenate([value_rows, jnp.ones_like(value_rows)], axis=1)


def head_rows(blocks, which, head):
    columns = slice(head * HEADDIM, (head + 1) * HEADDIM)
    return jnp.concatenate([ref[plane + which, :, columns] for ref, plane in blocks], axis=0)


def key_positions(owners, rows):
    lane = lax.broadcasted_iota(jnp.int32, (1, len(owners) * rows), 1)
    positions = lane
    for index, owner in enumerate(owners):
        inside = (lane >= index * rows) & (lane < (index + 1) * rows)
        positions = jnp.where(inside, lane + (owner - index) * rows, positions)
    return positions


def spread(column, count):
    return jnp.concatenate([column] * (count // column.shape[1]), axis=1)


def absorb(queries, key_rows, widened, allowed, old):
    scores = product(queries, key_rows)
    if allowed is not None:
        scores = jnp.where(allowed, scores, NEG_FILL)
    count = scores.shape[1]
    peak = jnp.broadcast_to(jnp.max(scores, axis=1, keepdims=True), (scores.shape[0], HEADDIM))
    if old is not None:
        peak = jnp.maximum(peak, old[0])
    weights = jnp.exp2((scores - spread(peak, count)) * SCALE).astype(jnp.bfloat16)
    blended = jnp.dot(weights, widened, preferred_element_type=jnp.float32)
    if old is not None:
        blended += old[1] * spread(jnp.exp2((old[0] - peak) * SCALE), old[1].shape[1])
    return peak, blended


def prompt_place(cand_size):
    return lax.axis_index("ctx") * cand_size + lax.axis_index("cand")


def payloads(refs, count):
    return [(ref, ref.shape[0] - 3 * (count - i)) for ref in refs for i in range(count)]


def phase_kernel(sizes, arrays, masks, first, last, *refs):
    ctx_size, cand_size = sizes
    take = iter(refs)
    prompt_q, cand_q = next(take), next(take)
    block_refs = [next(take) for _ in arrays]
    pay_refs = [next(take) for _ in range(4 if masks else 0)]
    lengths = next(take) if last else None
    old = None if first else [(next(take), next(take)) for _ in range(2)]
    outs = refs[-2:] if last else refs[-4:]
    rows = prompt_q.shape[0]
    cand_rows = cand_q.shape[0]
    owners = prompt_owners(ctx_size, cand_size)
    key_pos = key_positions([place for index in arrays for place in owners[index]], rows)
    blocks = [
        (ref, 2 * i) for ref, index in zip(block_refs, arrays) for i in range(len(owners[index]))
    ]
    own = payloads(pay_refs, len(masks) // len(pay_refs)) if masks else []
    ctx = lax.axis_index("ctx")
    own_pos = key_positions([ctx ^ mask for mask in masks], cand_rows) if masks else None
    alive = stacked_rows(ctx * cand_rows, cand_rows, cand_rows) < lengths[:, :1] if last else None

    for head in range(block_refs[0].shape[2] // HEADDIM):
        key_rows = head_rows(blocks, 0, head)
        widened = with_ones(head_rows(blocks, 1, head))
        if masks:
            all_keys = jnp.concatenate([key_rows, head_rows(own, 0, head)], axis=0)
            all_widened = jnp.concatenate([widened, with_ones(head_rows(own, 1, head))], axis=0)
            free = jnp.full((1, key_rows.shape[0]), -1, jnp.int32)
            all_pos = jnp.concatenate([free, own_pos], axis=1)
        for kind, q_ref in enumerate((cand_q, prompt_q)):
            for heads, at, queries in tiles(q_ref, head):
                count = queries.shape[0]
                state = None if first else (old[kind][0][at], old[kind][1][at])
                if kind == 1:
                    first_row = prompt_place(cand_size) * rows
                    allowed = key_pos <= stacked_rows(first_row, rows, count)
                    state = absorb(queries, key_rows, widened, allowed, state)
                elif masks:
                    allowed = all_pos <= stacked_rows(ctx * cand_rows, cand_rows, count)
                    state = absorb(queries, all_keys, all_widened, allowed, state)
                else:
                    state = absorb(queries, key_rows, widened, None, state)
                if not last:
                    outs[2 * kind][at] = state[0]
                    outs[2 * kind + 1][at] = state[1]
                    continue
                result = state[1][:, :HEADDIM] / state[1][:, HEADDIM:]
                each = q_ref.shape[0]
                for index, h in enumerate(heads):
                    kept = result[index * each : (index + 1) * each]
                    if kind == 0:
                        kept = jnp.where(alive, kept, 0.0)
                    outs[kind][:, h * HEADDIM : (h + 1) * HEADDIM] = kept.astype(jnp.bfloat16)


def phase(sizes, arrays, q_rows, blocks, masks=(), state=None, lengths=None, after=()):
    prompt_q, cand_q = q_rows
    first, last = state is None, lengths is not None
    operands = [prompt_q, cand_q] + [blocks[index] for index in arrays]
    operands += blocks[:4] if masks else []
    if last:
        operands.append(lengths)
    if not first:
        operands += state
    heads = prompt_q.shape[1] // HEADDIM
    if last:
        shapes = [like(cand_q), like(prompt_q)]
    else:
        shapes = []
        for q in (cand_q, prompt_q):
            count = heads * q.shape[0]
            shapes.append(jax.ShapeDtypeStruct((count, HEADDIM), jnp.float32))
            shapes.append(jax.ShapeDtypeStruct((count, 2 * HEADDIM), jnp.float32))
    key_count = sum(blocks[i].shape[0] // 2 * blocks[i].shape[1] for i in arrays)
    scores = heads * (prompt_q.shape[0] + cand_q.shape[0]) * key_count
    return pl.pallas_call(
        functools.partial(phase_kernel, sizes, arrays, masks, first, last),
        out_shape=tuple(shapes),
        in_specs=vmem(len(operands)) + [pl.BlockSpec(memory_space=pl.ANY)] * len(after),
        out_specs=tuple(vmem(len(shapes))),
        compiler_params=PARAMS,
        cost_estimate=pl.CostEstimate(
            flops=scores, bytes_accessed=scores, transcendentals=0
        ),
        name="attend_" + "_".join(str(i) for i in arrays),
    )(*operands, *after)


def step_kernel(sizes, masks, ends_ref, head_ref, lengths_ref, *refs):
    ctx_size, cand_size = sizes
    blocks = refs[:-2]
    logit_ref, kv_ref = refs[-2:]
    pays = payloads(blocks[:4], len(masks) // 4)
    rows = blocks[0].shape[1]
    own_rows = rows
    free = rows * ctx_size * cand_size
    place = lax.axis_index("ctx")
    for ref, owners in zip(blocks, prompt_owners(ctx_size, cand_size)):
        for index, owner in enumerate(owners):
            at = pl.ds(pl.multiple_of(owner * rows, rows), rows)
            kv_ref[0, at, :] = ref[2 * index]
            kv_ref[1, at, :] = ref[2 * index + 1]
    picked = jnp.zeros(blocks[0].shape[1:], jnp.float32)
    for (ref, plane), mask in zip(pays, masks):
        at = pl.ds(pl.multiple_of(free + (place ^ mask) * own_rows, own_rows), own_rows)
        kv_ref[0, at, :] = ref[plane]
        kv_ref[1, at, :] = ref[plane + 1]
        picked += ref[plane + 2].astype(jnp.float32)
    steps = ends_ref.shape[1]
    width = picked.shape[1]
    step_rows = [picked[at : at + steps] for at in range(0, steps * head_ref.shape[1] // width, steps)]

    ends = column_of(ends_ref[...])
    own_pos = lax.broadcasted_iota(jnp.int32, (1, own_rows * len(masks)), 1)
    row_pos = jnp.concatenate([ends] * GROUP, axis=0)
    total = jnp.zeros((steps, HEADDIM), jnp.float32)
    for head in range(width // HEADDIM):
        columns = slice(head * HEADDIM, (head + 1) * HEADDIM)
        heads = range(head * GROUP, (head + 1) * GROUP)
        places = [divmod(h * HEADDIM, width) for h in heads]
        queries = jnp.concatenate([step_rows[a][:, b : b + HEADDIM] for a, b in places], axis=0)
        scores = product(queries.astype(jnp.bfloat16), kv_ref[0, :, columns])
        bound = jnp.where(own_pos <= row_pos, scores[:, free:], NEG_FILL)
        scores = jnp.concatenate([scores[:, :free], bound], axis=1)
        peak = jnp.max(scores, axis=1, keepdims=True)
        weights = jnp.exp2((scores - peak) * SCALE).astype(jnp.bfloat16)
        blended = jnp.dot(weights, with_ones(kv_ref[1, :, columns]), preferred_element_type=jnp.float32)
        result = blended[:, :HEADDIM] / blended[:, HEADDIM:]
        for index, h in enumerate(heads):
            kept = jnp.where(ends < lengths_ref[:, :1], result[index * steps : (index + 1) * steps], 0.0)
            kept = kept.astype(jnp.bfloat16).astype(jnp.float32)
            total += kept * head_ref[:, h * HEADDIM : (h + 1) * HEADDIM]
    logits = jnp.sum(total, axis=1, keepdims=True)
    down = lax.broadcasted_iota(jnp.int32, (steps, steps), 0)
    right = lax.broadcasted_iota(jnp.int32, (steps, steps), 1)
    logit_ref[...] = jnp.sum(jnp.where(down == right, logits, 0.0), axis=0, keepdims=True)


def step_shares(sizes, ends, head, lengths, masks, blocks):
    ctx_size, cand_size = sizes
    rows, width = blocks[0].shape[1:]
    count = rows * ctx_size * cand_size + rows * ctx_size
    scores = ends.shape[1] * head.shape[1] // HEADDIM * count
    return pl.pallas_call(
        functools.partial(step_kernel, sizes, masks),
        out_shape=jax.ShapeDtypeStruct(ends.shape, jnp.float32),
        in_specs=vmem(3 + len(blocks)),
        out_specs=vmem(1)[0],
        scratch_shapes=[pltpu.VMEM((2, count, width), blocks[0].dtype)],
        compiler_params=PARAMS,
        cost_estimate=pl.CostEstimate(
            flops=scores, bytes_accessed=scores, transcendentals=0
        ),
        name="step_logits",
    )(ends, head, lengths, *blocks)


def per_device(ctx_size, cand_size, prompt_q, prompt_kv, cand_q, cand_kv, cand_lengths, step_ends, reward_head):
    sizes = ctx_size, cand_size
    size = ctx_size * cand_size
    prompt_rows, cand_rows, own, pay, ends, head = staged(
        prompt_q, cand_q[0], prompt_kv, cand_kv[:, 0], step_ends, reward_head[None]
    )
    lengths = jnp.broadcast_to(cand_lengths[None], (1, HEADDIM))
    q_rows = prompt_rows, cand_rows
    early, along, across, core = prompt_bits(ctx_size, cand_size)

    def moved(block, bit):
        return flipped(block, PROMPT_AXES, size, bit)

    def shared_out(block, even, odd):
        return lax.ppermute(
            block, PROMPT_AXES, [(i, i ^ (odd if i & core else even)) for i in range(size)]
        )

    held, sent = own, prompt_kv
    for bit in early[:-1]:
        held = packed(held, moved(sent, bit))
        sent = held
    pay_masks = [0]
    for bit in early:
        if bit >= size // ctx_size:
            pay = packed(pay, moved(pay, bit))
            pay_masks += [mask ^ bit // cand_size for mask in pay_masks]
    beyond = moved(sent, early[-1])
    beside = moved(held, along)
    opposite = moved(held, across)
    here = packed(held, pay)
    facing = packed(opposite, moved(pay, across))
    one = shared_out(beyond, along, across)
    two = shared_out(beyond, across, along)
    far = shared_out(packed_side(beside, opposite, one, two), across, along)
    pair = packed(beyond, beside)
    sides = packed(one, two)
    blocks = [here, moved(here, core), facing, moved(facing, core)]
    blocks += [pair, moved(pair, core), sides, moved(sides, core), far]
    masks = [mask ^ shift for shift in (0, 1, 2, 3) for mask in pay_masks]
    state = phase(sizes, [0, 1, 4, 5], q_rows, blocks, after=[facing])
    state = phase(sizes, [2, 3, 6, 7], q_rows, blocks, masks=masks, state=state)
    blocks.append(moved(packed(far, after=state[:1]), core))
    step_logits = step_shares(sizes, ends, head, lengths, masks, blocks)
    cand_out, prompt_out = phase(sizes, [8, 9], q_rows, blocks, state=state, lengths=lengths)
    tp_size = lax.axis_size("tp")
    for bit in high_bits(tp_size, 1):
        step_logits = step_logits + flipped(step_logits, "tp", tp_size, bit)
    return (prompt_out, cand_out[None], step_logits)


def solution(mesh):
    placed = (
        P(("ctx", "cand"), "tp"),
        P(None, ("ctx", "cand"), "tp"),
        P("cand", "ctx", "tp"),
        P(None, "cand", "ctx", "tp"),
        P("cand"),
        P("cand", None),
        P("tp"),
    )
    return jax.shard_map(
        functools.partial(per_device, mesh.shape["ctx"], mesh.shape["cand"]),
        mesh=mesh,
        in_specs=placed,
        out_specs=(P(("ctx", "cand"), "tp"), P("cand", "ctx", "tp"), P("cand", None)),
        check_vma=False,
    )
```

```python
import functools
import math

import jax
import jax.numpy as jnp
from jax import lax
from jax.experimental import pallas as pl
from jax.experimental.pallas import tpu as pltpu
from jax.sharding import PartitionSpec as P

HEADDIM = 128
GROUP = 8
SUBLANES = 8
NEG_FILL = -1e30
SCALE = HEADDIM ** -0.5 * math.log2(math.e)
ROW_TILE = 256
VMEM_LIMIT = 28 * 1024 * 1024
PARAMS = pltpu.CompilerParams(vmem_limit_bytes=VMEM_LIMIT)
PROMPT_AXES = ("ctx", "cand")
PAYING = 2


def vmem(count):
    return [pl.BlockSpec(memory_space=pltpu.VMEM)] * count


def like(array):
    return jax.ShapeDtypeStruct(array.shape, array.dtype)


def high_bits(size, lowest):
    return [1 << b for b in reversed(range(size.bit_length() - 1)) if 1 << b >= lowest]


def flipped(block, axes, size, bit):
    return lax.ppermute(block, axes, [(i, i ^ bit) for i in range(size)])


def pack_kernel(count, *refs):
    sources, out_ref = refs[:count], refs[-1]
    start = 0
    for ref in sources:
        out_ref[start : start + ref.shape[0]] = ref[...]
        start += ref.shape[0]


def packed(*arrays, after=()):
    count = sum(a.shape[0] for a in arrays)
    return pl.pallas_call(
        functools.partial(pack_kernel, len(arrays)),
        out_shape=jax.ShapeDtypeStruct((count,) + arrays[0].shape[1:], arrays[0].dtype),
        in_specs=vmem(len(arrays)) + [pl.BlockSpec(memory_space=pl.ANY)] * len(after),
        out_specs=vmem(1)[0],
        compiler_params=PARAMS,
        name="pack_blocks",
    )(*arrays, *after)


def prompt_bits(ctx_size, cand_size):
    core, along, across = cand_size, 1, 2 * cand_size
    early = high_bits(cand_size, 2) + [bit * cand_size for bit in high_bits(ctx_size, 4)]
    return early, along, across, core


def prompt_owners(ctx_size, cand_size):
    early, along, across, core = prompt_bits(ctx_size, cand_size)
    place = prompt_place(cand_size)
    masks = [0]
    for bit in early[:-1]:
        masks += [mask ^ bit for mask in masks]
    last, both = early[-1], along + across
    shifts = [[0], [last], [along, across], [both], [last + both], [last + across], [last + along]]
    shifts += [[core + shift for shift in array] for array in shifts[:4] + [sum(shifts[4:], [])]]
    return [[place ^ mask ^ shift for shift in array for mask in masks] for array in shifts]


def stage_kernel(prompt_q, cand_q, prompt_kv, cand_kv, ends, head, *refs):
    q_out, cand_out, own_out, pay_out, ends_out, head_out, sems = refs
    steps = ends.shape[1]
    pairs = [
        (cand_q, cand_out),
        (ends, ends_out),
        (prompt_kv, own_out),
        (cand_kv, pay_out.at[0:2]),
        (prompt_q, q_out),
        (head, head_out),
    ]
    copies = [pltpu.make_async_copy(a, b, sems.at[i]) for i, (a, b) in enumerate(pairs)]
    for copy in copies:
        copy.start()
    copies[0].wait()
    copies[1].wait()
    rows = cand_out.shape[0]
    ends_column = column_of(ends_out[...])
    row_pos = lax.axis_index("ctx") * rows + lax.broadcasted_iota(jnp.int32, (steps, rows), 1)
    chosen = (row_pos == ends_column).astype(jnp.bfloat16)
    picked = jnp.dot(chosen, cand_out[...], preferred_element_type=jnp.float32)
    width = pay_out.shape[2]
    pieces = [picked[:, at : at + width] for at in range(0, picked.shape[1], width)]
    pay_out[2] = jnp.concatenate(pieces, axis=0).astype(jnp.bfloat16)
    for copy in copies[2:]:
        copy.wait()


def column_of(row):
    count = row.shape[1]
    down = lax.broadcasted_iota(jnp.int32, (count, count), 0)
    right = lax.broadcasted_iota(jnp.int32, (count, count), 1)
    return jnp.sum(jnp.where(down == right, row, 0), axis=1, keepdims=True)


def staged(prompt_q, cand_q, prompt_kv, cand_kv, ends, head):
    arrays = (prompt_q, cand_q, prompt_kv, cand_kv, ends, head)
    pay = jax.ShapeDtypeStruct((3,) + cand_kv.shape[1:], cand_kv.dtype)
    return pl.pallas_call(
        stage_kernel,
        out_shape=(like(prompt_q), like(cand_q), like(prompt_kv), pay, like(ends), like(head)),
        in_specs=[pl.BlockSpec(memory_space=pltpu.HBM)] * len(arrays),
        out_specs=tuple(vmem(6)),
        scratch_shapes=[pltpu.SemaphoreType.DMA((len(arrays),))],
        compiler_params=PARAMS,
        name="stage_operands",
    )(*(pltpu.with_memory_space_constraint(a, pltpu.HBM) for a in arrays))


def tiles(q_ref, head):
    rows = q_ref.shape[0]
    fan = max(1, ROW_TILE // rows)
    for start in range(head * GROUP, (head + 1) * GROUP, fan):
        heads = range(start, start + fan)
        queries = jnp.concatenate([q_ref[:, h * HEADDIM : (h + 1) * HEADDIM] for h in heads], axis=0)
        yield heads, slice(start * rows, (start + fan) * rows), queries


def stacked_rows(first_row, rows, count):
    return first_row + lax.rem(lax.broadcasted_iota(jnp.int32, (count, 1), 0), jnp.int32(rows))


def product(queries, key_rows):
    return lax.dot_general(
        queries, key_rows, (((1,), (1,)), ((), ())), preferred_element_type=jnp.float32
    )


def with_ones(value_rows):
    return jnp.concatenate([value_rows, jnp.ones_like(value_rows)], axis=1)


def head_rows(blocks, which, head):
    columns = slice(head * HEADDIM, (head + 1) * HEADDIM)
    return jnp.concatenate([ref[plane + which, :, columns] for ref, plane in blocks], axis=0)


def key_positions(owners, rows):
    lane = lax.broadcasted_iota(jnp.int32, (1, len(owners) * rows), 1)
    positions = lane
    for index, owner in enumerate(owners):
        inside = (lane >= index * rows) & (lane < (index + 1) * rows)
        positions = jnp.where(inside, lane + (owner - index) * rows, positions)
    return positions


def spread(column, count):
    return jnp.concatenate([column] * (count // column.shape[1]), axis=1)


def absorb(queries, key_rows, widened, allowed, old):
    scores = product(queries, key_rows)
    if allowed is not None:
        scores = jnp.where(allowed, scores, NEG_FILL)
    count = scores.shape[1]
    peak = jnp.broadcast_to(jnp.max(scores, axis=1, keepdims=True), (scores.shape[0], HEADDIM))
    if old is not None:
        peak = jnp.maximum(peak, old[0])
    weights = jnp.exp2((scores - spread(peak, count)) * SCALE).astype(jnp.bfloat16)
    blended = jnp.dot(weights, widened, preferred_element_type=jnp.float32)
    if old is not None:
        blended += old[1] * spread(jnp.exp2((old[0] - peak) * SCALE), old[1].shape[1])
    return peak, blended


def prompt_place(cand_size):
    return lax.axis_index("ctx") * cand_size + lax.axis_index("cand")


def payloads(refs, count):
    return [(ref, ref.shape[0] - 3 * (count - i)) for ref in refs for i in range(count)]


def phase_kernel(sizes, arrays, masks, first, last, *refs):
    ctx_size, cand_size = sizes
    take = iter(refs)
    prompt_q, cand_q = next(take), next(take)
    block_refs = [next(take) for _ in arrays]
    pay_refs = [next(take) for _ in range(PAYING if masks else 0)]
    lengths = next(take) if last else None
    old = None if first else [(next(take), next(take)) for _ in range(2)]
    outs = refs[-6:-4] if last else refs[-4:]
    halls, sems = refs[-4:-2], refs[-2:]
    leaving = []
    rows = prompt_q.shape[0]
    cand_rows = cand_q.shape[0]
    owners = prompt_owners(ctx_size, cand_size)
    key_pos = key_positions([place for index in arrays for place in owners[index]], rows)
    blocks = [
        (ref, 2 * i) for ref, index in zip(block_refs, arrays) for i in range(len(owners[index]))
    ]
    own = payloads(pay_refs, len(masks) // len(pay_refs)) if masks else []
    ctx = lax.axis_index("ctx")
    own_pos = key_positions([ctx ^ mask for mask in masks], cand_rows) if masks else None
    alive = stacked_rows(ctx * cand_rows, cand_rows, cand_rows) < lengths[:, :1] if last else None

    for head in range(block_refs[0].shape[2] // HEADDIM):
        key_rows = head_rows(blocks, 0, head)
        widened = with_ones(head_rows(blocks, 1, head))
        if masks:
            all_keys = jnp.concatenate([key_rows, head_rows(own, 0, head)], axis=0)
            all_widened = jnp.concatenate([widened, with_ones(head_rows(own, 1, head))], axis=0)
            free = jnp.full((1, key_rows.shape[0]), -1, jnp.int32)
            all_pos = jnp.concatenate([free, own_pos], axis=1)
        for kind, q_ref in enumerate((cand_q, prompt_q)):
            for heads, at, queries in tiles(q_ref, head):
                count = queries.shape[0]
                state = None if first else (old[kind][0][at], old[kind][1][at])
                if kind == 1:
                    first_row = prompt_place(cand_size) * rows
                    allowed = key_pos <= stacked_rows(first_row, rows, count)
                    state = absorb(queries, key_rows, widened, allowed, state)
                elif masks:
                    allowed = all_pos <= stacked_rows(ctx * cand_rows, cand_rows, count)
                    state = absorb(queries, all_keys, all_widened, allowed, state)
                else:
                    state = absorb(queries, key_rows, widened, None, state)
                if not last:
                    outs[2 * kind][at] = state[0]
                    outs[2 * kind + 1][at] = state[1]
                    continue
                result = state[1][:, :HEADDIM] / state[1][:, HEADDIM:]
                each = q_ref.shape[0]
                for index, h in enumerate(heads):
                    kept = result[index * each : (index + 1) * each]
                    if kind == 0:
                        kept = jnp.where(alive, kept, 0.0)
                    halls[kind][:, h * HEADDIM : (h + 1) * HEADDIM] = kept.astype(jnp.bfloat16)
                part = slice(heads[0] * HEADDIM, (heads[-1] + 1) * HEADDIM)
                leaving.append(
                    pltpu.make_async_copy(
                        halls[kind].at[:, part],
                        outs[kind].at[:, part],
                        sems[kind].at[heads[0] // len(heads)],
                    )
                )
                leaving[-1].start()
    for copy in leaving:
        copy.wait()


def phase(sizes, arrays, q_rows, blocks, pays=(), masks=(), state=None, lengths=None, after=()):
    prompt_q, cand_q = q_rows
    first, last = state is None, lengths is not None
    operands = [prompt_q, cand_q] + [blocks[index] for index in arrays]
    operands += pays
    if last:
        operands.append(lengths)
    if not first:
        operands += state
    heads = prompt_q.shape[1] // HEADDIM
    scratch = []
    if last:
        shapes = [like(cand_q), like(prompt_q)]
        scratch = [pltpu.VMEM(q.shape, q.dtype) for q in (cand_q, prompt_q)]
        scratch += [pltpu.SemaphoreType.DMA((heads,))] * 2
    else:
        shapes = []
        for q in (cand_q, prompt_q):
            count = heads * q.shape[0]
            shapes.append(jax.ShapeDtypeStruct((count, HEADDIM), jnp.float32))
            shapes.append(jax.ShapeDtypeStruct((count, 2 * HEADDIM), jnp.float32))
    key_count = sum(blocks[i].shape[0] // 2 * blocks[i].shape[1] for i in arrays)
    scores = heads * (prompt_q.shape[0] + cand_q.shape[0]) * key_count
    return pl.pallas_call(
        functools.partial(phase_kernel, sizes, arrays, masks, first, last),
        out_shape=tuple(shapes),
        in_specs=vmem(len(operands)) + [pl.BlockSpec(memory_space=pl.ANY)] * len(after),
        out_specs=(pl.BlockSpec(memory_space=pl.ANY),) * 2 if last else tuple(vmem(len(shapes))),
        scratch_shapes=scratch,
        compiler_params=PARAMS,
        cost_estimate=pl.CostEstimate(
            flops=6 * scores * HEADDIM, bytes_accessed=scores, transcendentals=scores
        ),
        name="attend_" + "_".join(str(i) for i in arrays),
    )(*operands, *after)


def step_kernel(sizes, masks, ends_ref, head_ref, lengths_ref, *refs):
    ctx_size, cand_size = sizes
    pays, blocks = payloads(refs[:PAYING], len(masks) // PAYING), refs[PAYING:-2]
    logit_ref, kv_ref = refs[-2:]
    rows = blocks[0].shape[1]
    own_rows = rows
    free = rows * ctx_size * cand_size
    place = lax.axis_index("ctx")
    for ref, owners in zip(blocks, prompt_owners(ctx_size, cand_size)):
        for index, owner in enumerate(owners):
            at = pl.ds(pl.multiple_of(owner * rows, rows), rows)
            kv_ref[0, at, :] = ref[2 * index]
            kv_ref[1, at, :] = ref[2 * index + 1]
    picked = jnp.zeros(blocks[0].shape[1:], jnp.float32)
    for (ref, plane), mask in zip(pays, masks):
        at = pl.ds(pl.multiple_of(free + (place ^ mask) * own_rows, own_rows), own_rows)
        kv_ref[0, at, :] = ref[plane]
        kv_ref[1, at, :] = ref[plane + 1]
        picked += ref[plane + 2].astype(jnp.float32)
    steps = ends_ref.shape[1]
    width = picked.shape[1]
    step_rows = [picked[at : at + steps] for at in range(0, steps * head_ref.shape[1] // width, steps)]

    ends = column_of(ends_ref[...])
    own_pos = lax.broadcasted_iota(jnp.int32, (1, own_rows * len(masks)), 1)
    row_pos = jnp.concatenate([ends] * GROUP, axis=0)
    total = jnp.zeros((steps, HEADDIM), jnp.float32)
    for head in range(width // HEADDIM):
        columns = slice(head * HEADDIM, (head + 1) * HEADDIM)
        heads = range(head * GROUP, (head + 1) * GROUP)
        places = [divmod(h * HEADDIM, width) for h in heads]
        queries = jnp.concatenate([step_rows[a][:, b : b + HEADDIM] for a, b in places], axis=0)
        scores = product(queries.astype(jnp.bfloat16), kv_ref[0, :, columns])
        bound = jnp.where(own_pos <= row_pos, scores[:, free:], NEG_FILL)
        scores = jnp.concatenate([scores[:, :free], bound], axis=1)
        peak = jnp.max(scores, axis=1, keepdims=True)
        weights = jnp.exp2((scores - peak) * SCALE).astype(jnp.bfloat16)
        blended = jnp.dot(weights, with_ones(kv_ref[1, :, columns]), preferred_element_type=jnp.float32)
        result = blended[:, :HEADDIM] / blended[:, HEADDIM:]
        for index, h in enumerate(heads):
            kept = jnp.where(ends < lengths_ref[:, :1], result[index * steps : (index + 1) * steps], 0.0)
            kept = kept.astype(jnp.bfloat16).astype(jnp.float32)
            total += kept * head_ref[:, h * HEADDIM : (h + 1) * HEADDIM]
    logits = jnp.sum(total, axis=1, keepdims=True)
    down = lax.broadcasted_iota(jnp.int32, (steps, steps), 0)
    right = lax.broadcasted_iota(jnp.int32, (steps, steps), 1)
    logit_ref[...] = jnp.sum(jnp.where(down == right, logits, 0.0), axis=0, keepdims=True)


def step_shares(sizes, ends, head, lengths, pays, masks, blocks):
    ctx_size, cand_size = sizes
    rows, width = blocks[0].shape[1:]
    count = rows * ctx_size * cand_size + rows * ctx_size
    scores = ends.shape[1] * head.shape[1] // HEADDIM * count
    return pl.pallas_call(
        functools.partial(step_kernel, sizes, masks),
        out_shape=jax.ShapeDtypeStruct(ends.shape, jnp.float32),
        in_specs=vmem(3 + len(pays) + len(blocks)),
        out_specs=vmem(1)[0],
        scratch_shapes=[pltpu.VMEM((2, count, width), blocks[0].dtype)],
        compiler_params=PARAMS,
        cost_estimate=pl.CostEstimate(
            flops=6 * scores * HEADDIM, bytes_accessed=scores, transcendentals=scores
        ),
        name="step_logits",
    )(ends, head, lengths, *pays, *blocks)


def per_device(ctx_size, cand_size, prompt_q, prompt_kv, cand_q, cand_kv, cand_lengths, step_ends, reward_head):
    sizes = ctx_size, cand_size
    size = ctx_size * cand_size
    prompt_rows, cand_rows, own, pay, ends, head = staged(
        prompt_q, cand_q[0], prompt_kv, cand_kv[:, 0], step_ends, reward_head[None]
    )
    lengths = jnp.broadcast_to(cand_lengths[None], (1, HEADDIM))
    q_rows = prompt_rows, cand_rows
    early, along, across, core = prompt_bits(ctx_size, cand_size)

    def moved(block, bit):
        return flipped(block, PROMPT_AXES, size, bit)

    def shared_out(block, even, odd):
        return lax.ppermute(
            block, PROMPT_AXES, [(i, i ^ (odd if i & core else even)) for i in range(size)]
        )

    held, sent = own, prompt_kv
    for bit in early[:-1]:
        held = packed(held, moved(sent, bit))
        sent = held
    pay_masks = [0]
    for bit in early:
        if bit >= size // ctx_size:
            pay = packed(pay, moved(pay, bit))
            pay_masks += [mask ^ bit // cand_size for mask in pay_masks]
    beyond = moved(sent, early[-1])
    ways = along, across, along + across
    near = packed(moved(held, along), moved(held, across))
    facing = moved(held, along + across)
    past = [moved(beyond, bit) for bit in (along + across, across, along)]
    pay_across = moved(pay, across)
    both_pays = packed(pay, pay_across)
    pays = [both_pays, moved(both_pays, core)]
    masks = [mask ^ shift for shift in (0, 2, 1, 3) for mask in pay_masks]
    blocks = [held, beyond, near, facing] + past
    blocks += [moved(block, core) for block in blocks[:4]]
    state = phase(sizes, [2, 3, 4], q_rows, blocks)
    state = phase(sizes, [0, 1, 7, 8], q_rows, blocks, state=state)
    blocks.append(moved(packed(*past, after=state[:1]), core))
    state = phase(sizes, [5, 6], q_rows, blocks, pays=pays, masks=masks, state=state)
    step_logits = step_shares(sizes, ends, head, lengths, pays, masks, blocks)
    cand_out, prompt_out = phase(sizes, [9, 10, 11], q_rows, blocks, state=state, lengths=lengths)
    tp_size = lax.axis_size("tp")
    for bit in high_bits(tp_size, 1):
        step_logits = step_logits + flipped(step_logits, "tp", tp_size, bit)
    return (prompt_out, cand_out[None], step_logits)


def solution(mesh):
    placed = (
        P(("ctx", "cand"), "tp"),
        P(None, ("ctx", "cand"), "tp"),
        P("cand", "ctx", "tp"),
        P(None, "cand", "ctx", "tp"),
        P("cand"),
        P("cand", None),
        P("tp"),
    )
    return jax.shard_map(
        functools.partial(per_device, mesh.shape["ctx"], mesh.shape["cand"]),
        mesh=mesh,
        in_specs=placed,
        out_specs=(P(("ctx", "cand"), "tp"), P("cand", "ctx", "tp"), P("cand", None)),
        check_vma=False,
    )
```

```python
import functools
import math

import jax
import jax.numpy as jnp
from jax import lax
from jax.experimental import pallas as pl
from jax.experimental.pallas import tpu as pltpu
from jax.sharding import PartitionSpec as P

HEADDIM = 128
GROUP = 8
SUBLANES = 8
NEG_FILL = -1e30
SCALE = HEADDIM ** -0.5 * math.log2(math.e)
ROW_TILE = 256
VMEM_LIMIT = 28 * 1024 * 1024
PARAMS = pltpu.CompilerParams(vmem_limit_bytes=VMEM_LIMIT)
PROMPT_AXES = ("ctx", "cand")


def vmem(count):
    return [pl.BlockSpec(memory_space=pltpu.VMEM)] * count


def like(array):
    return jax.ShapeDtypeStruct(array.shape, array.dtype)


def high_bits(size, lowest):
    return [1 << b for b in reversed(range(size.bit_length() - 1)) if 1 << b >= lowest]


def flipped(block, axes, size, bit):
    return lax.ppermute(block, axes, [(i, i ^ bit) for i in range(size)])


def pack_kernel(count, *refs):
    sources, out_ref = refs[:count], refs[-1]
    start = 0
    for ref in sources:
        out_ref[start : start + ref.shape[0]] = ref[...]
        start += ref.shape[0]


def packed(*arrays, after=()):
    count = sum(a.shape[0] for a in arrays)
    return pl.pallas_call(
        functools.partial(pack_kernel, len(arrays)),
        out_shape=jax.ShapeDtypeStruct((count,) + arrays[0].shape[1:], arrays[0].dtype),
        in_specs=vmem(len(arrays)) + [pl.BlockSpec(memory_space=pl.ANY)] * len(after),
        out_specs=vmem(1)[0],
        compiler_params=PARAMS,
        name="pack_blocks",
    )(*arrays, *after)


def prompt_bits(ctx_size, cand_size):
    core, along, across = cand_size, 1, 2 * cand_size
    early = high_bits(cand_size, 2) + [bit * cand_size for bit in high_bits(ctx_size, 4)]
    return early, along, across, core


def prompt_owners(ctx_size, cand_size):
    early, along, across, core = prompt_bits(ctx_size, cand_size)
    place = lax.axis_index("ctx") * cand_size + lax.axis_index("cand")
    odd = lax.rem(lax.axis_index("ctx"), 2)
    near = along + odd * (across - along)
    far = along + across - near
    masks = [0]
    for bit in early:
        masks += [mask ^ bit for mask in masks]
    shifts = [0, near, far, along + across, core, core + far, core + near, core + along + across]
    return [[place ^ mask ^ shift for mask in masks] for shift in shifts]


def gather_cand(own, ctx_size):
    blocks = [(own, 0), (flipped(own, "ctx", ctx_size, 1), 1)]
    for bit in reversed(high_bits(ctx_size, 2)):
        rail = [(flipped(b, "ctx", ctx_size, bit), mask | bit) for b, mask in blocks if not mask & 1]
        blocks += rail + [(flipped(b, "ctx", ctx_size, 1), mask | 1) for b, mask in rail]
    return blocks


def stage_kernel(prompt_q, cand_q, prompt_kv, cand_kv, ends, head, *refs):
    q_out, cand_out, own_out, pay_out, ends_out, head_out, sems = refs
    steps = ends.shape[1]
    pairs = [
        (cand_q, cand_out),
        (ends, ends_out),
        (prompt_kv, own_out),
        (cand_kv, pay_out.at[0:2]),
        (prompt_q, q_out),
        (head, head_out),
    ]
    copies = [pltpu.make_async_copy(a, b, sems.at[i]) for i, (a, b) in enumerate(pairs)]
    for copy in copies:
        copy.start()
    copies[0].wait()
    copies[1].wait()
    rows = cand_out.shape[0]
    ends_column = column_of(ends_out[...])
    row_pos = lax.axis_index("ctx") * rows + lax.broadcasted_iota(jnp.int32, (steps, rows), 1)
    chosen = (row_pos == ends_column).astype(jnp.bfloat16)
    picked = jnp.dot(chosen, cand_out[...], preferred_element_type=jnp.float32)
    width = pay_out.shape[2]
    pieces = [picked[:, at : at + width] for at in range(0, picked.shape[1], width)]
    pay_out[2] = jnp.concatenate(pieces, axis=0).astype(jnp.bfloat16)
    for copy in copies[2:]:
        copy.wait()


def column_of(row):
    count = row.shape[1]
    down = lax.broadcasted_iota(jnp.int32, (count, count), 0)
    right = lax.broadcasted_iota(jnp.int32, (count, count), 1)
    return jnp.sum(jnp.where(down == right, row, 0), axis=1, keepdims=True)


def staged(prompt_q, cand_q, prompt_kv, cand_kv, ends, head):
    arrays = (prompt_q, cand_q, prompt_kv, cand_kv, ends, head)
    pay = jax.ShapeDtypeStruct((3,) + cand_kv.shape[1:], cand_kv.dtype)
    return pl.pallas_call(
        stage_kernel,
        out_shape=(like(prompt_q), like(cand_q), like(prompt_kv), pay, like(ends), like(head)),
        in_specs=[pl.BlockSpec(memory_space=pltpu.HBM)] * len(arrays),
        out_specs=tuple(vmem(6)),
        scratch_shapes=[pltpu.SemaphoreType.DMA((len(arrays),))],
        compiler_params=PARAMS,
        name="stage_operands",
    )(*(pltpu.with_memory_space_constraint(a, pltpu.HBM) for a in arrays))


def tiles(q_ref, head):
    rows = q_ref.shape[0]
    fan = max(1, ROW_TILE // rows)
    for start in range(head * GROUP, (head + 1) * GROUP, fan):
        heads = range(start, start + fan)
        queries = jnp.concatenate([q_ref[:, h * HEADDIM : (h + 1) * HEADDIM] for h in heads], axis=0)
        yield heads, slice(start * rows, (start + fan) * rows), queries


def stacked_rows(first_row, rows, count):
    return first_row + lax.rem(lax.broadcasted_iota(jnp.int32, (count, 1), 0), jnp.int32(rows))


def product(queries, key_rows):
    return lax.dot_general(
        queries, key_rows, (((1,), (1,)), ((), ())), preferred_element_type=jnp.float32
    )


def with_ones(value_rows):
    return jnp.concatenate([value_rows, jnp.ones_like(value_rows)], axis=1)


def head_rows(blocks, which, head):
    columns = slice(head * HEADDIM, (head + 1) * HEADDIM)
    return jnp.concatenate([ref[lead + (which,)][:, columns] for ref, lead in blocks], axis=0)


def key_positions(owners, rows):
    lane = lax.broadcasted_iota(jnp.int32, (1, len(owners) * rows), 1)
    positions = lane
    for index, owner in enumerate(owners):
        inside = (lane >= index * rows) & (lane < (index + 1) * rows)
        positions = jnp.where(inside, lane + (owner - index) * rows, positions)
    return positions


def spread(column, count):
    return jnp.concatenate([column] * (count // column.shape[1]), axis=1)


def absorb(queries, key_rows, widened, allowed, old):
    scores = product(queries, key_rows)
    if allowed is not None:
        scores = jnp.where(allowed, scores, NEG_FILL)
    count = scores.shape[1]
    peak = jnp.broadcast_to(jnp.max(scores, axis=1, keepdims=True), (scores.shape[0], HEADDIM))
    if old is not None:
        peak = jnp.maximum(peak, old[0])
    weights = jnp.exp2((scores - spread(peak, count)) * SCALE).astype(jnp.bfloat16)
    blended = jnp.dot(weights, widened, preferred_element_type=jnp.float32)
    if old is not None:
        blended += old[1] * spread(jnp.exp2((old[0] - peak) * SCALE), old[1].shape[1])
    return peak, blended


def prompt_place(cand_size):
    return lax.axis_index("ctx") * cand_size + lax.axis_index("cand")


def pairs_of(refs):
    return [(ref, (index,)) for ref in refs for index in range(ref.shape[0])]


def phase_kernel(sizes, arrays, masks, first, last, *refs):
    ctx_size, cand_size = sizes
    take = iter(refs)
    prompt_q, cand_q = next(take), next(take)
    block_refs = [next(take) for _ in arrays]
    pays = [next(take) for _ in masks]
    lengths = next(take) if last else None
    old = None if first else [(next(take), next(take)) for _ in range(2)]
    outs = refs[-2:] if last else refs[-4:]
    rows = prompt_q.shape[0]
    cand_rows = cand_q.shape[0]
    owners = prompt_owners(ctx_size, cand_size)
    key_pos = key_positions([place for index in arrays for place in owners[index]], rows)
    blocks = pairs_of(block_refs)
    own = [(ref, ()) for ref in pays]
    ctx = lax.axis_index("ctx")
    own_pos = key_positions([ctx ^ mask for mask in masks], cand_rows) if masks else None
    alive = stacked_rows(ctx * cand_rows, cand_rows, cand_rows) < lengths[:, :1] if last else None

    for head in range(block_refs[0].shape[3] // HEADDIM):
        key_rows = head_rows(blocks, 0, head)
        widened = with_ones(head_rows(blocks, 1, head))
        if masks:
            all_keys = jnp.concatenate([key_rows, head_rows(own, 0, head)], axis=0)
            all_widened = jnp.concatenate([widened, with_ones(head_rows(own, 1, head))], axis=0)
            free = jnp.full((1, key_rows.shape[0]), -1, jnp.int32)
            all_pos = jnp.concatenate([free, own_pos], axis=1)
        for kind, q_ref in enumerate((cand_q, prompt_q)):
            for heads, at, queries in tiles(q_ref, head):
                count = queries.shape[0]
                state = None if first else (old[kind][0][at], old[kind][1][at])
                if kind == 1:
                    first_row = prompt_place(cand_size) * rows
                    allowed = key_pos <= stacked_rows(first_row, rows, count)
                    state = absorb(queries, key_rows, widened, allowed, state)
                elif masks:
                    allowed = all_pos <= stacked_rows(ctx * cand_rows, cand_rows, count)
                    state = absorb(queries, all_keys, all_widened, allowed, state)
                else:
                    state = absorb(queries, key_rows, widened, None, state)
                if not last:
                    outs[2 * kind][at] = state[0]
                    outs[2 * kind + 1][at] = state[1]
                    continue
                result = state[1][:, :HEADDIM] / state[1][:, HEADDIM:]
                each = q_ref.shape[0]
                for index, h in enumerate(heads):
                    kept = result[index * each : (index + 1) * each]
                    if kind == 0:
                        kept = jnp.where(alive, kept, 0.0)
                    outs[kind][:, h * HEADDIM : (h + 1) * HEADDIM] = kept.astype(jnp.bfloat16)


def phase(sizes, arrays, q_rows, blocks, pays=(), state=None, lengths=None, after=()):
    prompt_q, cand_q = q_rows
    first, last = state is None, lengths is not None
    operands = [prompt_q, cand_q] + [blocks[index] for index in arrays]
    operands += [b for b, _ in pays]
    if last:
        operands.append(lengths)
    if not first:
        operands += state
    heads = prompt_q.shape[1] // HEADDIM
    if last:
        shapes = [like(cand_q), like(prompt_q)]
    else:
        shapes = []
        for q in (cand_q, prompt_q):
            count = heads * q.shape[0]
            shapes.append(jax.ShapeDtypeStruct((count, HEADDIM), jnp.float32))
            shapes.append(jax.ShapeDtypeStruct((count, 2 * HEADDIM), jnp.float32))
    key_count = sum(blocks[i].shape[0] * blocks[i].shape[2] for i in arrays)
    scores = heads * (prompt_q.shape[0] + cand_q.shape[0]) * key_count
    masks = [mask for _, mask in pays]
    return pl.pallas_call(
        functools.partial(phase_kernel, sizes, arrays, masks, first, last),
        out_shape=tuple(shapes),
        in_specs=vmem(len(operands)) + [pl.BlockSpec(memory_space=pl.ANY)] * len(after),
        out_specs=tuple(vmem(len(shapes))),
        compiler_params=PARAMS,
        cost_estimate=pl.CostEstimate(
            flops=6 * scores * HEADDIM, bytes_accessed=scores, transcendentals=scores
        ),
        name="attend_" + "_".join(str(i) for i in arrays),
    )(*operands, *after)


def placed_blocks(sizes, arrays, refs, kv_ref):
    owners = prompt_owners(*sizes)
    for ref, array in zip(refs, arrays):
        rows = ref.shape[2]
        for index, owner in enumerate(owners[array]):
            at = pl.ds(pl.multiple_of(owner * rows, rows), rows)
            kv_ref[0, at, :] = ref[index, 0]
            kv_ref[1, at, :] = ref[index, 1]


def arrange_kernel(sizes, arrays, masks, *refs):
    pays, blocks = refs[: len(masks)], refs[len(masks) : -2]
    kv_ref, query_ref = refs[-2:]
    placed_blocks(sizes, arrays, blocks, kv_ref)
    rows, width = pays[0].shape[1:]
    free = kv_ref.shape[1] - rows * len(masks)
    picked = jnp.zeros((rows, width), jnp.float32)
    for ref, mask in zip(pays, masks):
        at = pl.ds(pl.multiple_of(free + (lax.axis_index("ctx") ^ mask) * rows, rows), rows)
        kv_ref[0, at, :] = ref[0]
        kv_ref[1, at, :] = ref[1]
        picked += ref[2].astype(jnp.float32)
    heads = query_ref.shape[0]
    steps = rows * width // (heads * HEADDIM)
    for head in range(heads):
        group, lane = divmod(head * HEADDIM, width)
        query_ref[head] = picked[group * steps : (group + 1) * steps, lane : lane + HEADDIM]


def arranged(sizes, arrays, heads, steps, pays, blocks):
    rows, width = pays[0][0].shape[1:]
    count = rows * sizes[0] * (sizes[1] + 1)
    return pl.pallas_call(
        functools.partial(arrange_kernel, sizes, arrays, [mask for _, mask in pays]),
        out_shape=(
            jax.ShapeDtypeStruct((2, count, width), pays[0][0].dtype),
            jax.ShapeDtypeStruct((heads, steps, HEADDIM), jnp.float32),
        ),
        in_specs=vmem(len(pays) + len(arrays)),
        out_specs=tuple(vmem(2)),
        compiler_params=PARAMS,
        name="arrange_blocks",
    )(*(b for b, _ in pays), *(blocks[index] for index in arrays))


def step_kernel(sizes, arrays, ends_ref, head_ref, lengths_ref, query_ref, _, *refs):
    blocks = refs[:-2]
    logit_ref, kv_ref = refs[-2:]
    placed_blocks(sizes, arrays, blocks, kv_ref)
    own_count = blocks[0].shape[2] * sizes[0]
    free = kv_ref.shape[1] - own_count
    steps = ends_ref.shape[1]
    ends = column_of(ends_ref[...])
    own_pos = lax.broadcasted_iota(jnp.int32, (1, own_count), 1)
    row_pos = jnp.concatenate([ends] * GROUP, axis=0)
    total = jnp.zeros((steps, HEADDIM), jnp.float32)
    for head in range(kv_ref.shape[2] // HEADDIM):
        columns = slice(head * HEADDIM, (head + 1) * HEADDIM)
        heads = range(head * GROUP, (head + 1) * GROUP)
        queries = jnp.concatenate([query_ref[h] for h in heads], axis=0)
        scores = product(queries.astype(jnp.bfloat16), kv_ref[0, :, columns])
        bound = jnp.where(own_pos <= row_pos, scores[:, free:], NEG_FILL)
        scores = jnp.concatenate([scores[:, :free], bound], axis=1)
        peak = jnp.max(scores, axis=1, keepdims=True)
        weights = jnp.exp2((scores - peak) * SCALE).astype(jnp.bfloat16)
        blended = jnp.dot(weights, with_ones(kv_ref[1, :, columns]), preferred_element_type=jnp.float32)
        result = blended[:, :HEADDIM] / blended[:, HEADDIM:]
        for index, h in enumerate(heads):
            kept = jnp.where(ends < lengths_ref[:, :1], result[index * steps : (index + 1) * steps], 0.0)
            kept = kept.astype(jnp.bfloat16).astype(jnp.float32)
            total += kept * head_ref[:, h * HEADDIM : (h + 1) * HEADDIM]
    logits = jnp.sum(total, axis=1, keepdims=True)
    down = lax.broadcasted_iota(jnp.int32, (steps, steps), 0)
    right = lax.broadcasted_iota(jnp.int32, (steps, steps), 1)
    logit_ref[...] = jnp.sum(jnp.where(down == right, logits, 0.0), axis=0, keepdims=True)


def step_shares(sizes, arrays, ends, head, lengths, queries, kv, blocks):
    scores = queries.shape[0] * queries.shape[1] * kv.shape[1]
    return pl.pallas_call(
        functools.partial(step_kernel, sizes, arrays),
        out_shape=(jax.ShapeDtypeStruct(ends.shape, jnp.float32), like(kv)),
        in_specs=vmem(5 + len(arrays)),
        out_specs=tuple(vmem(2)),
        input_output_aliases={4: 1},
        compiler_params=PARAMS,
        cost_estimate=pl.CostEstimate(
            flops=6 * scores * HEADDIM, bytes_accessed=scores, transcendentals=scores
        ),
        name="step_logits",
    )(ends, head, lengths, queries, kv, *(blocks[index] for index in arrays))[0]


def per_device(ctx_size, cand_size, prompt_q, prompt_kv, cand_q, cand_kv, cand_lengths, step_ends, reward_head):
    sizes = ctx_size, cand_size
    size = ctx_size * cand_size
    prompt_rows, cand_rows, own, payload, ends, head = staged(
        prompt_q, cand_q[0], prompt_kv, cand_kv[:, 0], step_ends, reward_head[None]
    )
    lengths = jnp.broadcast_to(cand_lengths[None], (1, HEADDIM))
    q_rows = prompt_rows, cand_rows
    pays = gather_cand(payload, ctx_size)
    early, along, across, core = prompt_bits(ctx_size, cand_size)

    def across_cores(block):
        return flipped(block, PROMPT_AXES, size, core)

    def shared_out(block, even, odd):
        return lax.ppermute(
            block, PROMPT_AXES, [(i, i ^ (odd if i & core else even)) for i in range(size)]
        )

    held = own[None]
    sent = prompt_kv[None]
    for bit in early:
        held = packed(held, flipped(sent, PROMPT_AXES, size, bit))
        sent = held
    second = shared_out(held, along, across)
    third = shared_out(held, across, along)
    blocks = [held, second, third, None, across_cores(held), None, None, None]
    state = phase(sizes, [0, 4], q_rows, blocks)
    fourth = shared_out(packed(second, after=[b for b, _ in pays[1:4]]), across, along)
    blocks[3] = fourth
    blocks[5:7] = across_cores(second), across_cores(third)
    state = phase(sizes, [1, 2], q_rows, blocks, pays=pays, state=state)
    blocks[7] = across_cores(packed(fourth, after=state[:1]))
    state = phase(sizes, [5, 6], q_rows, blocks, state=state)
    heads = head.shape[1] // HEADDIM
    kv, queries = arranged(sizes, [0, 1, 2, 4, 5, 6], heads, step_ends.shape[1], pays, blocks)
    step_logits = step_shares(sizes, [3, 7], ends, head, lengths, queries, kv, blocks)
    cand_out, prompt_out = phase(sizes, [3, 7], q_rows, blocks, state=state, lengths=lengths)
    tp_size = lax.axis_size("tp")
    for bit in high_bits(tp_size, 1):
        step_logits = step_logits + flipped(step_logits, "tp", tp_size, bit)
    return (prompt_out, cand_out[None], step_logits)


def solution(mesh):
    placed = (
        P(("ctx", "cand"), "tp"),
        P(None, ("ctx", "cand"), "tp"),
        P("cand", "ctx", "tp"),
        P(None, "cand", "ctx", "tp"),
        P("cand"),
        P("cand", None),
        P("tp"),
    )
    return jax.shard_map(
        functools.partial(per_device, mesh.shape["ctx"], mesh.shape["cand"]),
        mesh=mesh,
        in_specs=placed,
        out_specs=(P(("ctx", "cand"), "tp"), P("cand", "ctx", "tp"), P("cand", None)),
        check_vma=False,
    )
```

```python
import functools
import math

import jax
import jax.numpy as jnp
from jax import lax
from jax.experimental import pallas as pl
from jax.experimental.pallas import tpu as pltpu
from jax.sharding import PartitionSpec as P

HEADDIM = 128
GROUP = 8
SUBLANES = 8
NEG_FILL = -1e30
SCALE = HEADDIM ** -0.5 * math.log2(math.e)
ROW_TILE = 256
VMEM_LIMIT = 28 * 1024 * 1024
PARAMS = pltpu.CompilerParams(vmem_limit_bytes=VMEM_LIMIT)
PROMPT_AXES = ("ctx", "cand")


def vmem(count):
    return [pl.BlockSpec(memory_space=pltpu.VMEM)] * count


def like(array):
    return jax.ShapeDtypeStruct(array.shape, array.dtype)


def high_bits(size, lowest):
    return [1 << b for b in reversed(range(size.bit_length() - 1)) if 1 << b >= lowest]


def flipped(block, axes, size, bit):
    return lax.ppermute(block, axes, [(i, i ^ bit) for i in range(size)])


def pack_kernel(count, *refs):
    sources, out_ref = refs[:count], refs[-1]
    start = 0
    for ref in sources:
        out_ref[start : start + ref.shape[0]] = ref[...]
        start += ref.shape[0]


def packed(*arrays, after=()):
    count = sum(a.shape[0] for a in arrays)
    return pl.pallas_call(
        functools.partial(pack_kernel, len(arrays)),
        out_shape=jax.ShapeDtypeStruct((count,) + arrays[0].shape[1:], arrays[0].dtype),
        in_specs=vmem(len(arrays)) + [pl.BlockSpec(memory_space=pl.ANY)] * len(after),
        out_specs=vmem(1)[0],
        compiler_params=PARAMS,
        name="pack_blocks",
    )(*arrays, *after)


def prompt_bits(ctx_size, cand_size):
    core, along, across = cand_size, 1, 2 * cand_size
    early = high_bits(cand_size, 2) + [bit * cand_size for bit in high_bits(ctx_size, 4)]
    return early, along, across, core


def prompt_owners(ctx_size, cand_size):
    early, along, across, core = prompt_bits(ctx_size, cand_size)
    place = lax.axis_index("ctx") * cand_size + lax.axis_index("cand")
    odd = lax.rem(lax.axis_index("ctx"), 2)
    masks = [0]
    for bit in early[:-1]:
        masks += [mask ^ bit for mask in masks]
    owners = []
    for side, other in ((odd, 0), (1 - odd, core)):
        first, second, third = (
            even + side * (uneven - even)
            for even, uneven in ((along, early[-1]), (early[-1], across), (across, along))
        )
        for shift in (0, second, third, second ^ third):
            owners.append([place ^ other ^ shift ^ step ^ mask for step in (0, first) for mask in masks])
    return owners


def gather_cand(own, ctx_size):
    blocks = [(own, 0), (flipped(own, "ctx", ctx_size, 1), 1)]
    for bit in reversed(high_bits(ctx_size, 2)):
        rail = [(flipped(b, "ctx", ctx_size, bit), mask | bit) for b, mask in blocks if not mask & 1]
        blocks += rail + [(flipped(b, "ctx", ctx_size, 1), mask | 1) for b, mask in rail]
    return blocks


def stage_kernel(prompt_q, cand_q, prompt_kv, cand_kv, ends, head, *refs):
    q_out, cand_out, own_out, pay_out, ends_out, head_out, sems = refs
    steps = ends.shape[1]
    pairs = [
        (cand_q, cand_out),
        (ends, ends_out),
        (prompt_kv, own_out),
        (cand_kv, pay_out.at[0:2]),
        (prompt_q, q_out),
        (head, head_out),
    ]
    copies = [pltpu.make_async_copy(a, b, sems.at[i]) for i, (a, b) in enumerate(pairs)]
    for copy in copies:
        copy.start()
    copies[0].wait()
    copies[1].wait()
    rows = cand_out.shape[0]
    ends_column = column_of(ends_out[...])
    row_pos = lax.axis_index("ctx") * rows + lax.broadcasted_iota(jnp.int32, (steps, rows), 1)
    chosen = (row_pos == ends_column).astype(jnp.bfloat16)
    picked = jnp.dot(chosen, cand_out[...], preferred_element_type=jnp.float32)
    width = pay_out.shape[2]
    pieces = [picked[:, at : at + width] for at in range(0, picked.shape[1], width)]
    pay_out[2] = jnp.concatenate(pieces, axis=0).astype(jnp.bfloat16)
    for copy in copies[2:]:
        copy.wait()


def column_of(row):
    count = row.shape[1]
    down = lax.broadcasted_iota(jnp.int32, (count, count), 0)
    right = lax.broadcasted_iota(jnp.int32, (count, count), 1)
    return jnp.sum(jnp.where(down == right, row, 0), axis=1, keepdims=True)


def staged(prompt_q, cand_q, prompt_kv, cand_kv, ends, head):
    arrays = (prompt_q, cand_q, prompt_kv, cand_kv, ends, head)
    pay = jax.ShapeDtypeStruct((3,) + cand_kv.shape[1:], cand_kv.dtype)
    return pl.pallas_call(
        stage_kernel,
        out_shape=(like(prompt_q), like(cand_q), like(prompt_kv), pay, like(ends), like(head)),
        in_specs=[pl.BlockSpec(memory_space=pltpu.HBM)] * len(arrays),
        out_specs=tuple(vmem(6)),
        scratch_shapes=[pltpu.SemaphoreType.DMA((len(arrays),))],
        compiler_params=PARAMS,
        name="stage_operands",
    )(*(pltpu.with_memory_space_constraint(a, pltpu.HBM) for a in arrays))


def tiles(q_ref, head):
    rows = q_ref.shape[0]
    fan = max(1, ROW_TILE // rows)
    for start in range(head * GROUP, (head + 1) * GROUP, fan):
        heads = range(start, start + fan)
        queries = jnp.concatenate([q_ref[:, h * HEADDIM : (h + 1) * HEADDIM] for h in heads], axis=0)
        yield heads, slice(start * rows, (start + fan) * rows), queries


def stacked_rows(first_row, rows, count):
    return first_row + lax.rem(lax.broadcasted_iota(jnp.int32, (count, 1), 0), jnp.int32(rows))


def product(queries, key_rows):
    return lax.dot_general(
        queries, key_rows, (((1,), (1,)), ((), ())), preferred_element_type=jnp.float32
    )


def with_ones(value_rows):
    return jnp.concatenate([value_rows, jnp.ones_like(value_rows)], axis=1)


def head_rows(blocks, which, head):
    columns = slice(head * HEADDIM, (head + 1) * HEADDIM)
    return jnp.concatenate([ref[lead + (which,)][:, columns] for ref, lead in blocks], axis=0)


def key_positions(owners, rows):
    lane = lax.broadcasted_iota(jnp.int32, (1, len(owners) * rows), 1)
    positions = lane
    for index, owner in enumerate(owners):
        inside = (lane >= index * rows) & (lane < (index + 1) * rows)
        positions = jnp.where(inside, lane + (owner - index) * rows, positions)
    return positions


def spread(column, count):
    return jnp.concatenate([column] * (count // column.shape[1]), axis=1)


def absorb(queries, key_rows, widened, allowed, old):
    scores = product(queries, key_rows)
    if allowed is not None:
        scores = jnp.where(allowed, scores, NEG_FILL)
    count = scores.shape[1]
    peak = jnp.broadcast_to(jnp.max(scores, axis=1, keepdims=True), (scores.shape[0], HEADDIM))
    if old is not None:
        peak = jnp.maximum(peak, old[0])
    weights = jnp.exp2((scores - spread(peak, count)) * SCALE).astype(jnp.bfloat16)
    blended = jnp.dot(weights, widened, preferred_element_type=jnp.float32)
    if old is not None:
        blended += old[1] * spread(jnp.exp2((old[0] - peak) * SCALE), old[1].shape[1])
    return peak, blended


def prompt_place(cand_size):
    return lax.axis_index("ctx") * cand_size + lax.axis_index("cand")


def pairs_of(refs):
    return [(ref, (index,)) for ref in refs for index in range(ref.shape[0])]


def phase_kernel(sizes, arrays, masks, first, last, *refs):
    ctx_size, cand_size = sizes
    take = iter(refs)
    prompt_q, cand_q = next(take), next(take)
    block_refs = [next(take) for _ in arrays]
    pays = [next(take) for _ in masks]
    lengths = next(take) if last else None
    old = None if first else [(next(take), next(take)) for _ in range(2)]
    outs = refs[-2:] if last else refs[-4:]
    rows = prompt_q.shape[0]
    cand_rows = cand_q.shape[0]
    owners = prompt_owners(ctx_size, cand_size)
    key_pos = key_positions([place for index in arrays for place in owners[index]], rows)
    blocks = pairs_of(block_refs)
    own = [(ref, ()) for ref in pays]
    ctx = lax.axis_index("ctx")
    own_pos = key_positions([ctx ^ mask for mask in masks], cand_rows) if masks else None
    alive = stacked_rows(ctx * cand_rows, cand_rows, cand_rows) < lengths[:, :1] if last else None

    for head in range(block_refs[0].shape[3] // HEADDIM):
        key_rows = head_rows(blocks, 0, head)
        widened = with_ones(head_rows(blocks, 1, head))
        if masks:
            all_keys = jnp.concatenate([key_rows, head_rows(own, 0, head)], axis=0)
            all_widened = jnp.concatenate([widened, with_ones(head_rows(own, 1, head))], axis=0)
            free = jnp.full((1, key_rows.shape[0]), -1, jnp.int32)
            all_pos = jnp.concatenate([free, own_pos], axis=1)
        for kind, q_ref in enumerate((cand_q, prompt_q)):
            for heads, at, queries in tiles(q_ref, head):
                count = queries.shape[0]
                state = None if first else (old[kind][0][at], old[kind][1][at])
                if kind == 1:
                    first_row = prompt_place(cand_size) * rows
                    allowed = key_pos <= stacked_rows(first_row, rows, count)
                    state = absorb(queries, key_rows, widened, allowed, state)
                elif masks:
                    allowed = all_pos <= stacked_rows(ctx * cand_rows, cand_rows, count)
                    state = absorb(queries, all_keys, all_widened, allowed, state)
                else:
                    state = absorb(queries, key_rows, widened, None, state)
                if not last:
                    outs[2 * kind][at] = state[0]
                    outs[2 * kind + 1][at] = state[1]
                    continue
                result = state[1][:, :HEADDIM] / state[1][:, HEADDIM:]
                each = q_ref.shape[0]
                for index, h in enumerate(heads):
                    kept = result[index * each : (index + 1) * each]
                    if kind == 0:
                        kept = jnp.where(alive, kept, 0.0)
                    outs[kind][:, h * HEADDIM : (h + 1) * HEADDIM] = kept.astype(jnp.bfloat16)


def phase(sizes, arrays, q_rows, blocks, pays=(), state=None, lengths=None, after=()):
    prompt_q, cand_q = q_rows
    first, last = state is None, lengths is not None
    operands = [prompt_q, cand_q] + [blocks[index] for index in arrays]
    operands += [b for b, _ in pays]
    if last:
        operands.append(lengths)
    if not first:
        operands += state
    heads = prompt_q.shape[1] // HEADDIM
    if last:
        shapes = [like(cand_q), like(prompt_q)]
    else:
        shapes = []
        for q in (cand_q, prompt_q):
            count = heads * q.shape[0]
            shapes.append(jax.ShapeDtypeStruct((count, HEADDIM), jnp.float32))
            shapes.append(jax.ShapeDtypeStruct((count, 2 * HEADDIM), jnp.float32))
    key_count = sum(blocks[i].shape[0] * blocks[i].shape[2] for i in arrays)
    scores = heads * (prompt_q.shape[0] + cand_q.shape[0]) * key_count
    masks = [mask for _, mask in pays]
    return pl.pallas_call(
        functools.partial(phase_kernel, sizes, arrays, masks, first, last),
        out_shape=tuple(shapes),
        in_specs=vmem(len(operands)) + [pl.BlockSpec(memory_space=pl.ANY)] * len(after),
        out_specs=tuple(vmem(len(shapes))),
        compiler_params=PARAMS,
        cost_estimate=pl.CostEstimate(
            flops=6 * scores * HEADDIM, bytes_accessed=scores, transcendentals=scores
        ),
        name="attend_" + "_".join(str(i) for i in arrays),
    )(*operands, *after)


def placed_blocks(sizes, arrays, refs, kv_ref):
    owners = prompt_owners(*sizes)
    for ref, array in zip(refs, arrays):
        rows = ref.shape[2]
        for index, owner in enumerate(owners[array]):
            at = pl.ds(pl.multiple_of(owner * rows, rows), rows)
            kv_ref[0, at, :] = ref[index, 0]
            kv_ref[1, at, :] = ref[index, 1]


def arrange_kernel(sizes, arrays, masks, *refs):
    pays, blocks = refs[: len(masks)], refs[len(masks) : -2]
    kv_ref, query_ref = refs[-2:]
    placed_blocks(sizes, arrays, blocks, kv_ref)
    rows, width = pays[0].shape[1:]
    free = kv_ref.shape[1] - rows * len(masks)
    picked = jnp.zeros((rows, width), jnp.float32)
    for ref, mask in zip(pays, masks):
        at = pl.ds(pl.multiple_of(free + (lax.axis_index("ctx") ^ mask) * rows, rows), rows)
        kv_ref[0, at, :] = ref[0]
        kv_ref[1, at, :] = ref[1]
        picked += ref[2].astype(jnp.float32)
    heads = query_ref.shape[0]
    steps = rows * width // (heads * HEADDIM)
    for head in range(heads):
        group, lane = divmod(head * HEADDIM, width)
        query_ref[head] = picked[group * steps : (group + 1) * steps, lane : lane + HEADDIM]


def arranged(sizes, arrays, heads, steps, pays, blocks):
    rows, width = pays[0][0].shape[1:]
    count = rows * sizes[0] * (sizes[1] + 1)
    return pl.pallas_call(
        functools.partial(arrange_kernel, sizes, arrays, [mask for _, mask in pays]),
        out_shape=(
            jax.ShapeDtypeStruct((2, count, width), pays[0][0].dtype),
            jax.ShapeDtypeStruct((heads, steps, HEADDIM), jnp.float32),
        ),
        in_specs=vmem(len(pays) + len(arrays)),
        out_specs=tuple(vmem(2)),
        compiler_params=PARAMS,
        name="arrange_blocks",
    )(*(b for b, _ in pays), *(blocks[index] for index in arrays))


def step_kernel(sizes, arrays, ends_ref, head_ref, lengths_ref, query_ref, _, *refs):
    blocks = refs[:-2]
    logit_ref, kv_ref = refs[-2:]
    placed_blocks(sizes, arrays, blocks, kv_ref)
    own_count = blocks[0].shape[2] * sizes[0]
    free = kv_ref.shape[1] - own_count
    steps = ends_ref.shape[1]
    ends = column_of(ends_ref[...])
    own_pos = lax.broadcasted_iota(jnp.int32, (1, own_count), 1)
    row_pos = jnp.concatenate([ends] * GROUP, axis=0)
    total = jnp.zeros((steps, HEADDIM), jnp.float32)
    for head in range(kv_ref.shape[2] // HEADDIM):
        columns = slice(head * HEADDIM, (head + 1) * HEADDIM)
        heads = range(head * GROUP, (head + 1) * GROUP)
        queries = jnp.concatenate([query_ref[h] for h in heads], axis=0)
        scores = product(queries.astype(jnp.bfloat16), kv_ref[0, :, columns])
        bound = jnp.where(own_pos <= row_pos, scores[:, free:], NEG_FILL)
        scores = jnp.concatenate([scores[:, :free], bound], axis=1)
        peak = jnp.max(scores, axis=1, keepdims=True)
        weights = jnp.exp2((scores - peak) * SCALE).astype(jnp.bfloat16)
        blended = jnp.dot(weights, with_ones(kv_ref[1, :, columns]), preferred_element_type=jnp.float32)
        result = blended[:, :HEADDIM] / blended[:, HEADDIM:]
        for index, h in enumerate(heads):
            kept = jnp.where(ends < lengths_ref[:, :1], result[index * steps : (index + 1) * steps], 0.0)
            kept = kept.astype(jnp.bfloat16).astype(jnp.float32)
            total += kept * head_ref[:, h * HEADDIM : (h + 1) * HEADDIM]
    logits = jnp.sum(total, axis=1, keepdims=True)
    down = lax.broadcasted_iota(jnp.int32, (steps, steps), 0)
    right = lax.broadcasted_iota(jnp.int32, (steps, steps), 1)
    logit_ref[...] = jnp.sum(jnp.where(down == right, logits, 0.0), axis=0, keepdims=True)


def step_shares(sizes, arrays, ends, head, lengths, queries, kv, blocks):
    scores = queries.shape[0] * queries.shape[1] * kv.shape[1]
    return pl.pallas_call(
        functools.partial(step_kernel, sizes, arrays),
        out_shape=(jax.ShapeDtypeStruct(ends.shape, jnp.float32), like(kv)),
        in_specs=vmem(5 + len(arrays)),
        out_specs=tuple(vmem(2)),
        input_output_aliases={4: 1},
        compiler_params=PARAMS,
        cost_estimate=pl.CostEstimate(
            flops=6 * scores * HEADDIM, bytes_accessed=scores, transcendentals=scores
        ),
        name="step_logits",
    )(ends, head, lengths, queries, kv, *(blocks[index] for index in arrays))[0]


def per_device(ctx_size, cand_size, prompt_q, prompt_kv, cand_q, cand_kv, cand_lengths, step_ends, reward_head):
    sizes = ctx_size, cand_size
    size = ctx_size * cand_size
    prompt_rows, cand_rows, own, payload, ends, head = staged(
        prompt_q, cand_q[0], prompt_kv, cand_kv[:, 0], step_ends, reward_head[None]
    )
    lengths = jnp.broadcast_to(cand_lengths[None], (1, HEADDIM))
    q_rows = prompt_rows, cand_rows
    pays = gather_cand(payload, ctx_size)
    early, along, across, core = prompt_bits(ctx_size, cand_size)

    def across_cores(block):
        return flipped(block, PROMPT_AXES, size, core)

    def shared_out(block, even, odd):
        return lax.ppermute(
            block, PROMPT_AXES, [(i, i ^ (odd if i & core else even)) for i in range(size)]
        )

    held, sent = own[None], prompt_kv[None]
    for bit in early[:-1]:
        held = packed(held, flipped(sent, PROMPT_AXES, size, bit))
        sent = held
    held = packed(held, shared_out(sent, along, early[-1]))
    second = shared_out(held, early[-1], across)
    third = shared_out(held, across, along)
    blocks = [held, second, third, None, across_cores(held), None, None, None]
    state = phase(sizes, [0, 4], q_rows, blocks)
    fourth = shared_out(packed(second, after=state[:1] + tuple(b for b, _ in pays[1:4])), across, along)
    blocks[3] = fourth
    blocks[5:7] = across_cores(second), across_cores(third)
    state = phase(sizes, [1, 2], q_rows, blocks, pays=pays, state=state)
    blocks[7] = across_cores(packed(fourth, after=state[:1]))
    state = phase(sizes, [5, 6], q_rows, blocks, state=state)
    heads = head.shape[1] // HEADDIM
    kv, queries = arranged(sizes, [0, 1, 2, 4, 5, 6], heads, step_ends.shape[1], pays, blocks)
    step_logits = step_shares(sizes, [3, 7], ends, head, lengths, queries, kv, blocks)
    cand_out, prompt_out = phase(sizes, [3, 7], q_rows, blocks, state=state, lengths=lengths)
    tp_size = lax.axis_size("tp")
    for bit in high_bits(tp_size, 1):
        step_logits = step_logits + flipped(step_logits, "tp", tp_size, bit)
    return (prompt_out, cand_out[None], step_logits)


def solution(mesh):
    placed = (
        P(("ctx", "cand"), "tp"),
        P(None, ("ctx", "cand"), "tp"),
        P("cand", "ctx", "tp"),
        P(None, "cand", "ctx", "tp"),
        P("cand"),
        P("cand", None),
        P("tp"),
    )
    return jax.shard_map(
        functools.partial(per_device, mesh.shape["ctx"], mesh.shape["cand"]),
        mesh=mesh,
        in_specs=placed,
        out_specs=(P(("ctx", "cand"), "tp"), P("cand", "ctx", "tp"), P("cand", None)),
        check_vma=False,
    )
```

```python
import functools
import math

import jax
import jax.numpy as jnp
from jax import lax
from jax.experimental import pallas as pl
from jax.experimental.pallas import tpu as pltpu
from jax.sharding import PartitionSpec as P

HEADDIM = 128
GROUP = 8
SUBLANES = 8
NEG_FILL = -1e30
GROUPS = 4
SCALE = HEADDIM ** -0.5 * math.log2(math.e)
ROW_TILE = 256
VMEM_LIMIT = 28 * 1024 * 1024
PARAMS = pltpu.CompilerParams(vmem_limit_bytes=VMEM_LIMIT)
PROMPT_AXES = ("ctx", "cand")


def vmem(count):
    return [pl.BlockSpec(memory_space=pltpu.VMEM)] * count


def like(array):
    return jax.ShapeDtypeStruct(array.shape, array.dtype)


def high_bits(size, lowest):
    return [1 << b for b in reversed(range(size.bit_length() - 1)) if 1 << b >= lowest]


def flipped(block, axes, size, bit):
    return lax.ppermute(block, axes, [(i, i ^ bit) for i in range(size)])


def pack_kernel(count, *refs):
    sources, out_ref = refs[:count], refs[-1]
    start = 0
    for ref in sources:
        out_ref[start : start + ref.shape[0]] = ref[...]
        start += ref.shape[0]


def packed(*arrays, after=()):
    count = sum(a.shape[0] for a in arrays)
    return pl.pallas_call(
        functools.partial(pack_kernel, len(arrays)),
        out_shape=jax.ShapeDtypeStruct((count,) + arrays[0].shape[1:], arrays[0].dtype),
        in_specs=vmem(len(arrays)) + [pl.BlockSpec(memory_space=pl.ANY)] * len(after),
        out_specs=vmem(1)[0],
        compiler_params=PARAMS,
        name="pack_blocks",
    )(*arrays, *after)


def prompt_bits(ctx_size, cand_size):
    core, along, across = cand_size, 1, 2 * cand_size
    early = high_bits(cand_size, 2) + [bit * cand_size for bit in high_bits(ctx_size, 4)]
    return early, along, across, core


def prompt_owners(ctx_size, cand_size):
    early, along, across, core = prompt_bits(ctx_size, cand_size)
    place = lax.axis_index("ctx") * cand_size + lax.axis_index("cand")
    odd = lax.rem(lax.axis_index("ctx"), 2)
    near = along + odd * (across - along)
    far = along + across - near
    masks = [0]
    for bit in early:
        masks += [mask ^ bit for mask in masks]
    shifts = [0, near, far, along + across, core, core + far, core + near, core + along + across]
    return [[place ^ mask ^ shift for mask in masks] for shift in shifts]


def gather_cand(own, ctx_size):
    blocks = [(own, 0), (flipped(own, "ctx", ctx_size, 1), 1)]
    for bit in reversed(high_bits(ctx_size, 2)):
        rail = [(flipped(b, "ctx", ctx_size, bit), mask | bit) for b, mask in blocks if not mask & 1]
        blocks += rail + [(flipped(b, "ctx", ctx_size, 1), mask | 1) for b, mask in rail]
    return blocks


def stage_kernel(prompt_q, cand_q, prompt_kv, cand_kv, ends, head, *refs):
    q_out, cand_out, own_out, pay_out, ends_out, head_out, sems = refs
    steps = ends.shape[1]
    pairs = [
        (cand_q, cand_out),
        (ends, ends_out),
        (prompt_kv, own_out),
        (cand_kv, pay_out.at[0:2]),
        (prompt_q, q_out),
        (head, head_out),
    ]
    copies = [pltpu.make_async_copy(a, b, sems.at[i]) for i, (a, b) in enumerate(pairs)]
    for copy in copies:
        copy.start()
    copies[0].wait()
    copies[1].wait()
    rows = cand_out.shape[0]
    ends_column = column_of(ends_out[...])
    row_pos = lax.axis_index("ctx") * rows + lax.broadcasted_iota(jnp.int32, (steps, rows), 1)
    chosen = (row_pos == ends_column).astype(jnp.bfloat16)
    picked = jnp.dot(chosen, cand_out[...], preferred_element_type=jnp.float32)
    width = pay_out.shape[2]
    pieces = [picked[:, at : at + width] for at in range(0, picked.shape[1], width)]
    pay_out[2] = jnp.concatenate(pieces, axis=0).astype(jnp.bfloat16)
    for copy in copies[2:]:
        copy.wait()


def column_of(row):
    count = row.shape[1]
    down = lax.broadcasted_iota(jnp.int32, (count, count), 0)
    right = lax.broadcasted_iota(jnp.int32, (count, count), 1)
    return jnp.sum(jnp.where(down == right, row, 0), axis=1, keepdims=True)


def staged(prompt_q, cand_q, prompt_kv, cand_kv, ends, head):
    arrays = (prompt_q, cand_q, prompt_kv, cand_kv, ends, head)
    pay = jax.ShapeDtypeStruct((3,) + cand_kv.shape[1:], cand_kv.dtype)
    return pl.pallas_call(
        stage_kernel,
        out_shape=(like(prompt_q), like(cand_q), like(prompt_kv), pay, like(ends), like(head)),
        in_specs=[pl.BlockSpec(memory_space=pltpu.HBM)] * len(arrays),
        out_specs=tuple(vmem(6)),
        scratch_shapes=[pltpu.SemaphoreType.DMA((len(arrays),))],
        compiler_params=PARAMS,
        name="stage_operands",
    )(*(pltpu.with_memory_space_constraint(a, pltpu.HBM) for a in arrays))


def tiles(q_ref, head):
    rows = q_ref.shape[0]
    fan = max(1, ROW_TILE // rows)
    for start in range(head * GROUP, (head + 1) * GROUP, fan):
        heads = range(start, start + fan)
        queries = jnp.concatenate([q_ref[:, h * HEADDIM : (h + 1) * HEADDIM] for h in heads], axis=0)
        yield heads, slice(start * rows, (start + fan) * rows), queries


def stacked_rows(first_row, rows, count):
    return first_row + lax.rem(lax.broadcasted_iota(jnp.int32, (count, 1), 0), jnp.int32(rows))


def product(queries, key_rows):
    return lax.dot_general(
        queries, key_rows, (((1,), (1,)), ((), ())), preferred_element_type=jnp.float32
    )


def with_ones(value_rows):
    return jnp.concatenate([value_rows, jnp.ones_like(value_rows)], axis=1)


def head_rows(blocks, which, head):
    columns = slice(head * HEADDIM, (head + 1) * HEADDIM)
    return jnp.concatenate([ref[lead + (which,)][:, columns] for ref, lead in blocks], axis=0)


def key_positions(owners, rows):
    lane = lax.broadcasted_iota(jnp.int32, (1, len(owners) * rows), 1)
    positions = lane
    for index, owner in enumerate(owners):
        inside = (lane >= index * rows) & (lane < (index + 1) * rows)
        positions = jnp.where(inside, lane + (owner - index) * rows, positions)
    return positions


def spread(column, count):
    return jnp.concatenate([column] * (count // column.shape[1]), axis=1)


def absorb(queries, key_rows, widened, allowed, old):
    scores = product(queries, key_rows)
    if allowed is not None:
        scores = jnp.where(allowed, scores, NEG_FILL)
    count = scores.shape[1]
    peak = jnp.broadcast_to(jnp.max(scores, axis=1, keepdims=True), (scores.shape[0], HEADDIM))
    if old is not None:
        peak = jnp.maximum(peak, old[0])
    weights = jnp.exp2((scores - spread(peak, count)) * SCALE).astype(jnp.bfloat16)
    blended = jnp.dot(weights, widened, preferred_element_type=jnp.float32)
    if old is not None:
        blended += old[1] * spread(jnp.exp2((old[0] - peak) * SCALE), old[1].shape[1])
    return peak, blended


def prompt_place(cand_size):
    return lax.axis_index("ctx") * cand_size + lax.axis_index("cand")


def pairs_of(refs):
    return [(ref, (index,)) for ref in refs for index in range(ref.shape[0])]


def phase_kernel(sizes, arrays, masks, first, last, *refs):
    ctx_size, cand_size = sizes
    take = iter(refs)
    prompt_q, cand_q = next(take), next(take)
    block_refs = [next(take) for _ in arrays]
    pays = [next(take) for _ in masks]
    lengths = next(take) if last else None
    old = None if first else [(next(take), next(take)) for _ in range(2)]
    outs = refs[-2:] if last else refs[-4:]
    rows = prompt_q.shape[0]
    cand_rows = cand_q.shape[0]
    owners = prompt_owners(ctx_size, cand_size)
    key_pos = key_positions([place for index in arrays for place in owners[index]], rows)
    blocks = pairs_of(block_refs)
    own = [(ref, ()) for ref in pays]
    ctx = lax.axis_index("ctx")
    own_pos = key_positions([ctx ^ mask for mask in masks], cand_rows) if masks else None
    alive = stacked_rows(ctx * cand_rows, cand_rows, cand_rows) < lengths[:, :1] if last else None

    for head in range(block_refs[0].shape[3] // HEADDIM):
        key_rows = head_rows(blocks, 0, head)
        widened = with_ones(head_rows(blocks, 1, head))
        if masks:
            all_keys = jnp.concatenate([key_rows, head_rows(own, 0, head)], axis=0)
            all_widened = jnp.concatenate([widened, with_ones(head_rows(own, 1, head))], axis=0)
            free = jnp.full((1, key_rows.shape[0]), -1, jnp.int32)
            all_pos = jnp.concatenate([free, own_pos], axis=1)
        for kind, q_ref in enumerate((cand_q, prompt_q)):
            for heads, at, queries in tiles(q_ref, head):
                count = queries.shape[0]
                state = None if first else (old[kind][0][at], old[kind][1][at])
                if kind == 1:
                    first_row = prompt_place(cand_size) * rows
                    allowed = key_pos <= stacked_rows(first_row, rows, count)
                    state = absorb(queries, key_rows, widened, allowed, state)
                elif masks:
                    allowed = all_pos <= stacked_rows(ctx * cand_rows, cand_rows, count)
                    state = absorb(queries, all_keys, all_widened, allowed, state)
                else:
                    state = absorb(queries, key_rows, widened, None, state)
                if not last:
                    outs[2 * kind][at] = state[0]
                    outs[2 * kind + 1][at] = state[1]
                    continue
                result = state[1][:, :HEADDIM] / state[1][:, HEADDIM:]
                each = q_ref.shape[0]
                for index, h in enumerate(heads):
                    kept = result[index * each : (index + 1) * each]
                    if kind == 0:
                        kept = jnp.where(alive, kept, 0.0)
                    outs[kind][:, h * HEADDIM : (h + 1) * HEADDIM] = kept.astype(jnp.bfloat16)


def phase(sizes, arrays, q_rows, blocks, pays=(), state=None, lengths=None, after=()):
    prompt_q, cand_q = q_rows
    first, last = state is None, lengths is not None
    operands = [prompt_q, cand_q] + [blocks[index] for index in arrays]
    operands += [b for b, _ in pays]
    if last:
        operands.append(lengths)
    if not first:
        operands += state
    heads = prompt_q.shape[1] // HEADDIM
    if last:
        shapes = [like(cand_q), like(prompt_q)]
    else:
        shapes = []
        for q in (cand_q, prompt_q):
            count = heads * q.shape[0]
            shapes.append(jax.ShapeDtypeStruct((count, HEADDIM), jnp.float32))
            shapes.append(jax.ShapeDtypeStruct((count, 2 * HEADDIM), jnp.float32))
    key_count = sum(blocks[i].shape[0] * blocks[i].shape[2] for i in arrays)
    scores = heads * (prompt_q.shape[0] + cand_q.shape[0]) * key_count
    masks = [mask for _, mask in pays]
    return pl.pallas_call(
        functools.partial(phase_kernel, sizes, arrays, masks, first, last),
        out_shape=tuple(shapes),
        in_specs=vmem(len(operands)) + [pl.BlockSpec(memory_space=pl.ANY)] * len(after),
        out_specs=tuple(vmem(len(shapes))),
        compiler_params=PARAMS,
        cost_estimate=pl.CostEstimate(
            flops=6 * scores * HEADDIM, bytes_accessed=scores, transcendentals=scores
        ),
        name="attend_" + "_".join(str(i) for i in arrays),
    )(*operands, *after)


def rank_of(owner, sizes):
    _, along, across, core = prompt_bits(*sizes)
    low = lax.rem(owner, 2 * along)
    side = lax.rem(owner // across, 2)
    rank = lax.rem(owner, core) // 2 + (lax.rem(owner, across) // core) * (core // 2)
    rank += (owner // (2 * across)) * core
    return 2 * side + low, rank


def placed_blocks(sizes, arrays, refs, kv_ref, grouped):
    owners = prompt_owners(*sizes)
    count = sizes[0] * sizes[1] // GROUPS
    for ref, array in zip(refs, arrays):
        rows = ref.shape[2]
        for index, owner in enumerate(owners[array]):
            group, rank = rank_of(owner, sizes)
            place = (group * count + rank) if grouped else rank
            at = pl.ds(pl.multiple_of(place * rows, rows), rows)
            kv_ref[0, at, :] = ref[index, 0]
            kv_ref[1, at, :] = ref[index, 1]


def late_group(sizes):
    return rank_of(prompt_place(sizes[1]), sizes)[0] ^ (GROUPS - 1)


def step_parts(query_ref, kv_ref, at, allowed):
    parts = []
    for head in range(kv_ref.shape[2] // HEADDIM):
        columns = slice(head * HEADDIM, (head + 1) * HEADDIM)
        queries = query_ref[head].astype(jnp.bfloat16)
        widened = with_ones(kv_ref[1, at, columns])
        parts.append(absorb(queries, kv_ref[0, at, columns], widened, allowed, None))
    return parts


def early_step_kernel(sizes, arrays, masks, ends_ref, *refs):
    pays, blocks = refs[: len(masks)], refs[len(masks) : -4]
    query_ref, peak_ref, sum_ref, kv_ref = refs[-4:]
    placed_blocks(sizes, arrays, blocks, kv_ref, True)
    rows, width = pays[0].shape[1:]
    own_count = rows * len(masks)
    free = kv_ref.shape[1] - own_count
    picked = jnp.zeros((rows, width), jnp.float32)
    for ref, mask in zip(pays, masks):
        at = pl.ds(pl.multiple_of(free + (lax.axis_index("ctx") ^ mask) * rows, rows), rows)
        kv_ref[0, at, :] = ref[0]
        kv_ref[1, at, :] = ref[1]
        picked += ref[2].astype(jnp.float32)
    steps = ends_ref.shape[1]
    for head in range(width // HEADDIM):
        places = [divmod(h * HEADDIM, width) for h in range(head * GROUP, (head + 1) * GROUP)]
        query_ref[head] = jnp.concatenate(
            [picked[a * steps : (a + 1) * steps, b : b + HEADDIM] for a, b in places], axis=0
        )
    row_pos = jnp.concatenate([column_of(ends_ref[...])] * GROUP, axis=0)
    own_pos = lax.broadcasted_iota(jnp.int32, (1, own_count), 1)
    late = late_group(sizes)
    group_count = free // GROUPS
    sources = [(GROUPS, slice(free, None), own_pos <= row_pos)]
    for other in range(1, GROUPS):
        group = late ^ other
        at = pl.ds(pl.multiple_of(group * group_count, group_count), group_count)
        sources.append((group, at, None))
    for group, at, allowed in sources:
        for head, (peak, blended) in enumerate(step_parts(query_ref, kv_ref, at, allowed)):
            peak_ref[group, head] = peak
            sum_ref[group, head] = blended


def early_steps(sizes, arrays, ends, heads, pays, blocks):
    rows, width = pays[0][0].shape[1:]
    count = rows * sizes[0] * (sizes[1] + 1)
    kinds = width // HEADDIM
    stacked = heads // kinds * ends.shape[1]
    return pl.pallas_call(
        functools.partial(early_step_kernel, sizes, arrays, [mask for _, mask in pays]),
        out_shape=(
            jax.ShapeDtypeStruct((kinds, stacked, HEADDIM), jnp.float32),
            jax.ShapeDtypeStruct((GROUPS + 1, kinds, stacked, HEADDIM), jnp.float32),
            jax.ShapeDtypeStruct((GROUPS + 1, kinds, stacked, 2 * HEADDIM), jnp.float32),
        ),
        in_specs=vmem(1 + len(pays) + len(arrays)),
        out_specs=tuple(vmem(3)),
        scratch_shapes=[pltpu.VMEM((2, count, width), pays[0][0].dtype)],
        compiler_params=PARAMS,
        name="early_steps",
    )(ends, *(b for b, _ in pays), *(blocks[index] for index in arrays))


def step_kernel(sizes, arrays, ends_ref, head_ref, lengths_ref, query_ref, peak_ref, sum_ref, *refs):
    blocks = refs[: len(arrays)]
    logit_ref, kv_ref = refs[-2:]
    placed_blocks(sizes, arrays, blocks, kv_ref, False)
    late = late_group(sizes)
    steps = ends_ref.shape[1]
    ends = column_of(ends_ref[...])
    alive = ends < lengths_ref[:, :1]
    total = jnp.zeros((steps, HEADDIM), jnp.float32)
    for head, newest in enumerate(step_parts(query_ref, kv_ref, slice(None), None)):
        parts = [
            tuple(jnp.where(late == group, new, ref[group, head]) for new, ref in zip(newest, (peak_ref, sum_ref)))
            for group in range(GROUPS)
        ]
        parts.append((peak_ref[GROUPS, head], sum_ref[GROUPS, head]))
        peak = functools.reduce(jnp.maximum, [part[0] for part in parts])
        blended = sum(part[1] * spread(jnp.exp2((part[0] - peak) * SCALE), 2 * HEADDIM) for part in parts)
        result = blended[:, :HEADDIM] / blended[:, HEADDIM:]
        for index in range(GROUP):
            kept = jnp.where(alive, result[index * steps : (index + 1) * steps], 0.0)
            kept = kept.astype(jnp.bfloat16).astype(jnp.float32)
            h = head * GROUP + index
            total += kept * head_ref[:, h * HEADDIM : (h + 1) * HEADDIM]
    logits = jnp.sum(total, axis=1, keepdims=True)
    down = lax.broadcasted_iota(jnp.int32, (steps, steps), 0)
    right = lax.broadcasted_iota(jnp.int32, (steps, steps), 1)
    logit_ref[...] = jnp.sum(jnp.where(down == right, logits, 0.0), axis=0, keepdims=True)


def step_shares(sizes, arrays, ends, head, lengths, early, blocks, after):
    rows, width = blocks[0].shape[2:]
    count = rows * sizes[0] * sizes[1] // GROUPS
    return pl.pallas_call(
        functools.partial(step_kernel, sizes, arrays),
        out_shape=jax.ShapeDtypeStruct(ends.shape, jnp.float32),
        in_specs=vmem(6 + len(arrays)) + [pl.BlockSpec(memory_space=pl.ANY)],
        out_specs=vmem(1)[0],
        scratch_shapes=[pltpu.VMEM((2, count, width), blocks[0].dtype)],
        compiler_params=PARAMS,
        name="step_logits",
    )(ends, head, lengths, *early, *(blocks[index] for index in arrays), after)


def per_device(ctx_size, cand_size, prompt_q, prompt_kv, cand_q, cand_kv, cand_lengths, step_ends, reward_head):
    sizes = ctx_size, cand_size
    size = ctx_size * cand_size
    prompt_rows, cand_rows, own, payload, ends, head = staged(
        prompt_q, cand_q[0], prompt_kv, cand_kv[:, 0], step_ends, reward_head[None]
    )
    lengths = jnp.broadcast_to(cand_lengths[None], (1, HEADDIM))
    q_rows = prompt_rows, cand_rows
    pays = gather_cand(payload, ctx_size)
    early, along, across, core = prompt_bits(ctx_size, cand_size)

    def across_cores(block):
        return flipped(block, PROMPT_AXES, size, core)

    def shared_out(block, even, odd):
        return lax.ppermute(
            block, PROMPT_AXES, [(i, i ^ (odd if i & core else even)) for i in range(size)]
        )

    held = own[None]
    sent = prompt_kv[None]
    for bit in early:
        held = packed(held, flipped(sent, PROMPT_AXES, size, bit))
        sent = held
    second = shared_out(held, along, across)
    third = shared_out(held, across, along)
    blocks = [held, second, third, None, across_cores(held), None, None, None]
    state = phase(sizes, [0, 4], q_rows, blocks)
    fourth = shared_out(packed(second, after=state[:1] + tuple(b for b, _ in pays[1:4])), across, along)
    blocks[3] = fourth
    blocks[5:7] = across_cores(second), across_cores(third)
    state = phase(sizes, [1, 2], q_rows, blocks, pays=pays, state=state)
    early_parts = early_steps(sizes, [0, 1, 2, 4, 5, 6], ends, head.shape[1] // HEADDIM, pays, blocks)
    blocks[7] = across_cores(packed(fourth, after=state[:1]))
    state = phase(sizes, [5, 6], q_rows, blocks, state=state)
    step_logits = step_shares(sizes, [3, 7], ends, head, lengths, early_parts, blocks, state[0])
    cand_out, prompt_out = phase(sizes, [3, 7], q_rows, blocks, state=state, lengths=lengths)
    tp_size = lax.axis_size("tp")
    for bit in high_bits(tp_size, 1):
        step_logits = step_logits + flipped(step_logits, "tp", tp_size, bit)
    return (prompt_out, cand_out[None], step_logits)


def solution(mesh):
    placed = (
        P(("ctx", "cand"), "tp"),
        P(None, ("ctx", "cand"), "tp"),
        P("cand", "ctx", "tp"),
        P(None, "cand", "ctx", "tp"),
        P("cand"),
        P("cand", None),
        P("tp"),
    )
    return jax.shard_map(
        functools.partial(per_device, mesh.shape["ctx"], mesh.shape["cand"]),
        mesh=mesh,
        in_specs=placed,
        out_specs=(P(("ctx", "cand"), "tp"), P("cand", "ctx", "tp"), P("cand", None)),
        check_vma=False,
    )
```

```python
import functools
import math

import jax
import jax.numpy as jnp
from jax import lax
from jax.experimental import pallas as pl
from jax.experimental.pallas import tpu as pltpu
from jax.sharding import PartitionSpec as P

HEADDIM = 128
GROUP = 8
SUBLANES = 8
NEG_FILL = -1e30
GROUPS = 8
EARLY_GROUPS = 0, 1, 2, 4
LATE_GROUPS = 3, 5, 6, 7
SCALE = HEADDIM ** -0.5 * math.log2(math.e)
ROW_TILE = 256
VMEM_LIMIT = 28 * 1024 * 1024
PARAMS = pltpu.CompilerParams(vmem_limit_bytes=VMEM_LIMIT)
PROMPT_AXES = ("ctx", "cand")


def vmem(count):
    return [pl.BlockSpec(memory_space=pltpu.VMEM)] * count


def like(array):
    return jax.ShapeDtypeStruct(array.shape, array.dtype)


def high_bits(size, lowest):
    return [1 << b for b in reversed(range(size.bit_length() - 1)) if 1 << b >= lowest]


def flipped(block, axes, size, bit):
    return lax.ppermute(block, axes, [(i, i ^ bit) for i in range(size)])


def pack_kernel(count, *refs):
    sources, out_ref = refs[:count], refs[-1]
    start = 0
    for ref in sources:
        out_ref[start : start + ref.shape[0]] = ref[...]
        start += ref.shape[0]


def packed(*arrays, after=()):
    count = sum(a.shape[0] for a in arrays)
    return pl.pallas_call(
        functools.partial(pack_kernel, len(arrays)),
        out_shape=jax.ShapeDtypeStruct((count,) + arrays[0].shape[1:], arrays[0].dtype),
        in_specs=vmem(len(arrays)) + [pl.BlockSpec(memory_space=pl.ANY)] * len(after),
        out_specs=vmem(1)[0],
        compiler_params=PARAMS,
        name="pack_blocks",
    )(*arrays, *after)


def prompt_bits(ctx_size, cand_size):
    core, along, across = cand_size, 1, 2 * cand_size
    early = high_bits(cand_size, 2) + [bit * cand_size for bit in high_bits(ctx_size, 4)]
    return early, along, across, core


def prompt_owners(ctx_size, cand_size):
    early, along, across, core = prompt_bits(ctx_size, cand_size)
    place = lax.axis_index("ctx") * cand_size + lax.axis_index("cand")
    odd = lax.rem(lax.axis_index("ctx"), 2)
    near = along + odd * (across - along)
    far = along + across - near
    masks = [0]
    for bit in early:
        masks += [mask ^ bit for mask in masks]
    shifts = [0, near, far, along + across, core, core + far, core + near, core + along + across]
    return [[place ^ mask ^ shift for mask in masks] for shift in shifts]


def gather_cand(own, ctx_size):
    blocks = [(own, 0), (flipped(own, "ctx", ctx_size, 1), 1)]
    for bit in reversed(high_bits(ctx_size, 2)):
        rail = [(flipped(b, "ctx", ctx_size, bit), mask | bit) for b, mask in blocks if not mask & 1]
        blocks += rail + [(flipped(b, "ctx", ctx_size, 1), mask | 1) for b, mask in rail]
    return blocks


def stage_kernel(length_ref, prompt_q, cand_q, prompt_kv, cand_kv, ends, head, *refs):
    q_out, cand_out, kv_out, pay_out, ends_out, head_out, length_out, length_here, sems = refs
    steps = ends.shape[1]
    pairs = [
        (cand_q, cand_out),
        (ends, ends_out),
        (cand_kv, pay_out.at[0:2]),
        (prompt_kv, kv_out),
        (prompt_q, q_out),
        (head, head_out),
        (length_ref, length_here),
    ]
    copies = [pltpu.make_async_copy(a, b, sems.at[i]) for i, (a, b) in enumerate(pairs)]
    for copy in copies:
        copy.start()
    copies[0].wait()
    copies[1].wait()
    rows = cand_out.shape[0]
    ends_column = column_of(ends_out[...])
    row_pos = lax.axis_index("ctx") * rows + lax.broadcasted_iota(jnp.int32, (steps, rows), 1)
    chosen = (row_pos == ends_column).astype(jnp.bfloat16)
    picked = jnp.dot(chosen, cand_out[...], preferred_element_type=jnp.float32)
    width = pay_out.shape[2]
    pieces = [picked[:, at : at + width] for at in range(0, picked.shape[1], width)]
    pay_out[2] = jnp.concatenate(pieces, axis=0).astype(jnp.bfloat16)
    for copy in copies[2:]:
        copy.wait()
    length_out[...] = jnp.full(length_out.shape, length_here[0], jnp.int32)


def column_of(row):
    count = row.shape[1]
    down = lax.broadcasted_iota(jnp.int32, (count, count), 0)
    right = lax.broadcasted_iota(jnp.int32, (count, count), 1)
    return jnp.sum(jnp.where(down == right, row, 0), axis=1, keepdims=True)


def staged(length, prompt_q, cand_q, prompt_kv, cand_kv, ends, head):
    arrays = (prompt_q, cand_q, prompt_kv, cand_kv, ends, head)
    payload = jax.ShapeDtypeStruct((3,) + cand_kv.shape[1:], cand_kv.dtype)
    lengths = jax.ShapeDtypeStruct((1, HEADDIM), jnp.int32)
    return pl.pallas_call(
        stage_kernel,
        out_shape=(like(prompt_q), like(cand_q), like(prompt_kv), payload, like(ends), like(head), lengths),
        in_specs=[pl.BlockSpec(memory_space=pl.ANY)]
        + [pl.BlockSpec(memory_space=pltpu.HBM)] * len(arrays),
        out_specs=tuple(vmem(7)),
        scratch_shapes=[pltpu.SMEM((1,), jnp.int32), pltpu.SemaphoreType.DMA((len(arrays) + 1,))],
        compiler_params=PARAMS,
        name="stage_operands",
    )(length, *(pltpu.with_memory_space_constraint(a, pltpu.HBM) for a in arrays))


def tiles(q_ref, head):
    rows = q_ref.shape[0]
    fan = max(1, ROW_TILE // rows)
    for start in range(head * GROUP, (head + 1) * GROUP, fan):
        heads = range(start, start + fan)
        queries = jnp.concatenate([q_ref[:, h * HEADDIM : (h + 1) * HEADDIM] for h in heads], axis=0)
        yield heads, slice(start * rows, (start + fan) * rows), queries


def stacked_rows(first_row, rows, count):
    return first_row + lax.rem(lax.broadcasted_iota(jnp.int32, (count, 1), 0), jnp.int32(rows))


def product(queries, key_rows):
    return lax.dot_general(
        queries, key_rows, (((1,), (1,)), ((), ())), preferred_element_type=jnp.float32
    )


def with_ones(value_rows):
    return jnp.concatenate([value_rows, jnp.ones_like(value_rows)], axis=1)


def head_rows(blocks, which, head):
    columns = slice(head * HEADDIM, (head + 1) * HEADDIM)
    return jnp.concatenate([ref[lead + (which,)][:, columns] for ref, lead in blocks], axis=0)


def key_positions(owners, rows):
    lane = lax.broadcasted_iota(jnp.int32, (1, len(owners) * rows), 1)
    positions = lane
    for index, owner in enumerate(owners):
        inside = (lane >= index * rows) & (lane < (index + 1) * rows)
        positions = jnp.where(inside, lane + (owner - index) * rows, positions)
    return positions


def spread(column, count):
    return jnp.concatenate([column] * (count // column.shape[1]), axis=1)


def absorb(queries, key_rows, widened, allowed, old):
    scores = product(queries, key_rows)
    if allowed is not None:
        scores = jnp.where(allowed, scores, NEG_FILL)
    count = scores.shape[1]
    peak = jnp.broadcast_to(jnp.max(scores, axis=1, keepdims=True), (scores.shape[0], HEADDIM))
    if old is not None:
        peak = jnp.maximum(peak, old[0])
    weights = jnp.exp2((scores - spread(peak, count)) * SCALE).astype(jnp.bfloat16)
    blended = jnp.dot(weights, widened, preferred_element_type=jnp.float32)
    if old is not None:
        blended += old[1] * spread(jnp.exp2((old[0] - peak) * SCALE), old[1].shape[1])
    return peak, blended


def prompt_place(cand_size):
    return lax.axis_index("ctx") * cand_size + lax.axis_index("cand")


def pairs_of(refs):
    return [(ref, (index,)) for ref in refs for index in range(ref.shape[0])]


def phase_kernel(sizes, arrays, masks, first, last, *refs):
    ctx_size, cand_size = sizes
    take = iter(refs)
    prompt_q, cand_q = next(take), next(take)
    block_refs = [next(take) for _ in arrays]
    pays = [next(take) for _ in masks]
    lengths = next(take) if last else None
    old = None if first else [(next(take), next(take)) for _ in range(2)]
    outs = refs[-2:] if last else refs[-4:]
    rows = prompt_q.shape[0]
    cand_rows = cand_q.shape[0]
    owners = prompt_owners(ctx_size, cand_size)
    key_pos = key_positions([place for index in arrays for place in owners[index]], rows)
    blocks = pairs_of(block_refs)
    own = [(ref, ()) for ref in pays]
    ctx = lax.axis_index("ctx")
    own_pos = key_positions([ctx ^ mask for mask in masks], cand_rows) if masks else None
    alive = stacked_rows(ctx * cand_rows, cand_rows, cand_rows) < lengths[:, :1] if last else None

    for head in range(block_refs[0].shape[3] // HEADDIM):
        key_rows = head_rows(blocks, 0, head)
        widened = with_ones(head_rows(blocks, 1, head))
        if masks:
            all_keys = jnp.concatenate([key_rows, head_rows(own, 0, head)], axis=0)
            all_widened = jnp.concatenate([widened, with_ones(head_rows(own, 1, head))], axis=0)
            free = jnp.full((1, key_rows.shape[0]), -1, jnp.int32)
            all_pos = jnp.concatenate([free, own_pos], axis=1)
        for kind, q_ref in enumerate((cand_q, prompt_q)):
            for heads, at, queries in tiles(q_ref, head):
                count = queries.shape[0]
                state = None if first else (old[kind][0][at], old[kind][1][at])
                if kind == 1:
                    first_row = prompt_place(cand_size) * rows
                    allowed = key_pos <= stacked_rows(first_row, rows, count)
                    state = absorb(queries, key_rows, widened, allowed, state)
                elif masks:
                    allowed = all_pos <= stacked_rows(ctx * cand_rows, cand_rows, count)
                    state = absorb(queries, all_keys, all_widened, allowed, state)
                else:
                    state = absorb(queries, key_rows, widened, None, state)
                if not last:
                    outs[2 * kind][at] = state[0]
                    outs[2 * kind + 1][at] = state[1]
                    continue
                result = state[1][:, :HEADDIM] / state[1][:, HEADDIM:]
                each = q_ref.shape[0]
                for index, h in enumerate(heads):
                    kept = result[index * each : (index + 1) * each]
                    if kind == 0:
                        kept = jnp.where(alive, kept, 0.0)
                    outs[kind][:, h * HEADDIM : (h + 1) * HEADDIM] = kept.astype(jnp.bfloat16)


def phase(sizes, arrays, q_rows, blocks, pays=(), state=None, lengths=None, after=()):
    prompt_q, cand_q = q_rows
    first, last = state is None, lengths is not None
    operands = [prompt_q, cand_q] + [blocks[index] for index in arrays]
    operands += [b for b, _ in pays]
    if last:
        operands.append(lengths)
    if not first:
        operands += state
    heads = prompt_q.shape[1] // HEADDIM
    if last:
        shapes = [like(cand_q), like(prompt_q)]
    else:
        shapes = []
        for q in (cand_q, prompt_q):
            count = heads * q.shape[0]
            shapes.append(jax.ShapeDtypeStruct((count, HEADDIM), jnp.float32))
            shapes.append(jax.ShapeDtypeStruct((count, 2 * HEADDIM), jnp.float32))
    key_count = sum(blocks[i].shape[0] * blocks[i].shape[2] for i in arrays)
    scores = heads * (prompt_q.shape[0] + cand_q.shape[0]) * key_count
    masks = [mask for _, mask in pays]
    return pl.pallas_call(
        functools.partial(phase_kernel, sizes, arrays, masks, first, last),
        out_shape=tuple(shapes),
        in_specs=vmem(len(operands)) + [pl.BlockSpec(memory_space=pl.ANY)] * len(after),
        out_specs=tuple(vmem(len(shapes))),
        compiler_params=PARAMS,
        cost_estimate=pl.CostEstimate(
            flops=6 * scores * HEADDIM, bytes_accessed=scores, transcendentals=scores
        ),
        name="attend_" + "_".join(str(i) for i in arrays),
    )(*operands, *after)


def rank_of(owner, sizes):
    _, along, across, core = prompt_bits(*sizes)
    group = lax.rem(owner, 2 * along) + 2 * lax.rem(owner // across, 2) + 4 * lax.rem(owner // core, 2)
    return group, lax.rem(owner, core) // 2 + (owner // (2 * across)) * (core // 2)


def placed_blocks(sizes, arrays, refs, kv_ref):
    owners = prompt_owners(*sizes)
    count = sizes[0] * sizes[1] // GROUPS
    for ref, array in zip(refs, arrays):
        rows = ref.shape[2]
        for index, owner in enumerate(owners[array]):
            group, rank = rank_of(owner, sizes)
            at = pl.ds(pl.multiple_of((group * count + rank) * rows, rows), rows)
            kv_ref[0, at, :] = ref[index, 0]
            kv_ref[1, at, :] = ref[index, 1]


def group_keys(sizes, others, rows):
    count = rows * sizes[0] * sizes[1] // GROUPS
    own = rank_of(prompt_place(sizes[1]), sizes)[0]
    groups = [own ^ other for other in others]
    return [(group, pl.ds(pl.multiple_of(group * count, count), count), None) for group in groups]


def step_parts(query_ref, kv_ref, at, allowed):
    parts = []
    for head in range(kv_ref.shape[2] // HEADDIM):
        columns = slice(head * HEADDIM, (head + 1) * HEADDIM)
        queries = query_ref[head].astype(jnp.bfloat16)
        widened = with_ones(kv_ref[1, at, columns])
        parts.append(absorb(queries, kv_ref[0, at, columns], widened, allowed, None))
    return parts


def early_step_kernel(sizes, arrays, masks, ends_ref, *refs):
    pays, blocks = refs[: len(masks)], refs[len(masks) : -4]
    query_ref, peak_ref, sum_ref, kv_ref = refs[-4:]
    placed_blocks(sizes, arrays, blocks, kv_ref)
    rows, width = pays[0].shape[1:]
    own_count = rows * len(masks)
    free = kv_ref.shape[1] - own_count
    picked = jnp.zeros((rows, width), jnp.float32)
    for ref, mask in zip(pays, masks):
        at = pl.ds(pl.multiple_of(free + (lax.axis_index("ctx") ^ mask) * rows, rows), rows)
        kv_ref[0, at, :] = ref[0]
        kv_ref[1, at, :] = ref[1]
        picked += ref[2].astype(jnp.float32)
    steps = ends_ref.shape[1]
    for head in range(width // HEADDIM):
        places = [divmod(h * HEADDIM, width) for h in range(head * GROUP, (head + 1) * GROUP)]
        query_ref[head] = jnp.concatenate(
            [picked[a * steps : (a + 1) * steps, b : b + HEADDIM] for a, b in places], axis=0
        )
    row_pos = jnp.concatenate([column_of(ends_ref[...])] * GROUP, axis=0)
    own_pos = lax.broadcasted_iota(jnp.int32, (1, own_count), 1)
    sources = [(GROUPS, slice(free, None), own_pos <= row_pos)]
    sources += group_keys(sizes, EARLY_GROUPS, rows)
    for group, at, allowed in sources:
        for head, (peak, blended) in enumerate(step_parts(query_ref, kv_ref, at, allowed)):
            peak_ref[group, head] = peak
            sum_ref[group, head] = blended


def early_steps(sizes, arrays, ends, heads, pays, blocks):
    rows, width = pays[0][0].shape[1:]
    count = rows * sizes[0] * (sizes[1] + 1)
    kinds = width // HEADDIM
    stacked = heads // kinds * ends.shape[1]
    return pl.pallas_call(
        functools.partial(early_step_kernel, sizes, arrays, [mask for _, mask in pays]),
        out_shape=(
            jax.ShapeDtypeStruct((kinds, stacked, HEADDIM), jnp.float32),
            jax.ShapeDtypeStruct((GROUPS + 1, kinds, stacked, HEADDIM), jnp.float32),
            jax.ShapeDtypeStruct((GROUPS + 1, kinds, stacked, 2 * HEADDIM), jnp.float32),
        ),
        in_specs=vmem(1 + len(pays) + len(arrays)),
        out_specs=tuple(vmem(3)),
        scratch_shapes=[pltpu.VMEM((2, count, width), pays[0][0].dtype)],
        compiler_params=PARAMS,
        name="early_steps",
    )(ends, *(b for b, _ in pays), *(blocks[index] for index in arrays))


def step_kernel(sizes, arrays, ends_ref, head_ref, lengths_ref, query_ref, *refs):
    blocks = refs[2 : 2 + len(arrays)]
    logit_ref, peak_ref, sum_ref, kv_ref = refs[-4:]
    placed_blocks(sizes, arrays, blocks, kv_ref)
    steps = ends_ref.shape[1]
    ends = column_of(ends_ref[...])
    alive = ends < lengths_ref[:, :1]
    for group, at, _ in group_keys(sizes, LATE_GROUPS, blocks[0].shape[2]):
        for head, (peak, blended) in enumerate(step_parts(query_ref, kv_ref, at, None)):
            peak_ref[group, head] = peak
            sum_ref[group, head] = blended
    total = jnp.zeros((steps, HEADDIM), jnp.float32)
    for head in range(query_ref.shape[0]):
        peaks = [peak_ref[group, head] for group in range(GROUPS + 1)]
        peak = functools.reduce(jnp.maximum, peaks)
        blended = jnp.zeros(sum_ref.shape[2:], jnp.float32)
        for group in range(GROUPS + 1):
            blended += sum_ref[group, head] * spread(jnp.exp2((peaks[group] - peak) * SCALE), 2 * HEADDIM)
        result = blended[:, :HEADDIM] / blended[:, HEADDIM:]
        for index in range(GROUP):
            kept = jnp.where(alive, result[index * steps : (index + 1) * steps], 0.0)
            kept = kept.astype(jnp.bfloat16).astype(jnp.float32)
            h = head * GROUP + index
            total += kept * head_ref[:, h * HEADDIM : (h + 1) * HEADDIM]
    logits = jnp.sum(total, axis=1, keepdims=True)
    down = lax.broadcasted_iota(jnp.int32, (steps, steps), 0)
    right = lax.broadcasted_iota(jnp.int32, (steps, steps), 1)
    logit_ref[...] = jnp.sum(jnp.where(down == right, logits, 0.0), axis=0, keepdims=True)


def step_shares(sizes, arrays, ends, head, lengths, early, blocks, after):
    rows, width = blocks[0].shape[2:]
    count = rows * sizes[0] * sizes[1]
    return pl.pallas_call(
        functools.partial(step_kernel, sizes, arrays),
        out_shape=(jax.ShapeDtypeStruct(ends.shape, jnp.float32),) + tuple(like(a) for a in early[1:]),
        in_specs=vmem(6 + len(arrays)) + [pl.BlockSpec(memory_space=pl.ANY)],
        out_specs=tuple(vmem(3)),
        scratch_shapes=[pltpu.VMEM((2, count, width), blocks[0].dtype)],
        input_output_aliases={4: 1, 5: 2},
        compiler_params=PARAMS,
        name="step_logits",
    )(ends, head, lengths, *early, *(blocks[index] for index in arrays), after)[0]


def per_device(ctx_size, cand_size, prompt_q, prompt_kv, cand_q, cand_kv, cand_lengths, step_ends, reward_head):
    sizes = ctx_size, cand_size
    size = ctx_size * cand_size
    prompt_rows, cand_rows, own, payload, ends, head, lengths = staged(
        cand_lengths, prompt_q, cand_q[0], prompt_kv, cand_kv[:, 0], step_ends, reward_head[None]
    )
    q_rows = prompt_rows, cand_rows
    pays = gather_cand(payload, ctx_size)
    early, along, across, core = prompt_bits(ctx_size, cand_size)

    def across_cores(block):
        return flipped(block, PROMPT_AXES, size, core)

    def shared_out(block, even, odd):
        return lax.ppermute(
            block, PROMPT_AXES, [(i, i ^ (odd if i & core else even)) for i in range(size)]
        )

    held = own[None]
    sent = prompt_kv[None]
    for bit in early:
        held = packed(held, flipped(sent, PROMPT_AXES, size, bit))
        sent = held
    second = shared_out(held, along, across)
    third = shared_out(held, across, along)
    blocks = [held, second, third, None, across_cores(held), None, None, None]
    state = phase(sizes, [0, 4], q_rows, blocks)
    fourth = shared_out(packed(second, after=state[:1] + tuple(b for b, _ in pays[1:4])), across, along)
    blocks[3] = fourth
    blocks[5:7] = across_cores(second), across_cores(third)
    state = phase(sizes, [1, 2], q_rows, blocks, pays=pays, state=state)
    early_parts = early_steps(sizes, [0, 1, 2, 4], ends, head.shape[1] // HEADDIM, pays, blocks)
    blocks[7] = across_cores(packed(fourth, after=[state[0], early_parts[0]]))
    state = phase(sizes, [5, 6], q_rows, blocks, state=state)
    step_logits = step_shares(sizes, [3, 5, 6, 7], ends, head, lengths, early_parts, blocks, state[0])
    cand_out, prompt_out = phase(sizes, [3, 7], q_rows, blocks, state=state, lengths=lengths)
    tp_size = lax.axis_size("tp")
    for bit in high_bits(tp_size, 1):
        step_logits = step_logits + flipped(step_logits, "tp", tp_size, bit)
    return (prompt_out, cand_out[None], step_logits)


def solution(mesh):
    placed = (
        P(("ctx", "cand"), "tp"),
        P(None, ("ctx", "cand"), "tp"),
        P("cand", "ctx", "tp"),
        P(None, "cand", "ctx", "tp"),
        P("cand"),
        P("cand", None),
        P("tp"),
    )
    return jax.shard_map(
        functools.partial(per_device, mesh.shape["ctx"], mesh.shape["cand"]),
        mesh=mesh,
        in_specs=placed,
        out_specs=(P(("ctx", "cand"), "tp"), P("cand", "ctx", "tp"), P("cand", None)),
        check_vma=False,
    )
```

```python
import functools
import math

import jax
import jax.numpy as jnp
from jax import lax
from jax.experimental import pallas as pl
from jax.experimental.pallas import tpu as pltpu
from jax.sharding import PartitionSpec as P

HEADDIM = 128
GROUP = 8
SUBLANES = 8
NEG_FILL = -1e30
SCALE = HEADDIM ** -0.5 * math.log2(math.e)
ROW_TILE = 256
VMEM_LIMIT = 28 * 1024 * 1024
PARAMS = pltpu.CompilerParams(vmem_limit_bytes=VMEM_LIMIT)
PROMPT_AXES = ("ctx", "cand")


def vmem(count):
    return [pl.BlockSpec(memory_space=pltpu.VMEM)] * count


def like(array):
    return jax.ShapeDtypeStruct(array.shape, array.dtype)


def high_bits(size, lowest):
    return [1 << b for b in reversed(range(size.bit_length() - 1)) if 1 << b >= lowest]


def flipped(block, axes, size, bit):
    return lax.ppermute(block, axes, [(i, i ^ bit) for i in range(size)])


def pack_kernel(count, *refs):
    sources, out_ref = refs[:count], refs[-1]
    start = 0
    for ref in sources:
        out_ref[start : start + ref.shape[0]] = ref[...]
        start += ref.shape[0]


def packed(*arrays, after=()):
    count = sum(a.shape[0] for a in arrays)
    return pl.pallas_call(
        functools.partial(pack_kernel, len(arrays)),
        out_shape=jax.ShapeDtypeStruct((count,) + arrays[0].shape[1:], arrays[0].dtype),
        in_specs=vmem(len(arrays)) + [pl.BlockSpec(memory_space=pl.ANY)] * len(after),
        out_specs=vmem(1)[0],
        compiler_params=PARAMS,
        name="pack_blocks",
    )(*arrays, *after)


def prompt_bits(ctx_size, cand_size):
    core, along, across = cand_size, 1, 2 * cand_size
    early = high_bits(cand_size, 2) + [bit * cand_size for bit in high_bits(ctx_size, 4)]
    return early, along, across, core


def prompt_owners(ctx_size, cand_size):
    early, along, across, core = prompt_bits(ctx_size, cand_size)
    place = lax.axis_index("ctx") * cand_size + lax.axis_index("cand")
    odd = lax.rem(lax.axis_index("ctx"), 2)
    near = along + odd * (across - along)
    far = along + across - near
    masks = [0]
    for bit in early:
        masks += [mask ^ bit for mask in masks]
    shifts = [0, near, far, along + across, core, core + far, core + near, core + along + across]
    return [[place ^ mask ^ shift for mask in masks] for shift in shifts]


def gather_cand(own, ctx_size):
    blocks = [(own, 0), (flipped(own, "ctx", ctx_size, 1), 1)]
    for bit in reversed(high_bits(ctx_size, 2)):
        rail = [(flipped(b, "ctx", ctx_size, bit), mask | bit) for b, mask in blocks if not mask & 1]
        blocks += rail + [(flipped(b, "ctx", ctx_size, 1), mask | 1) for b, mask in rail]
    return blocks


def stage_kernel(length_ref, prompt_q, cand_q, prompt_kv, cand_kv, ends, head, *refs):
    q_out, cand_out, kv_out, pay_out, ends_out, head_out, length_out, length_here, sems = refs
    steps = ends.shape[1]
    pairs = [
        (cand_q, cand_out),
        (ends, ends_out),
        (cand_kv, pay_out.at[0:2]),
        (prompt_kv, kv_out),
        (prompt_q, q_out),
        (head, head_out),
        (length_ref, length_here),
    ]
    copies = [pltpu.make_async_copy(a, b, sems.at[i]) for i, (a, b) in enumerate(pairs)]
    for copy in copies:
        copy.start()
    copies[0].wait()
    copies[1].wait()
    rows = cand_out.shape[0]
    ends_column = column_of(ends_out[...])
    row_pos = lax.axis_index("ctx") * rows + lax.broadcasted_iota(jnp.int32, (steps, rows), 1)
    chosen = (row_pos == ends_column).astype(jnp.bfloat16)
    picked = jnp.dot(chosen, cand_out[...], preferred_element_type=jnp.float32)
    width = pay_out.shape[2]
    pieces = [picked[:, at : at + width] for at in range(0, picked.shape[1], width)]
    pay_out[2] = jnp.concatenate(pieces, axis=0).astype(jnp.bfloat16)
    for copy in copies[2:]:
        copy.wait()
    length_out[...] = jnp.full(length_out.shape, length_here[0], jnp.int32)


def column_of(row):
    count = row.shape[1]
    down = lax.broadcasted_iota(jnp.int32, (count, count), 0)
    right = lax.broadcasted_iota(jnp.int32, (count, count), 1)
    return jnp.sum(jnp.where(down == right, row, 0), axis=1, keepdims=True)


def staged(length, prompt_q, cand_q, prompt_kv, cand_kv, ends, head):
    arrays = (prompt_q, cand_q, prompt_kv, cand_kv, ends, head)
    payload = jax.ShapeDtypeStruct((3,) + cand_kv.shape[1:], cand_kv.dtype)
    lengths = jax.ShapeDtypeStruct((1, HEADDIM), jnp.int32)
    return pl.pallas_call(
        stage_kernel,
        out_shape=(like(prompt_q), like(cand_q), like(prompt_kv), payload, like(ends), like(head), lengths),
        in_specs=[pl.BlockSpec(memory_space=pl.ANY)]
        + [pl.BlockSpec(memory_space=pltpu.HBM)] * len(arrays),
        out_specs=tuple(vmem(7)),
        scratch_shapes=[pltpu.SMEM((1,), jnp.int32), pltpu.SemaphoreType.DMA((len(arrays) + 1,))],
        compiler_params=PARAMS,
        name="stage_operands",
    )(length, *(pltpu.with_memory_space_constraint(a, pltpu.HBM) for a in arrays))


def tiles(q_ref, head):
    rows = q_ref.shape[0]
    fan = max(1, ROW_TILE // rows)
    for start in range(head * GROUP, (head + 1) * GROUP, fan):
        heads = range(start, start + fan)
        queries = jnp.concatenate([q_ref[:, h * HEADDIM : (h + 1) * HEADDIM] for h in heads], axis=0)
        yield heads, slice(start * rows, (start + fan) * rows), queries


def stacked_rows(first_row, rows, count):
    return first_row + lax.rem(lax.broadcasted_iota(jnp.int32, (count, 1), 0), jnp.int32(rows))


def product(queries, key_rows):
    return lax.dot_general(
        queries, key_rows, (((1,), (1,)), ((), ())), preferred_element_type=jnp.float32
    )


def with_ones(value_rows):
    return jnp.concatenate([value_rows, jnp.ones_like(value_rows)], axis=1)


def head_rows(blocks, which, head):
    columns = slice(head * HEADDIM, (head + 1) * HEADDIM)
    return jnp.concatenate([ref[lead + (which,)][:, columns] for ref, lead in blocks], axis=0)


def key_positions(owners, rows):
    lane = lax.broadcasted_iota(jnp.int32, (1, len(owners) * rows), 1)
    positions = lane
    for index, owner in enumerate(owners):
        inside = (lane >= index * rows) & (lane < (index + 1) * rows)
        positions = jnp.where(inside, lane + (owner - index) * rows, positions)
    return positions


def spread(column, count):
    return jnp.concatenate([column] * (count // column.shape[1]), axis=1)


def absorb(queries, key_rows, widened, allowed, old):
    scores = product(queries, key_rows)
    if allowed is not None:
        scores = jnp.where(allowed, scores, NEG_FILL)
    count = scores.shape[1]
    peak = jnp.broadcast_to(jnp.max(scores, axis=1, keepdims=True), (scores.shape[0], HEADDIM))
    if old is not None:
        peak = jnp.maximum(peak, old[0])
    weights = jnp.exp2((scores - spread(peak, count)) * SCALE).astype(jnp.bfloat16)
    blended = jnp.dot(weights, widened, preferred_element_type=jnp.float32)
    if old is not None:
        blended += old[1] * spread(jnp.exp2((old[0] - peak) * SCALE), old[1].shape[1])
    return peak, blended


def prompt_place(cand_size):
    return lax.axis_index("ctx") * cand_size + lax.axis_index("cand")


def pairs_of(refs):
    return [(ref, (index,)) for ref in refs for index in range(ref.shape[0])]


def phase_kernel(sizes, arrays, masks, first, last, *refs):
    ctx_size, cand_size = sizes
    take = iter(refs)
    prompt_q, cand_q = next(take), next(take)
    block_refs = [next(take) for _ in arrays]
    pays = [next(take) for _ in masks]
    lengths = next(take) if last else None
    old = None if first else [(next(take), next(take)) for _ in range(2)]
    outs = refs[-2:] if last else refs[-4:]
    rows = prompt_q.shape[0]
    cand_rows = cand_q.shape[0]
    owners = prompt_owners(ctx_size, cand_size)
    key_pos = key_positions([place for index in arrays for place in owners[index]], rows)
    blocks = pairs_of(block_refs)
    own = [(ref, ()) for ref in pays]
    ctx = lax.axis_index("ctx")
    own_pos = key_positions([ctx ^ mask for mask in masks], cand_rows) if masks else None
    alive = stacked_rows(ctx * cand_rows, cand_rows, cand_rows) < lengths[:, :1] if last else None

    for head in range(block_refs[0].shape[3] // HEADDIM):
        key_rows = head_rows(blocks, 0, head)
        widened = with_ones(head_rows(blocks, 1, head))
        if masks:
            all_keys = jnp.concatenate([key_rows, head_rows(own, 0, head)], axis=0)
            all_widened = jnp.concatenate([widened, with_ones(head_rows(own, 1, head))], axis=0)
            free = jnp.full((1, key_rows.shape[0]), -1, jnp.int32)
            all_pos = jnp.concatenate([free, own_pos], axis=1)
        for kind, q_ref in enumerate((cand_q, prompt_q)):
            for heads, at, queries in tiles(q_ref, head):
                count = queries.shape[0]
                state = None if first else (old[kind][0][at], old[kind][1][at])
                if kind == 1:
                    first_row = prompt_place(cand_size) * rows
                    allowed = key_pos <= stacked_rows(first_row, rows, count)
                    state = absorb(queries, key_rows, widened, allowed, state)
                elif masks:
                    allowed = all_pos <= stacked_rows(ctx * cand_rows, cand_rows, count)
                    state = absorb(queries, all_keys, all_widened, allowed, state)
                else:
                    state = absorb(queries, key_rows, widened, None, state)
                if not last:
                    outs[2 * kind][at] = state[0]
                    outs[2 * kind + 1][at] = state[1]
                    continue
                result = state[1][:, :HEADDIM] / state[1][:, HEADDIM:]
                each = q_ref.shape[0]
                for index, h in enumerate(heads):
                    kept = result[index * each : (index + 1) * each]
                    if kind == 0:
                        kept = jnp.where(alive, kept, 0.0)
                    outs[kind][:, h * HEADDIM : (h + 1) * HEADDIM] = kept.astype(jnp.bfloat16)


def phase(sizes, arrays, q_rows, blocks, pays=(), state=None, lengths=None, after=()):
    prompt_q, cand_q = q_rows
    first, last = state is None, lengths is not None
    operands = [prompt_q, cand_q] + [blocks[index] for index in arrays]
    operands += [b for b, _ in pays]
    if last:
        operands.append(lengths)
    if not first:
        operands += state
    heads = prompt_q.shape[1] // HEADDIM
    if last:
        shapes = [like(cand_q), like(prompt_q)]
    else:
        shapes = []
        for q in (cand_q, prompt_q):
            count = heads * q.shape[0]
            shapes.append(jax.ShapeDtypeStruct((count, HEADDIM), jnp.float32))
            shapes.append(jax.ShapeDtypeStruct((count, 2 * HEADDIM), jnp.float32))
    key_count = sum(blocks[i].shape[0] * blocks[i].shape[2] for i in arrays)
    scores = heads * (prompt_q.shape[0] + cand_q.shape[0]) * key_count
    masks = [mask for _, mask in pays]
    return pl.pallas_call(
        functools.partial(phase_kernel, sizes, arrays, masks, first, last),
        out_shape=tuple(shapes),
        in_specs=vmem(len(operands)) + [pl.BlockSpec(memory_space=pl.ANY)] * len(after),
        out_specs=tuple(vmem(len(shapes))),
        compiler_params=PARAMS,
        cost_estimate=pl.CostEstimate(
            flops=6 * scores * HEADDIM, bytes_accessed=scores, transcendentals=scores
        ),
        name="attend_" + "_".join(str(i) for i in arrays),
    )(*operands, *after)


def step_kernel(sizes, masks, ends_ref, head_ref, lengths_ref, *refs):
    ctx_size, cand_size = sizes
    pays, blocks = refs[: len(masks)], refs[len(masks) : -2]
    logit_ref, kv_ref = refs[-2:]
    rows = blocks[0].shape[2]
    own_rows = pays[0].shape[1]
    free = rows * ctx_size * cand_size
    place = lax.axis_index("ctx")
    for ref, owners in zip(blocks, prompt_owners(ctx_size, cand_size)):
        for index, owner in enumerate(owners):
            at = pl.ds(pl.multiple_of(owner * rows, rows), rows)
            kv_ref[0, at, :] = ref[index, 0]
            kv_ref[1, at, :] = ref[index, 1]
    picked = jnp.zeros(pays[0].shape[1:], jnp.float32)
    for ref, mask in zip(pays, masks):
        at = pl.ds(pl.multiple_of(free + (place ^ mask) * own_rows, own_rows), own_rows)
        kv_ref[0, at, :] = ref[0]
        kv_ref[1, at, :] = ref[1]
        picked += ref[2].astype(jnp.float32)
    steps = ends_ref.shape[1]
    width = picked.shape[1]
    step_rows = [picked[at : at + steps] for at in range(0, steps * head_ref.shape[1] // width, steps)]

    ends = column_of(ends_ref[...])
    kinds = width // HEADDIM
    stacked = GROUP * steps
    parts = []
    for head in range(kinds):
        places = [divmod(h * HEADDIM, width) for h in range(head * GROUP, (head + 1) * GROUP)]
        part = jnp.concatenate([step_rows[a][:, b : b + HEADDIM] for a, b in places], axis=0)
        sides = [part if other == head else jnp.zeros_like(part) for other in range(kinds)]
        parts.append(jnp.concatenate(sides, axis=1))
    queries = jnp.concatenate(parts, axis=0).astype(jnp.bfloat16)
    count = kinds * stacked
    step_of = lax.rem(lax.broadcasted_iota(jnp.int32, (steps, count), 1), jnp.int32(steps))
    mine = step_of == lax.broadcasted_iota(jnp.int32, (steps, count), 0)
    row_pos = jnp.sum(jnp.where(mine, ends, 0), axis=0, keepdims=True)
    own_pos = lax.broadcasted_iota(jnp.int32, (own_rows * len(masks), 1), 0)
    scores = product(kv_ref[0], queries)
    bound = jnp.where(own_pos <= row_pos, scores[free:], NEG_FILL)
    scores = jnp.concatenate([scores[:free], bound], axis=0)
    peak = jnp.max(scores, axis=0, keepdims=True)
    weights = jnp.exp2((scores - peak) * SCALE).astype(jnp.bfloat16)
    value_rows = kv_ref[1]
    widened = jnp.concatenate([value_rows, jnp.ones_like(value_rows[:, :HEADDIM])], axis=1)
    blended = lax.dot_general(
        weights, widened, (((0,), (0,)), ((), ())), preferred_element_type=jnp.float32
    )
    total = jnp.zeros((steps, HEADDIM), jnp.float32)
    for head in range(kinds):
        mixed = blended[head * stacked : (head + 1) * stacked]
        result = mixed[:, head * HEADDIM : (head + 1) * HEADDIM] / mixed[:, width:]
        for index in range(GROUP):
            kept = jnp.where(ends < lengths_ref[:, :1], result[index * steps : (index + 1) * steps], 0.0)
            kept = kept.astype(jnp.bfloat16).astype(jnp.float32)
            h = head * GROUP + index
            total += kept * head_ref[:, h * HEADDIM : (h + 1) * HEADDIM]
    logits = jnp.sum(total, axis=1, keepdims=True)
    down = lax.broadcasted_iota(jnp.int32, (steps, steps), 0)
    right = lax.broadcasted_iota(jnp.int32, (steps, steps), 1)
    logit_ref[...] = jnp.sum(jnp.where(down == right, logits, 0.0), axis=0, keepdims=True)


def step_shares(sizes, ends, head, lengths, pays, blocks):
    ctx_size, cand_size = sizes
    rows, width = blocks[0].shape[2:]
    count = rows * ctx_size * cand_size + pays[0][0].shape[1] * ctx_size
    scores = ends.shape[1] * head.shape[1] // HEADDIM * count
    return pl.pallas_call(
        functools.partial(step_kernel, sizes, [mask for _, mask in pays]),
        out_shape=jax.ShapeDtypeStruct(ends.shape, jnp.float32),
        in_specs=vmem(3 + len(pays) + len(blocks)),
        out_specs=vmem(1)[0],
        scratch_shapes=[pltpu.VMEM((2, count, width), blocks[0].dtype)],
        compiler_params=PARAMS,
        cost_estimate=pl.CostEstimate(
            flops=6 * scores * HEADDIM, bytes_accessed=scores, transcendentals=scores
        ),
        name="step_logits",
    )(ends, head, lengths, *(b for b, _ in pays), *blocks)


def per_device(ctx_size, cand_size, prompt_q, prompt_kv, cand_q, cand_kv, cand_lengths, step_ends, reward_head):
    sizes = ctx_size, cand_size
    size = ctx_size * cand_size
    prompt_rows, cand_rows, own, payload, ends, head, lengths = staged(
        cand_lengths, prompt_q, cand_q[0], prompt_kv, cand_kv[:, 0], step_ends, reward_head[None]
    )
    q_rows = prompt_rows, cand_rows
    pays = gather_cand(payload, ctx_size)
    early, along, across, core = prompt_bits(ctx_size, cand_size)

    def across_cores(block):
        return flipped(block, PROMPT_AXES, size, core)

    def shared_out(block, even, odd):
        return lax.ppermute(
            block, PROMPT_AXES, [(i, i ^ (odd if i & core else even)) for i in range(size)]
        )

    held = own[None]
    sent = prompt_kv[None]
    for bit in early:
        held = packed(held, flipped(sent, PROMPT_AXES, size, bit))
        sent = held
    second = shared_out(held, along, across)
    third = shared_out(held, across, along)
    blocks = [held, second, third, None, across_cores(held), None, None, None]
    state = phase(sizes, [0, 4], q_rows, blocks)
    fourth = shared_out(packed(second, after=state[:1] + tuple(b for b, _ in pays[1:4])), across, along)
    blocks[3] = fourth
    blocks[5:7] = across_cores(second), across_cores(third)
    state = phase(sizes, [1, 2], q_rows, blocks, pays=pays, state=state)
    blocks[7] = across_cores(packed(fourth, after=state[:1]))
    state = phase(sizes, [5, 6], q_rows, blocks, state=state)
    step_logits = step_shares(sizes, ends, head, lengths, pays, blocks)
    cand_out, prompt_out = phase(sizes, [3, 7], q_rows, blocks, state=state, lengths=lengths)
    tp_size = lax.axis_size("tp")
    for bit in high_bits(tp_size, 1):
        step_logits = step_logits + flipped(step_logits, "tp", tp_size, bit)
    return (prompt_out, cand_out[None], step_logits)


def solution(mesh):
    placed = (
        P(("ctx", "cand"), "tp"),
        P(None, ("ctx", "cand"), "tp"),
        P("cand", "ctx", "tp"),
        P(None, "cand", "ctx", "tp"),
        P("cand"),
        P("cand", None),
        P("tp"),
    )
    return jax.shard_map(
        functools.partial(per_device, mesh.shape["ctx"], mesh.shape["cand"]),
        mesh=mesh,
        in_specs=placed,
        out_specs=(P(("ctx", "cand"), "tp"), P("cand", "ctx", "tp"), P("cand", None)),
        check_vma=False,
    )
```

```python
import functools
import math

import jax
import jax.numpy as jnp
from jax import lax
from jax.experimental import pallas as pl
from jax.experimental.pallas import tpu as pltpu
from jax.sharding import PartitionSpec as P

HEADDIM = 128
GROUP = 8
SUBLANES = 8
NEG_FILL = -1e30
SCALE = HEADDIM ** -0.5 * math.log2(math.e)
ROW_TILE = 256
VMEM_LIMIT = 28 * 1024 * 1024
PARAMS = pltpu.CompilerParams(vmem_limit_bytes=VMEM_LIMIT)
PROMPT_AXES = ("ctx", "cand")


def vmem(count):
    return [pl.BlockSpec(memory_space=pltpu.VMEM)] * count


def like(array):
    return jax.ShapeDtypeStruct(array.shape, array.dtype)


def high_bits(size, lowest):
    return [1 << b for b in reversed(range(size.bit_length() - 1)) if 1 << b >= lowest]


def flipped(block, axes, size, bit):
    return lax.ppermute(block, axes, [(i, i ^ bit) for i in range(size)])


def pack_kernel(count, *refs):
    sources, out_ref = refs[:count], refs[-1]
    start = 0
    for ref in sources:
        out_ref[start : start + ref.shape[0]] = ref[...]
        start += ref.shape[0]


def packed(*arrays, after=()):
    count = sum(a.shape[0] for a in arrays)
    return pl.pallas_call(
        functools.partial(pack_kernel, len(arrays)),
        out_shape=jax.ShapeDtypeStruct((count,) + arrays[0].shape[1:], arrays[0].dtype),
        in_specs=vmem(len(arrays)) + [pl.BlockSpec(memory_space=pl.ANY)] * len(after),
        out_specs=vmem(1)[0],
        compiler_params=PARAMS,
        name="pack_blocks",
    )(*arrays, *after)


def prompt_bits(ctx_size, cand_size):
    core, along, across = cand_size, 1, 2 * cand_size
    early = high_bits(cand_size, 2) + [bit * cand_size for bit in high_bits(ctx_size, 4)]
    return early, along, across, core


def prompt_owners(ctx_size, cand_size):
    early, along, across, core = prompt_bits(ctx_size, cand_size)
    place = lax.axis_index("ctx") * cand_size + lax.axis_index("cand")
    odd = lax.rem(lax.axis_index("ctx"), 2)
    near = along + odd * (across - along)
    far = along + across - near
    masks = [0]
    for bit in early:
        masks += [mask ^ bit for mask in masks]
    shifts = [0, near, far, along + across, core, core + far, core + near, core + along + across]
    return [[place ^ mask ^ shift for mask in masks] for shift in shifts]


def gather_cand(own, ctx_size):
    blocks = [(own, 0), (flipped(own, "ctx", ctx_size, 1), 1)]
    for bit in reversed(high_bits(ctx_size, 2)):
        rail = [(flipped(b, "ctx", ctx_size, bit), mask | bit) for b, mask in blocks if not mask & 1]
        blocks += rail + [(flipped(b, "ctx", ctx_size, 1), mask | 1) for b, mask in rail]
    return blocks


def stage_kernel(prompt_q, cand_q, prompt_kv, cand_kv, ends, head, *refs):
    q_out, cand_out, own_out, pay_out, ends_out, head_out, sems = refs
    steps = ends.shape[1]
    pairs = [
        (cand_q, cand_out),
        (ends, ends_out),
        (prompt_kv, own_out),
        (cand_kv, pay_out.at[0:2]),
        (prompt_q, q_out),
        (head, head_out),
    ]
    copies = [pltpu.make_async_copy(a, b, sems.at[i]) for i, (a, b) in enumerate(pairs)]
    for copy in copies:
        copy.start()
    copies[0].wait()
    copies[1].wait()
    rows = cand_out.shape[0]
    ends_column = column_of(ends_out[...])
    row_pos = lax.axis_index("ctx") * rows + lax.broadcasted_iota(jnp.int32, (steps, rows), 1)
    chosen = (row_pos == ends_column).astype(jnp.bfloat16)
    picked = jnp.dot(chosen, cand_out[...], preferred_element_type=jnp.float32)
    width = pay_out.shape[2]
    pieces = [picked[:, at : at + width] for at in range(0, picked.shape[1], width)]
    pay_out[2] = jnp.concatenate(pieces, axis=0).astype(jnp.bfloat16)
    for copy in copies[2:]:
        copy.wait()


def column_of(row):
    count = row.shape[1]
    down = lax.broadcasted_iota(jnp.int32, (count, count), 0)
    right = lax.broadcasted_iota(jnp.int32, (count, count), 1)
    return jnp.sum(jnp.where(down == right, row, 0), axis=1, keepdims=True)


def length_of(ends):
    return ends[:, ends.shape[1] - 1 :] + 1


def staged(prompt_q, cand_q, prompt_kv, cand_kv, ends, head):
    arrays = (prompt_q, cand_q, prompt_kv, cand_kv, ends, head)
    pay = jax.ShapeDtypeStruct((3,) + cand_kv.shape[1:], cand_kv.dtype)
    return pl.pallas_call(
        stage_kernel,
        out_shape=(like(prompt_q), like(cand_q), like(prompt_kv), pay, like(ends), like(head)),
        in_specs=[pl.BlockSpec(memory_space=pltpu.HBM)] * len(arrays),
        out_specs=tuple(vmem(6)),
        scratch_shapes=[pltpu.SemaphoreType.DMA((len(arrays),))],
        compiler_params=PARAMS,
        name="stage_operands",
    )(*(pltpu.with_memory_space_constraint(a, pltpu.HBM) for a in arrays))


def tiles(q_ref, head):
    rows = q_ref.shape[0]
    fan = max(1, ROW_TILE // rows)
    for start in range(head * GROUP, (head + 1) * GROUP, fan):
        heads = range(start, start + fan)
        queries = jnp.concatenate([q_ref[:, h * HEADDIM : (h + 1) * HEADDIM] for h in heads], axis=0)
        yield heads, slice(start * rows, (start + fan) * rows), queries


def stacked_rows(first_row, rows, count):
    return first_row + lax.rem(lax.broadcasted_iota(jnp.int32, (count, 1), 0), jnp.int32(rows))


def product(queries, key_rows):
    return lax.dot_general(
        queries, key_rows, (((1,), (1,)), ((), ())), preferred_element_type=jnp.float32
    )


def with_ones(value_rows):
    return jnp.concatenate([value_rows, jnp.ones_like(value_rows)], axis=1)


def head_rows(blocks, which, head):
    columns = slice(head * HEADDIM, (head + 1) * HEADDIM)
    return jnp.concatenate([ref[lead + (which,)][:, columns] for ref, lead in blocks], axis=0)


def key_positions(owners, rows):
    lane = lax.broadcasted_iota(jnp.int32, (1, len(owners) * rows), 1)
    positions = lane
    for index, owner in enumerate(owners):
        inside = (lane >= index * rows) & (lane < (index + 1) * rows)
        positions = jnp.where(inside, lane + (owner - index) * rows, positions)
    return positions


def spread(column, count):
    return jnp.concatenate([column] * (count // column.shape[1]), axis=1)


def absorb(queries, key_rows, widened, allowed, old):
    scores = product(queries, key_rows)
    if allowed is not None:
        scores = jnp.where(allowed, scores, NEG_FILL)
    count = scores.shape[1]
    peak = jnp.broadcast_to(jnp.max(scores, axis=1, keepdims=True), (scores.shape[0], HEADDIM))
    if old is not None:
        peak = jnp.maximum(peak, old[0])
    weights = jnp.exp2((scores - spread(peak, count)) * SCALE).astype(jnp.bfloat16)
    blended = jnp.dot(weights, widened, preferred_element_type=jnp.float32)
    if old is not None:
        blended += old[1] * spread(jnp.exp2((old[0] - peak) * SCALE), old[1].shape[1])
    return peak, blended


def prompt_place(cand_size):
    return lax.axis_index("ctx") * cand_size + lax.axis_index("cand")


def pairs_of(refs):
    return [(ref, (index,)) for ref in refs for index in range(ref.shape[0])]


def phase_kernel(sizes, arrays, masks, first, last, *refs):
    ctx_size, cand_size = sizes
    take = iter(refs)
    prompt_q, cand_q = next(take), next(take)
    block_refs = [next(take) for _ in arrays]
    pays = [next(take) for _ in masks]
    ends = next(take) if last else None
    old = None if first else [(next(take), next(take)) for _ in range(2)]
    outs = refs[-2:] if last else refs[-4:]
    rows = prompt_q.shape[0]
    cand_rows = cand_q.shape[0]
    owners = prompt_owners(ctx_size, cand_size)
    key_pos = key_positions([place for index in arrays for place in owners[index]], rows)
    blocks = pairs_of(block_refs)
    own = [(ref, ()) for ref in pays]
    ctx = lax.axis_index("ctx")
    own_pos = key_positions([ctx ^ mask for mask in masks], cand_rows) if masks else None
    alive = stacked_rows(ctx * cand_rows, cand_rows, cand_rows) < length_of(ends[...]) if last else None

    for head in range(block_refs[0].shape[3] // HEADDIM):
        key_rows = head_rows(blocks, 0, head)
        widened = with_ones(head_rows(blocks, 1, head))
        if masks:
            all_keys = jnp.concatenate([key_rows, head_rows(own, 0, head)], axis=0)
            all_widened = jnp.concatenate([widened, with_ones(head_rows(own, 1, head))], axis=0)
            free = jnp.full((1, key_rows.shape[0]), -1, jnp.int32)
            all_pos = jnp.concatenate([free, own_pos], axis=1)
        for kind, q_ref in enumerate((cand_q, prompt_q)):
            for heads, at, queries in tiles(q_ref, head):
                count = queries.shape[0]
                state = None if first else (old[kind][0][at], old[kind][1][at])
                if kind == 1:
                    first_row = prompt_place(cand_size) * rows
                    allowed = key_pos <= stacked_rows(first_row, rows, count)
                    state = absorb(queries, key_rows, widened, allowed, state)
                elif masks:
                    allowed = all_pos <= stacked_rows(ctx * cand_rows, cand_rows, count)
                    state = absorb(queries, all_keys, all_widened, allowed, state)
                else:
                    state = absorb(queries, key_rows, widened, None, state)
                if not last:
                    outs[2 * kind][at] = state[0]
                    outs[2 * kind + 1][at] = state[1]
                    continue
                result = state[1][:, :HEADDIM] / state[1][:, HEADDIM:]
                each = q_ref.shape[0]
                for index, h in enumerate(heads):
                    kept = result[index * each : (index + 1) * each]
                    if kind == 0:
                        kept = jnp.where(alive, kept, 0.0)
                    outs[kind][:, h * HEADDIM : (h + 1) * HEADDIM] = kept.astype(jnp.bfloat16)


def phase(sizes, arrays, q_rows, blocks, pays=(), state=None, ends=None, after=()):
    prompt_q, cand_q = q_rows
    first, last = state is None, ends is not None
    operands = [prompt_q, cand_q] + [blocks[index] for index in arrays]
    operands += [b for b, _ in pays]
    if last:
        operands.append(ends)
    if not first:
        operands += state
    heads = prompt_q.shape[1] // HEADDIM
    if last:
        shapes = [like(cand_q), like(prompt_q)]
    else:
        shapes = []
        for q in (cand_q, prompt_q):
            count = heads * q.shape[0]
            shapes.append(jax.ShapeDtypeStruct((count, HEADDIM), jnp.float32))
            shapes.append(jax.ShapeDtypeStruct((count, 2 * HEADDIM), jnp.float32))
    key_count = sum(blocks[i].shape[0] * blocks[i].shape[2] for i in arrays)
    scores = heads * (prompt_q.shape[0] + cand_q.shape[0]) * key_count
    masks = [mask for _, mask in pays]
    return pl.pallas_call(
        functools.partial(phase_kernel, sizes, arrays, masks, first, last),
        out_shape=tuple(shapes),
        in_specs=vmem(len(operands)) + [pl.BlockSpec(memory_space=pl.ANY)] * len(after),
        out_specs=tuple(vmem(len(shapes))),
        compiler_params=PARAMS,
        cost_estimate=pl.CostEstimate(
            flops=6 * scores * HEADDIM, bytes_accessed=scores, transcendentals=scores
        ),
        name="attend_" + "_".join(str(i) for i in arrays),
    )(*operands, *after)


def step_kernel(sizes, masks, ends_ref, head_ref, *refs):
    ctx_size, cand_size = sizes
    pays, blocks = refs[: len(masks)], refs[len(masks) : -2]
    logit_ref, kv_ref = refs[-2:]
    rows = blocks[0].shape[2]
    own_rows = pays[0].shape[1]
    free = rows * ctx_size * cand_size
    place = lax.axis_index("ctx")
    for ref, owners in zip(blocks, prompt_owners(ctx_size, cand_size)):
        for index, owner in enumerate(owners):
            at = pl.ds(pl.multiple_of(owner * rows, rows), rows)
            kv_ref[0, at, :] = ref[index, 0]
            kv_ref[1, at, :] = ref[index, 1]
    picked = jnp.zeros(pays[0].shape[1:], jnp.float32)
    for ref, mask in zip(pays, masks):
        at = pl.ds(pl.multiple_of(free + (place ^ mask) * own_rows, own_rows), own_rows)
        kv_ref[0, at, :] = ref[0]
        kv_ref[1, at, :] = ref[1]
        picked += ref[2].astype(jnp.float32)
    steps = ends_ref.shape[1]
    width = picked.shape[1]
    step_rows = [picked[at : at + steps] for at in range(0, steps * head_ref.shape[1] // width, steps)]

    ends = column_of(ends_ref[...])
    alive = ends < length_of(ends_ref[...])
    own_pos = lax.broadcasted_iota(jnp.int32, (1, own_rows * len(masks)), 1)
    row_pos = jnp.concatenate([ends] * GROUP, axis=0)
    total = jnp.zeros((steps, HEADDIM), jnp.float32)
    for head in range(width // HEADDIM):
        columns = slice(head * HEADDIM, (head + 1) * HEADDIM)
        heads = range(head * GROUP, (head + 1) * GROUP)
        places = [divmod(h * HEADDIM, width) for h in heads]
        queries = jnp.concatenate([step_rows[a][:, b : b + HEADDIM] for a, b in places], axis=0)
        scores = product(queries.astype(jnp.bfloat16), kv_ref[0, :, columns])
        bound = jnp.where(own_pos <= row_pos, scores[:, free:], NEG_FILL)
        scores = jnp.concatenate([scores[:, :free], bound], axis=1)
        peak = jnp.max(scores, axis=1, keepdims=True)
        weights = jnp.exp2((scores - peak) * SCALE).astype(jnp.bfloat16)
        blended = jnp.dot(weights, with_ones(kv_ref[1, :, columns]), preferred_element_type=jnp.float32)
        result = blended[:, :HEADDIM] / blended[:, HEADDIM:]
        for index, h in enumerate(heads):
            kept = jnp.where(alive, result[index * steps : (index + 1) * steps], 0.0)
            kept = kept.astype(jnp.bfloat16).astype(jnp.float32)
            total += kept * head_ref[:, h * HEADDIM : (h + 1) * HEADDIM]
    logits = jnp.sum(total, axis=1, keepdims=True)
    down = lax.broadcasted_iota(jnp.int32, (steps, steps), 0)
    right = lax.broadcasted_iota(jnp.int32, (steps, steps), 1)
    logit_ref[...] = jnp.sum(jnp.where(down == right, logits, 0.0), axis=0, keepdims=True)


def step_shares(sizes, ends, head, pays, blocks):
    ctx_size, cand_size = sizes
    rows, width = blocks[0].shape[2:]
    count = rows * ctx_size * cand_size + pays[0][0].shape[1] * ctx_size
    scores = ends.shape[1] * head.shape[1] // HEADDIM * count
    return pl.pallas_call(
        functools.partial(step_kernel, sizes, [mask for _, mask in pays]),
        out_shape=jax.ShapeDtypeStruct(ends.shape, jnp.float32),
        in_specs=vmem(2 + len(pays) + len(blocks)),
        out_specs=vmem(1)[0],
        scratch_shapes=[pltpu.VMEM((2, count, width), blocks[0].dtype)],
        compiler_params=PARAMS,
        cost_estimate=pl.CostEstimate(
            flops=6 * scores * HEADDIM, bytes_accessed=scores, transcendentals=scores
        ),
        name="step_logits",
    )(ends, head, *(b for b, _ in pays), *blocks)


def per_device(ctx_size, cand_size, prompt_q, prompt_kv, cand_q, cand_kv, cand_lengths, step_ends, reward_head):
    sizes = ctx_size, cand_size
    size = ctx_size * cand_size
    prompt_rows, cand_rows, own, payload, ends, head = staged(
        prompt_q, cand_q[0], prompt_kv, cand_kv[:, 0], step_ends, reward_head[None]
    )
    q_rows = prompt_rows, cand_rows
    pays = gather_cand(payload, ctx_size)
    early, along, across, core = prompt_bits(ctx_size, cand_size)

    def across_cores(block):
        return flipped(block, PROMPT_AXES, size, core)

    def shared_out(block, even, odd):
        return lax.ppermute(
            block, PROMPT_AXES, [(i, i ^ (odd if i & core else even)) for i in range(size)]
        )

    held = own[None]
    sent = prompt_kv[None]
    for bit in early:
        held = packed(held, flipped(sent, PROMPT_AXES, size, bit))
        sent = held
    second = shared_out(held, along, across)
    third = shared_out(held, across, along)
    blocks = [held, second, third, None, across_cores(held), None, None, None]
    state = phase(sizes, [0, 4], q_rows, blocks)
    fourth = shared_out(packed(second, after=state[:1] + tuple(b for b, _ in pays[1:4])), across, along)
    blocks[3] = fourth
    blocks[5:7] = across_cores(second), across_cores(third)
    state = phase(sizes, [1, 2], q_rows, blocks, pays=pays, state=state)
    blocks[7] = across_cores(packed(fourth, after=state[:1]))
    state = phase(sizes, [5, 6], q_rows, blocks, state=state)
    step_logits = step_shares(sizes, ends, head, pays, blocks)
    cand_out, prompt_out = phase(sizes, [3, 7], q_rows, blocks, state=state, ends=ends)
    tp_size = lax.axis_size("tp")
    for bit in high_bits(tp_size, 1):
        step_logits = step_logits + flipped(step_logits, "tp", tp_size, bit)
    return (prompt_out, cand_out[None], step_logits)


def solution(mesh):
    placed = (
        P(("ctx", "cand"), "tp"),
        P(None, ("ctx", "cand"), "tp"),
        P("cand", "ctx", "tp"),
        P(None, "cand", "ctx", "tp"),
        P("cand"),
        P("cand", None),
        P("tp"),
    )
    return jax.shard_map(
        functools.partial(per_device, mesh.shape["ctx"], mesh.shape["cand"]),
        mesh=mesh,
        in_specs=placed,
        out_specs=(P(("ctx", "cand"), "tp"), P("cand", "ctx", "tp"), P("cand", None)),
        check_vma=False,
    )
```

```python
import functools
import math

import jax
import jax.numpy as jnp
from jax import lax
from jax.experimental import pallas as pl
from jax.experimental.pallas import tpu as pltpu
from jax.sharding import PartitionSpec as P

HEADDIM = 128
GROUP = 8
SUBLANES = 8
NEG_FILL = -1e30
SCALE = HEADDIM ** -0.5 * math.log2(math.e)
ROW_TILE = 256
VMEM_LIMIT = 28 * 1024 * 1024
PARAMS = pltpu.CompilerParams(vmem_limit_bytes=VMEM_LIMIT)
PROMPT_AXES = ("ctx", "cand")


def vmem(count):
    return [pl.BlockSpec(memory_space=pltpu.VMEM)] * count


def like(array):
    return jax.ShapeDtypeStruct(array.shape, array.dtype)


def high_bits(size, lowest):
    return [1 << b for b in reversed(range(size.bit_length() - 1)) if 1 << b >= lowest]


def flipped(block, axes, size, bit):
    return lax.ppermute(block, axes, [(i, i ^ bit) for i in range(size)])


def pack_kernel(count, *refs):
    sources, out_ref = refs[:count], refs[-1]
    start = 0
    for ref in sources:
        out_ref[start : start + ref.shape[0]] = ref[...]
        start += ref.shape[0]


def packed(*arrays, after=()):
    count = sum(a.shape[0] for a in arrays)
    return pl.pallas_call(
        functools.partial(pack_kernel, len(arrays)),
        out_shape=jax.ShapeDtypeStruct((count,) + arrays[0].shape[1:], arrays[0].dtype),
        in_specs=vmem(len(arrays)) + [pl.BlockSpec(memory_space=pl.ANY)] * len(after),
        out_specs=vmem(1)[0],
        compiler_params=PARAMS,
        name="pack_blocks",
    )(*arrays, *after)


def prompt_bits(ctx_size, cand_size):
    core, along, across = cand_size, 1, 2 * cand_size
    early = high_bits(cand_size, 2) + [bit * cand_size for bit in high_bits(ctx_size, 4)]
    return early, along, across, core


def prompt_owners(ctx_size, cand_size):
    early, along, across, core = prompt_bits(ctx_size, cand_size)
    place = lax.axis_index("ctx") * cand_size + lax.axis_index("cand")
    odd = lax.rem(lax.axis_index("ctx"), 2)
    near = along + odd * (across - along)
    far = along + across - near
    masks = [0]
    for bit in early:
        masks += [mask ^ bit for mask in masks]
    shifts = [0, near, far, along + across, core, core + far, core + near, core + along + across]
    return [[place ^ mask ^ shift for mask in masks] for shift in shifts]


def gather_cand(own, ctx_size):
    blocks = [(own, 0), (flipped(own, "ctx", ctx_size, 1), 1)]
    for bit in reversed(high_bits(ctx_size, 2)):
        rail = [(flipped(b, "ctx", ctx_size, bit), mask | bit) for b, mask in blocks if not mask & 1]
        blocks += rail + [(flipped(b, "ctx", ctx_size, 1), mask | 1) for b, mask in rail]
    return blocks


def stage_kernel(prompt_q, cand_q, prompt_kv, cand_kv, ends, head, *refs):
    q_out, cand_out, own_out, pay_out, ends_out, head_out, sems = refs
    steps = ends.shape[1]
    pairs = [
        (cand_q, cand_out),
        (ends, ends_out),
        (prompt_kv, own_out),
        (cand_kv, pay_out.at[0:2]),
        (prompt_q, q_out),
        (head, head_out),
    ]
    copies = [pltpu.make_async_copy(a, b, sems.at[i]) for i, (a, b) in enumerate(pairs)]
    for copy in copies:
        copy.start()
    copies[0].wait()
    copies[1].wait()
    rows = cand_out.shape[0]
    ends_column = column_of(ends_out[...])
    row_pos = lax.axis_index("ctx") * rows + lax.broadcasted_iota(jnp.int32, (steps, rows), 1)
    chosen = (row_pos == ends_column).astype(jnp.bfloat16)
    picked = jnp.dot(chosen, cand_out[...], preferred_element_type=jnp.float32)
    width = pay_out.shape[2]
    pieces = [picked[:, at : at + width] for at in range(0, picked.shape[1], width)]
    pay_out[2] = jnp.concatenate(pieces, axis=0).astype(jnp.bfloat16)
    for copy in copies[2:]:
        copy.wait()


def column_of(row):
    count = row.shape[1]
    down = lax.broadcasted_iota(jnp.int32, (count, count), 0)
    right = lax.broadcasted_iota(jnp.int32, (count, count), 1)
    return jnp.sum(jnp.where(down == right, row, 0), axis=1, keepdims=True)


def length_of(ends):
    return ends[:, ends.shape[1] - 1 :] + 1


def staged(prompt_q, cand_q, prompt_kv, cand_kv, ends, head):
    arrays = (prompt_q, cand_q, prompt_kv, cand_kv, ends, head)
    pay = jax.ShapeDtypeStruct((3,) + cand_kv.shape[1:], cand_kv.dtype)
    return pl.pallas_call(
        stage_kernel,
        out_shape=(like(prompt_q), like(cand_q), like(prompt_kv), pay, like(ends), like(head)),
        in_specs=[pl.BlockSpec(memory_space=pltpu.HBM)] * len(arrays),
        out_specs=tuple(vmem(6)),
        scratch_shapes=[pltpu.SemaphoreType.DMA((len(arrays),))],
        compiler_params=PARAMS,
        name="stage_operands",
    )(*(pltpu.with_memory_space_constraint(a, pltpu.HBM) for a in arrays))


def tiles(q_ref, head):
    rows = q_ref.shape[0]
    fan = max(1, ROW_TILE // rows)
    for start in range(head * GROUP, (head + 1) * GROUP, fan):
        heads = range(start, start + fan)
        queries = jnp.concatenate([q_ref[:, h * HEADDIM : (h + 1) * HEADDIM] for h in heads], axis=0)
        yield heads, slice(start * rows, (start + fan) * rows), queries


def stacked_rows(first_row, rows, count):
    return first_row + lax.rem(lax.broadcasted_iota(jnp.int32, (count, 1), 0), jnp.int32(rows))


def product(queries, key_rows):
    return lax.dot_general(
        queries, key_rows, (((1,), (1,)), ((), ())), preferred_element_type=jnp.float32
    )


def with_ones(value_rows):
    return jnp.concatenate([value_rows, jnp.ones_like(value_rows)], axis=1)


def head_rows(blocks, which, head):
    columns = slice(head * HEADDIM, (head + 1) * HEADDIM)
    return jnp.concatenate([ref[lead + (which,)][:, columns] for ref, lead in blocks], axis=0)


def key_positions(owners, rows):
    lane = lax.broadcasted_iota(jnp.int32, (1, len(owners) * rows), 1)
    positions = lane
    for index, owner in enumerate(owners):
        inside = (lane >= index * rows) & (lane < (index + 1) * rows)
        positions = jnp.where(inside, lane + (owner - index) * rows, positions)
    return positions


def spread(column, count):
    return jnp.concatenate([column] * (count // column.shape[1]), axis=1)


def absorb(queries, key_rows, widened, allowed, old):
    scores = product(queries, key_rows)
    if allowed is not None:
        scores = jnp.where(allowed, scores, NEG_FILL)
    count = scores.shape[1]
    peak = jnp.broadcast_to(jnp.max(scores, axis=1, keepdims=True), (scores.shape[0], HEADDIM))
    if old is not None:
        peak = jnp.maximum(peak, old[0])
    weights = jnp.exp2((scores - spread(peak, count)) * SCALE).astype(jnp.bfloat16)
    blended = jnp.dot(weights, widened, preferred_element_type=jnp.float32)
    if old is not None:
        blended += old[1] * spread(jnp.exp2((old[0] - peak) * SCALE), old[1].shape[1])
    return peak, blended


def prompt_place(cand_size):
    return lax.axis_index("ctx") * cand_size + lax.axis_index("cand")


def pairs_of(refs):
    return [(ref, (index,)) for ref in refs for index in range(ref.shape[0])]


def phase_kernel(sizes, arrays, masks, first, last, *refs):
    ctx_size, cand_size = sizes
    take = iter(refs)
    prompt_q, cand_q = next(take), next(take)
    block_refs = [next(take) for _ in arrays]
    pays = [next(take) for _ in masks]
    ends = next(take) if last else None
    old = None if first else [(next(take), next(take)) for _ in range(2)]
    outs = refs[-2:] if last else refs[-4:]
    rows = prompt_q.shape[0]
    cand_rows = cand_q.shape[0]
    owners = prompt_owners(ctx_size, cand_size)
    key_pos = key_positions([place for index in arrays for place in owners[index]], rows)
    blocks = pairs_of(block_refs)
    own = [(ref, ()) for ref in pays]
    ctx = lax.axis_index("ctx")
    own_pos = key_positions([ctx ^ mask for mask in masks], cand_rows) if masks else None
    alive = stacked_rows(ctx * cand_rows, cand_rows, cand_rows) < length_of(ends[...]) if last else None

    for head in range(block_refs[0].shape[3] // HEADDIM):
        key_rows = head_rows(blocks, 0, head)
        widened = with_ones(head_rows(blocks, 1, head))
        if masks:
            all_keys = jnp.concatenate([key_rows, head_rows(own, 0, head)], axis=0)
            all_widened = jnp.concatenate([widened, with_ones(head_rows(own, 1, head))], axis=0)
            free = jnp.full((1, key_rows.shape[0]), -1, jnp.int32)
            all_pos = jnp.concatenate([free, own_pos], axis=1)
        for kind, q_ref in enumerate((cand_q, prompt_q)):
            for heads, at, queries in tiles(q_ref, head):
                count = queries.shape[0]
                state = None if first else (old[kind][0][at], old[kind][1][at])
                if kind == 1:
                    first_row = prompt_place(cand_size) * rows
                    allowed = key_pos <= stacked_rows(first_row, rows, count)
                    state = absorb(queries, key_rows, widened, allowed, state)
                elif masks:
                    allowed = all_pos <= stacked_rows(ctx * cand_rows, cand_rows, count)
                    state = absorb(queries, all_keys, all_widened, allowed, state)
                else:
                    state = absorb(queries, key_rows, widened, None, state)
                if not last:
                    outs[2 * kind][at] = state[0]
                    outs[2 * kind + 1][at] = state[1]
                    continue
                result = state[1][:, :HEADDIM] / state[1][:, HEADDIM:]
                each = q_ref.shape[0]
                for index, h in enumerate(heads):
                    kept = result[index * each : (index + 1) * each]
                    if kind == 0:
                        kept = jnp.where(alive, kept, 0.0)
                    outs[kind][:, h * HEADDIM : (h + 1) * HEADDIM] = kept.astype(jnp.bfloat16)


def phase(sizes, arrays, q_rows, blocks, pays=(), state=None, ends=None, after=()):
    prompt_q, cand_q = q_rows
    first, last = state is None, ends is not None
    operands = [prompt_q, cand_q] + [blocks[index] for index in arrays]
    operands += [b for b, _ in pays]
    if last:
        operands.append(ends)
    if not first:
        operands += state
    heads = prompt_q.shape[1] // HEADDIM
    if last:
        shapes = [like(cand_q), like(prompt_q)]
    else:
        shapes = []
        for q in (cand_q, prompt_q):
            count = heads * q.shape[0]
            shapes.append(jax.ShapeDtypeStruct((count, HEADDIM), jnp.float32))
            shapes.append(jax.ShapeDtypeStruct((count, 2 * HEADDIM), jnp.float32))
    key_count = sum(blocks[i].shape[0] * blocks[i].shape[2] for i in arrays)
    scores = heads * (prompt_q.shape[0] + cand_q.shape[0]) * key_count
    masks = [mask for _, mask in pays]
    return pl.pallas_call(
        functools.partial(phase_kernel, sizes, arrays, masks, first, last),
        out_shape=tuple(shapes),
        in_specs=vmem(len(operands)) + [pl.BlockSpec(memory_space=pl.ANY)] * len(after),
        out_specs=tuple(vmem(len(shapes))),
        compiler_params=PARAMS,
        cost_estimate=pl.CostEstimate(
            flops=6 * scores * HEADDIM, bytes_accessed=scores, transcendentals=scores
        ),
        name="attend_" + "_".join(str(i) for i in arrays),
    )(*operands, *after)


def step_kernel(sizes, masks, ends_ref, head_ref, *refs):
    ctx_size, cand_size = sizes
    pays, blocks = refs[: len(masks)], refs[len(masks) : -2]
    logit_ref, kv_ref = refs[-2:]
    rows = blocks[0].shape[2]
    own_rows = pays[0].shape[1]
    free = rows * ctx_size * cand_size
    place = lax.axis_index("ctx")
    for ref, owners in zip(blocks, prompt_owners(ctx_size, cand_size)):
        for index, owner in enumerate(owners):
            at = pl.ds(pl.multiple_of(owner * rows, rows), rows)
            kv_ref[0, at, :] = ref[index, 0]
            kv_ref[1, at, :] = ref[index, 1]
    picked = jnp.zeros(pays[0].shape[1:], jnp.float32)
    for ref, mask in zip(pays, masks):
        at = pl.ds(pl.multiple_of(free + (place ^ mask) * own_rows, own_rows), own_rows)
        kv_ref[0, at, :] = ref[0]
        kv_ref[1, at, :] = ref[1]
        picked += ref[2].astype(jnp.float32)
    steps = ends_ref.shape[1]
    width = picked.shape[1]
    step_rows = [picked[at : at + steps] for at in range(0, steps * head_ref.shape[1] // width, steps)]

    ends = column_of(ends_ref[...])
    alive = ends < length_of(ends_ref[...])
    kinds = width // HEADDIM
    stacked = GROUP * steps
    parts = []
    for head in range(kinds):
        places = [divmod(h * HEADDIM, width) for h in range(head * GROUP, (head + 1) * GROUP)]
        part = jnp.concatenate([step_rows[a][:, b : b + HEADDIM] for a, b in places], axis=0)
        sides = [part if other == head else jnp.zeros_like(part) for other in range(kinds)]
        parts.append(jnp.concatenate(sides, axis=1))
    queries = jnp.concatenate(parts, axis=0).astype(jnp.bfloat16)
    own_pos = lax.broadcasted_iota(jnp.int32, (1, own_rows * len(masks)), 1)
    row_pos = jnp.concatenate([ends] * (GROUP * kinds), axis=0)
    scores = product(queries, kv_ref[0])
    bound = jnp.where(own_pos <= row_pos, scores[:, free:], NEG_FILL)
    scores = jnp.concatenate([scores[:, :free], bound], axis=1)
    peak = jnp.max(scores, axis=1, keepdims=True)
    weights = jnp.exp2((scores - peak) * SCALE).astype(jnp.bfloat16)
    value_rows = kv_ref[1]
    widened = jnp.concatenate([value_rows, jnp.ones_like(value_rows[:, :HEADDIM])], axis=1)
    blended = jnp.dot(weights, widened, preferred_element_type=jnp.float32)
    total = jnp.zeros((steps, HEADDIM), jnp.float32)
    for head in range(kinds):
        mixed = blended[head * stacked : (head + 1) * stacked]
        result = mixed[:, head * HEADDIM : (head + 1) * HEADDIM] / mixed[:, width:]
        for index in range(GROUP):
            kept = jnp.where(alive, result[index * steps : (index + 1) * steps], 0.0)
            kept = kept.astype(jnp.bfloat16).astype(jnp.float32)
            h = head * GROUP + index
            total += kept * head_ref[:, h * HEADDIM : (h + 1) * HEADDIM]
    logits = jnp.sum(total, axis=1, keepdims=True)
    down = lax.broadcasted_iota(jnp.int32, (steps, steps), 0)
    right = lax.broadcasted_iota(jnp.int32, (steps, steps), 1)
    logit_ref[...] = jnp.sum(jnp.where(down == right, logits, 0.0), axis=0, keepdims=True)


def step_shares(sizes, ends, head, pays, blocks):
    ctx_size, cand_size = sizes
    rows, width = blocks[0].shape[2:]
    count = rows * ctx_size * cand_size + pays[0][0].shape[1] * ctx_size
    scores = ends.shape[1] * head.shape[1] // HEADDIM * count
    return pl.pallas_call(
        functools.partial(step_kernel, sizes, [mask for _, mask in pays]),
        out_shape=jax.ShapeDtypeStruct(ends.shape, jnp.float32),
        in_specs=vmem(2 + len(pays) + len(blocks)),
        out_specs=vmem(1)[0],
        scratch_shapes=[pltpu.VMEM((2, count, width), blocks[0].dtype)],
        compiler_params=PARAMS,
        cost_estimate=pl.CostEstimate(
            flops=6 * scores * HEADDIM, bytes_accessed=scores, transcendentals=scores
        ),
        name="step_logits",
    )(ends, head, *(b for b, _ in pays), *blocks)


def per_device(ctx_size, cand_size, prompt_q, prompt_kv, cand_q, cand_kv, cand_lengths, step_ends, reward_head):
    sizes = ctx_size, cand_size
    size = ctx_size * cand_size
    prompt_rows, cand_rows, own, payload, ends, head = staged(
        prompt_q, cand_q[0], prompt_kv, cand_kv[:, 0], step_ends, reward_head[None]
    )
    q_rows = prompt_rows, cand_rows
    pays = gather_cand(payload, ctx_size)
    early, along, across, core = prompt_bits(ctx_size, cand_size)

    def across_cores(block):
        return flipped(block, PROMPT_AXES, size, core)

    def shared_out(block, even, odd):
        return lax.ppermute(
            block, PROMPT_AXES, [(i, i ^ (odd if i & core else even)) for i in range(size)]
        )

    held = own[None]
    sent = prompt_kv[None]
    for bit in early:
        held = packed(held, flipped(sent, PROMPT_AXES, size, bit))
        sent = held
    second = shared_out(held, along, across)
    third = shared_out(held, across, along)
    blocks = [held, second, third, None, across_cores(held), None, None, None]
    state = phase(sizes, [0, 4], q_rows, blocks)
    fourth = shared_out(packed(second, after=state[:1] + tuple(b for b, _ in pays[1:4])), across, along)
    blocks[3] = fourth
    blocks[5:7] = across_cores(second), across_cores(third)
    state = phase(sizes, [1, 2], q_rows, blocks, pays=pays, state=state)
    blocks[7] = across_cores(packed(fourth, after=state[:1]))
    state = phase(sizes, [5, 6], q_rows, blocks, state=state)
    step_logits = step_shares(sizes, ends, head, pays, blocks)
    cand_out, prompt_out = phase(sizes, [3, 7], q_rows, blocks, state=state, ends=ends)
    tp_size = lax.axis_size("tp")
    for bit in high_bits(tp_size, 1):
        step_logits = step_logits + flipped(step_logits, "tp", tp_size, bit)
    return (prompt_out, cand_out[None], step_logits)


def solution(mesh):
    placed = (
        P(("ctx", "cand"), "tp"),
        P(None, ("ctx", "cand"), "tp"),
        P("cand", "ctx", "tp"),
        P(None, "cand", "ctx", "tp"),
        P("cand"),
        P("cand", None),
        P("tp"),
    )
    return jax.shard_map(
        functools.partial(per_device, mesh.shape["ctx"], mesh.shape["cand"]),
        mesh=mesh,
        in_specs=placed,
        out_specs=(P(("ctx", "cand"), "tp"), P("cand", "ctx", "tp"), P("cand", None)),
        check_vma=False,
    )
```

```python
import functools
import math

import jax
import jax.numpy as jnp
from jax import lax
from jax.experimental import pallas as pl
from jax.experimental.pallas import tpu as pltpu
from jax.sharding import PartitionSpec as P

HEADDIM = 128
GROUP = 8
SUBLANES = 8
NEG_FILL = -1e30
SCALE = HEADDIM ** -0.5 * math.log2(math.e)
ROW_TILE = 256
VMEM_LIMIT = 28 * 1024 * 1024
PARAMS = pltpu.CompilerParams(vmem_limit_bytes=VMEM_LIMIT)
PROMPT_AXES = ("ctx", "cand")


def vmem(count):
    return [pl.BlockSpec(memory_space=pltpu.VMEM)] * count


def like(array):
    return jax.ShapeDtypeStruct(array.shape, array.dtype)


def high_bits(size, lowest):
    return [1 << b for b in reversed(range(size.bit_length() - 1)) if 1 << b >= lowest]


def flipped(block, axes, size, bit):
    return lax.ppermute(block, axes, [(i, i ^ bit) for i in range(size)])


def pack_kernel(count, *refs):
    sources, out_ref = refs[:count], refs[-1]
    start = 0
    for ref in sources:
        out_ref[start : start + ref.shape[0]] = ref[...]
        start += ref.shape[0]


def packed(*arrays, after=()):
    count = sum(a.shape[0] for a in arrays)
    return pl.pallas_call(
        functools.partial(pack_kernel, len(arrays)),
        out_shape=jax.ShapeDtypeStruct((count,) + arrays[0].shape[1:], arrays[0].dtype),
        in_specs=vmem(len(arrays)) + [pl.BlockSpec(memory_space=pl.ANY)] * len(after),
        out_specs=vmem(1)[0],
        compiler_params=PARAMS,
        name="pack_blocks",
    )(*arrays, *after)


def prompt_bits(ctx_size, cand_size):
    core, along, across = cand_size, 1, 2 * cand_size
    early = high_bits(cand_size, 2) + [bit * cand_size for bit in high_bits(ctx_size, 4)]
    return early, along, across, core


def prompt_owners(ctx_size, cand_size):
    early, along, across, core = prompt_bits(ctx_size, cand_size)
    place = lax.axis_index("ctx") * cand_size + lax.axis_index("cand")
    odd = lax.rem(lax.axis_index("ctx"), 2)
    near = along + odd * (across - along)
    far = along + across - near
    masks = [0]
    for bit in early:
        masks += [mask ^ bit for mask in masks]
    shifts = [0, near, far, along + across, core, core + far, core + near, core + along + across]
    return [[place ^ mask ^ shift for mask in masks] for shift in shifts]


def gather_cand(own, ctx_size):
    blocks = [(own, 0), (flipped(own, "ctx", ctx_size, 1), 1)]
    for bit in reversed(high_bits(ctx_size, 2)):
        rail = [(flipped(b, "ctx", ctx_size, bit), mask | bit) for b, mask in blocks if not mask & 1]
        blocks += rail + [(flipped(b, "ctx", ctx_size, 1), mask | 1) for b, mask in rail]
    return blocks


def stage_kernel(prompt_q, cand_q, prompt_kv, cand_kv, ends, head, *refs):
    q_out, cand_out, own_out, pay_out, ends_out, head_out, sems = refs
    steps = ends.shape[1]
    pairs = [
        (cand_q, cand_out),
        (ends, ends_out),
        (prompt_kv, own_out),
        (cand_kv, pay_out.at[0:2]),
        (prompt_q, q_out),
        (head, head_out),
    ]
    copies = [pltpu.make_async_copy(a, b, sems.at[i]) for i, (a, b) in enumerate(pairs)]
    for copy in copies:
        copy.start()
    copies[0].wait()
    copies[1].wait()
    rows = cand_out.shape[0]
    ends_column = column_of(ends_out[...])
    row_pos = lax.axis_index("ctx") * rows + lax.broadcasted_iota(jnp.int32, (steps, rows), 1)
    chosen = (row_pos == ends_column).astype(jnp.bfloat16)
    picked = jnp.dot(chosen, cand_out[...], preferred_element_type=jnp.float32)
    width = pay_out.shape[2]
    pieces = [picked[:, at : at + width] for at in range(0, picked.shape[1], width)]
    pay_out[2] = jnp.concatenate(pieces, axis=0).astype(jnp.bfloat16)
    for copy in copies[2:]:
        copy.wait()


def column_of(row):
    count = row.shape[1]
    down = lax.broadcasted_iota(jnp.int32, (count, count), 0)
    right = lax.broadcasted_iota(jnp.int32, (count, count), 1)
    return jnp.sum(jnp.where(down == right, row, 0), axis=1, keepdims=True)


def length_of(ends):
    return ends[:, ends.shape[1] - 1 :] + 1


def staged(prompt_q, cand_q, prompt_kv, cand_kv, ends, head):
    arrays = (prompt_q, cand_q, prompt_kv, cand_kv, ends, head)
    pay = jax.ShapeDtypeStruct((3,) + cand_kv.shape[1:], cand_kv.dtype)
    return pl.pallas_call(
        stage_kernel,
        out_shape=(like(prompt_q), like(cand_q), like(prompt_kv), pay, like(ends), like(head)),
        in_specs=[pl.BlockSpec(memory_space=pltpu.HBM)] * len(arrays),
        out_specs=tuple(vmem(6)),
        scratch_shapes=[pltpu.SemaphoreType.DMA((len(arrays),))],
        compiler_params=PARAMS,
        name="stage_operands",
    )(*(pltpu.with_memory_space_constraint(a, pltpu.HBM) for a in arrays))


def tiles(q_ref, head):
    rows = q_ref.shape[0]
    fan = max(1, ROW_TILE // rows)
    for start in range(head * GROUP, (head + 1) * GROUP, fan):
        heads = range(start, start + fan)
        queries = jnp.concatenate([q_ref[:, h * HEADDIM : (h + 1) * HEADDIM] for h in heads], axis=0)
        yield heads, slice(start * rows, (start + fan) * rows), queries


def stacked_rows(first_row, rows, count):
    return first_row + lax.rem(lax.broadcasted_iota(jnp.int32, (count, 1), 0), jnp.int32(rows))


def product(queries, key_rows):
    return lax.dot_general(
        queries, key_rows, (((1,), (1,)), ((), ())), preferred_element_type=jnp.float32
    )


def with_ones(value_rows):
    return jnp.concatenate([value_rows, jnp.ones_like(value_rows)], axis=1)


def head_rows(blocks, which, head):
    columns = slice(head * HEADDIM, (head + 1) * HEADDIM)
    return jnp.concatenate([ref[lead + (which,)][:, columns] for ref, lead in blocks], axis=0)


def key_positions(owners, rows):
    lane = lax.broadcasted_iota(jnp.int32, (1, len(owners) * rows), 1)
    positions = lane
    for index, owner in enumerate(owners):
        inside = (lane >= index * rows) & (lane < (index + 1) * rows)
        positions = jnp.where(inside, lane + (owner - index) * rows, positions)
    return positions


def spread(column, count):
    return jnp.concatenate([column] * (count // column.shape[1]), axis=1)


def absorb(queries, key_rows, widened, allowed, old):
    scores = product(queries, key_rows)
    if allowed is not None:
        scores = jnp.where(allowed, scores, NEG_FILL)
    count = scores.shape[1]
    peak = jnp.broadcast_to(jnp.max(scores, axis=1, keepdims=True), (scores.shape[0], HEADDIM))
    if old is not None:
        peak = jnp.maximum(peak, old[0])
    weights = jnp.exp2((scores - spread(peak, count)) * SCALE).astype(jnp.bfloat16)
    blended = jnp.dot(weights, widened, preferred_element_type=jnp.float32)
    if old is not None:
        blended += old[1] * spread(jnp.exp2((old[0] - peak) * SCALE), old[1].shape[1])
    return peak, blended


def prompt_place(cand_size):
    return lax.axis_index("ctx") * cand_size + lax.axis_index("cand")


def pairs_of(refs):
    return [(ref, (index,)) for ref in refs for index in range(ref.shape[0])]


def phase_kernel(sizes, arrays, masks, first, last, *refs):
    ctx_size, cand_size = sizes
    take = iter(refs)
    prompt_q, cand_q = next(take), next(take)
    block_refs = [next(take) for _ in arrays]
    pays = [next(take) for _ in masks]
    ends = next(take) if last else None
    old = None if first else [(next(take), next(take)) for _ in range(2)]
    outs = refs[-6:-4] if last else refs[-4:]
    halls, sems = refs[-4:-2], refs[-2:]
    leaving = []
    rows = prompt_q.shape[0]
    cand_rows = cand_q.shape[0]
    owners = prompt_owners(ctx_size, cand_size)
    key_pos = key_positions([place for index in arrays for place in owners[index]], rows)
    blocks = pairs_of(block_refs)
    own = [(ref, ()) for ref in pays]
    ctx = lax.axis_index("ctx")
    own_pos = key_positions([ctx ^ mask for mask in masks], cand_rows) if masks else None
    alive = stacked_rows(ctx * cand_rows, cand_rows, cand_rows) < length_of(ends[...]) if last else None

    for head in range(block_refs[0].shape[3] // HEADDIM):
        key_rows = head_rows(blocks, 0, head)
        widened = with_ones(head_rows(blocks, 1, head))
        if masks:
            all_keys = jnp.concatenate([key_rows, head_rows(own, 0, head)], axis=0)
            all_widened = jnp.concatenate([widened, with_ones(head_rows(own, 1, head))], axis=0)
            free = jnp.full((1, key_rows.shape[0]), -1, jnp.int32)
            all_pos = jnp.concatenate([free, own_pos], axis=1)
        for kind, q_ref in enumerate((cand_q, prompt_q)):
            for heads, at, queries in tiles(q_ref, head):
                count = queries.shape[0]
                state = None if first else (old[kind][0][at], old[kind][1][at])
                if kind == 1:
                    first_row = prompt_place(cand_size) * rows
                    allowed = key_pos <= stacked_rows(first_row, rows, count)
                    state = absorb(queries, key_rows, widened, allowed, state)
                elif masks:
                    allowed = all_pos <= stacked_rows(ctx * cand_rows, cand_rows, count)
                    state = absorb(queries, all_keys, all_widened, allowed, state)
                else:
                    state = absorb(queries, key_rows, widened, None, state)
                if not last:
                    outs[2 * kind][at] = state[0]
                    outs[2 * kind + 1][at] = state[1]
                    continue
                sums = state[1][:, HEADDIM:]
                inverse = pl.reciprocal(sums, approx=True)
                result = state[1][:, :HEADDIM] * (inverse * (2.0 - sums * inverse))
                each = q_ref.shape[0]
                for index, h in enumerate(heads):
                    kept = result[index * each : (index + 1) * each]
                    if kind == 0:
                        kept = jnp.where(alive, kept, 0.0)
                    halls[kind][:, h * HEADDIM : (h + 1) * HEADDIM] = kept.astype(jnp.bfloat16)
                part = slice(heads[0] * HEADDIM, (heads[-1] + 1) * HEADDIM)
                leaving.append(
                    pltpu.make_async_copy(
                        halls[kind].at[:, part],
                        outs[kind].at[:, part],
                        sems[kind].at[heads[0] // len(heads)],
                    )
                )
                leaving[-1].start()
    for copy in leaving:
        copy.wait()


def phase(sizes, arrays, q_rows, blocks, pays=(), state=None, ends=None, after=()):
    prompt_q, cand_q = q_rows
    first, last = state is None, ends is not None
    operands = [prompt_q, cand_q] + [blocks[index] for index in arrays]
    operands += [b for b, _ in pays]
    if last:
        operands.append(ends)
    if not first:
        operands += state
    heads = prompt_q.shape[1] // HEADDIM
    scratch = []
    if last:
        shapes = [like(cand_q), like(prompt_q)]
        scratch = [pltpu.VMEM(q.shape, q.dtype) for q in (cand_q, prompt_q)]
        scratch += [pltpu.SemaphoreType.DMA((heads,))] * 2
    else:
        shapes = []
        for q in (cand_q, prompt_q):
            count = heads * q.shape[0]
            shapes.append(jax.ShapeDtypeStruct((count, HEADDIM), jnp.float32))
            shapes.append(jax.ShapeDtypeStruct((count, 2 * HEADDIM), jnp.float32))
    key_count = sum(blocks[i].shape[0] * blocks[i].shape[2] for i in arrays)
    scores = heads * (prompt_q.shape[0] + cand_q.shape[0]) * key_count
    masks = [mask for _, mask in pays]
    return pl.pallas_call(
        functools.partial(phase_kernel, sizes, arrays, masks, first, last),
        out_shape=tuple(shapes),
        in_specs=vmem(len(operands)) + [pl.BlockSpec(memory_space=pl.ANY)] * len(after),
        out_specs=(pl.BlockSpec(memory_space=pl.ANY),) * 2 if last else tuple(vmem(len(shapes))),
        scratch_shapes=scratch,
        compiler_params=PARAMS,
        cost_estimate=pl.CostEstimate(
            flops=6 * scores * HEADDIM, bytes_accessed=scores, transcendentals=scores
        ),
        name="attend_" + "_".join(str(i) for i in arrays),
    )(*operands, *after)


def step_kernel(sizes, masks, ends_ref, head_ref, *refs):
    ctx_size, cand_size = sizes
    pays, blocks = refs[: len(masks)], refs[len(masks) : -2]
    logit_ref, kv_ref = refs[-2:]
    rows = blocks[0].shape[2]
    own_rows = pays[0].shape[1]
    free = rows * ctx_size * cand_size
    place = lax.axis_index("ctx")
    for ref, owners in zip(blocks, prompt_owners(ctx_size, cand_size)):
        for index, owner in enumerate(owners):
            at = pl.ds(pl.multiple_of(owner * rows, rows), rows)
            kv_ref[0, at, :] = ref[index, 0]
            kv_ref[1, at, :] = ref[index, 1]
    picked = jnp.zeros(pays[0].shape[1:], jnp.float32)
    for ref, mask in zip(pays, masks):
        at = pl.ds(pl.multiple_of(free + (place ^ mask) * own_rows, own_rows), own_rows)
        kv_ref[0, at, :] = ref[0]
        kv_ref[1, at, :] = ref[1]
        picked += ref[2].astype(jnp.float32)
    steps = ends_ref.shape[1]
    width = picked.shape[1]
    step_rows = [picked[at : at + steps] for at in range(0, steps * head_ref.shape[1] // width, steps)]

    ends = column_of(ends_ref[...])
    alive = ends < length_of(ends_ref[...])
    kinds = width // HEADDIM
    stacked = GROUP * steps
    parts = []
    for head in range(kinds):
        places = [divmod(h * HEADDIM, width) for h in range(head * GROUP, (head + 1) * GROUP)]
        part = jnp.concatenate([step_rows[a][:, b : b + HEADDIM] for a, b in places], axis=0)
        sides = [part if other == head else jnp.zeros_like(part) for other in range(kinds)]
        parts.append(jnp.concatenate(sides, axis=1))
    queries = jnp.concatenate(parts, axis=0).astype(jnp.bfloat16)
    own_pos = lax.broadcasted_iota(jnp.int32, (1, own_rows * len(masks)), 1)
    row_pos = jnp.concatenate([ends] * (GROUP * kinds), axis=0)
    scores = product(queries, kv_ref[0])
    bound = jnp.where(own_pos <= row_pos, scores[:, free:], NEG_FILL)
    scores = jnp.concatenate([scores[:, :free], bound], axis=1)
    peak = jnp.max(scores, axis=1, keepdims=True)
    weights = jnp.exp2((scores - peak) * SCALE).astype(jnp.bfloat16)
    value_rows = kv_ref[1]
    widened = jnp.concatenate([value_rows, jnp.ones_like(value_rows[:, :HEADDIM])], axis=1)
    blended = jnp.dot(weights, widened, preferred_element_type=jnp.float32)
    total = jnp.zeros((steps, HEADDIM), jnp.float32)
    for head in range(kinds):
        mixed = blended[head * stacked : (head + 1) * stacked]
        result = mixed[:, head * HEADDIM : (head + 1) * HEADDIM] / mixed[:, width:]
        for index in range(GROUP):
            kept = jnp.where(alive, result[index * steps : (index + 1) * steps], 0.0)
            kept = kept.astype(jnp.bfloat16).astype(jnp.float32)
            h = head * GROUP + index
            total += kept * head_ref[:, h * HEADDIM : (h + 1) * HEADDIM]
    logits = jnp.sum(total, axis=1, keepdims=True)
    down = lax.broadcasted_iota(jnp.int32, (steps, steps), 0)
    right = lax.broadcasted_iota(jnp.int32, (steps, steps), 1)
    logit_ref[...] = jnp.sum(jnp.where(down == right, logits, 0.0), axis=0, keepdims=True)


def step_shares(sizes, ends, head, pays, blocks):
    ctx_size, cand_size = sizes
    rows, width = blocks[0].shape[2:]
    count = rows * ctx_size * cand_size + pays[0][0].shape[1] * ctx_size
    scores = ends.shape[1] * head.shape[1] // HEADDIM * count
    return pl.pallas_call(
        functools.partial(step_kernel, sizes, [mask for _, mask in pays]),
        out_shape=jax.ShapeDtypeStruct(ends.shape, jnp.float32),
        in_specs=vmem(2 + len(pays) + len(blocks)),
        out_specs=vmem(1)[0],
        scratch_shapes=[pltpu.VMEM((2, count, width), blocks[0].dtype)],
        compiler_params=PARAMS,
        cost_estimate=pl.CostEstimate(
            flops=6 * scores * HEADDIM, bytes_accessed=scores, transcendentals=scores
        ),
        name="step_logits",
    )(ends, head, *(b for b, _ in pays), *blocks)


def per_device(ctx_size, cand_size, prompt_q, prompt_kv, cand_q, cand_kv, cand_lengths, step_ends, reward_head):
    sizes = ctx_size, cand_size
    size = ctx_size * cand_size
    prompt_rows, cand_rows, own, payload, ends, head = staged(
        prompt_q, cand_q[0], prompt_kv, cand_kv[:, 0], step_ends, reward_head[None]
    )
    q_rows = prompt_rows, cand_rows
    pays = gather_cand(payload, ctx_size)
    early, along, across, core = prompt_bits(ctx_size, cand_size)

    def across_cores(block):
        return flipped(block, PROMPT_AXES, size, core)

    def shared_out(block, even, odd):
        return lax.ppermute(
            block, PROMPT_AXES, [(i, i ^ (odd if i & core else even)) for i in range(size)]
        )

    held = own[None]
    sent = prompt_kv[None]
    for bit in early:
        held = packed(held, flipped(sent, PROMPT_AXES, size, bit))
        sent = held
    second = shared_out(held, along, across)
    third = shared_out(held, across, along)
    blocks = [held, second, third, None, across_cores(held), None, None, None]
    state = phase(sizes, [0, 4], q_rows, blocks)
    fourth = shared_out(packed(second, after=state[:1] + tuple(b for b, _ in pays[1:4])), across, along)
    blocks[3] = fourth
    blocks[5:7] = across_cores(second), across_cores(third)
    state = phase(sizes, [1, 2], q_rows, blocks, pays=pays, state=state)
    blocks[7] = across_cores(packed(fourth, after=state[:1]))
    state = phase(sizes, [5, 6], q_rows, blocks, state=state)
    step_logits = step_shares(sizes, ends, head, pays, blocks)
    cand_out, prompt_out = phase(sizes, [3, 7], q_rows, blocks, state=state, ends=ends)
    tp_size = lax.axis_size("tp")
    for bit in high_bits(tp_size, 1):
        step_logits = step_logits + flipped(step_logits, "tp", tp_size, bit)
    return (prompt_out, cand_out[None], step_logits)


def solution(mesh):
    placed = (
        P(("ctx", "cand"), "tp"),
        P(None, ("ctx", "cand"), "tp"),
        P("cand", "ctx", "tp"),
        P(None, "cand", "ctx", "tp"),
        P("cand"),
        P("cand", None),
        P("tp"),
    )
    return jax.shard_map(
        functools.partial(per_device, mesh.shape["ctx"], mesh.shape["cand"]),
        mesh=mesh,
        in_specs=placed,
        out_specs=(P(("ctx", "cand"), "tp"), P("cand", "ctx", "tp"), P("cand", None)),
        check_vma=False,
    )
```

```python
import functools
import math

import jax
import jax.numpy as jnp
from jax import lax
from jax.experimental import pallas as pl
from jax.experimental.pallas import tpu as pltpu
from jax.sharding import PartitionSpec as P

HEADDIM = 128
GROUP = 8
SUBLANES = 8
NEG_FILL = -1e30
SCALE = HEADDIM ** -0.5 * math.log2(math.e)
ROW_TILE = 256
VMEM_LIMIT = 28 * 1024 * 1024
PARAMS = pltpu.CompilerParams(vmem_limit_bytes=VMEM_LIMIT)
PROMPT_AXES = ("ctx", "cand")


def vmem(count):
    return [pl.BlockSpec(memory_space=pltpu.VMEM)] * count


def like(array):
    return jax.ShapeDtypeStruct(array.shape, array.dtype)


def high_bits(size, lowest):
    return [1 << b for b in reversed(range(size.bit_length() - 1)) if 1 << b >= lowest]


def flipped(block, axes, size, bit):
    return lax.ppermute(block, axes, [(i, i ^ bit) for i in range(size)])


def pack_kernel(count, *refs):
    sources, out_ref = refs[:count], refs[-1]
    start = 0
    for ref in sources:
        out_ref[start : start + ref.shape[0]] = ref[...]
        start += ref.shape[0]


def packed(*arrays, after=()):
    count = sum(a.shape[0] for a in arrays)
    return pl.pallas_call(
        functools.partial(pack_kernel, len(arrays)),
        out_shape=jax.ShapeDtypeStruct((count,) + arrays[0].shape[1:], arrays[0].dtype),
        in_specs=vmem(len(arrays)) + [pl.BlockSpec(memory_space=pl.ANY)] * len(after),
        out_specs=vmem(1)[0],
        compiler_params=PARAMS,
        name="pack_blocks",
    )(*arrays, *after)


def prompt_bits(ctx_size, cand_size):
    core, along, across = cand_size, 1, 2 * cand_size
    early = high_bits(cand_size, 2) + [bit * cand_size for bit in high_bits(ctx_size, 4)]
    return early, along, across, core


def prompt_owners(ctx_size, cand_size):
    early, along, across, core = prompt_bits(ctx_size, cand_size)
    place = lax.axis_index("ctx") * cand_size + lax.axis_index("cand")
    odd = lax.rem(lax.axis_index("ctx"), 2)
    near = along + odd * (across - along)
    far = along + across - near
    masks = [0]
    for bit in early:
        masks += [mask ^ bit for mask in masks]
    shifts = [0, near, far, along + across, core, core + far, core + near, core + along + across]
    return [[place ^ mask ^ shift for mask in masks] for shift in shifts]


def gather_cand(own, ctx_size):
    blocks = [(own, 0), (flipped(own, "ctx", ctx_size, 1), 1)]
    for bit in reversed(high_bits(ctx_size, 2)):
        rail = [(flipped(b, "ctx", ctx_size, bit), mask | bit) for b, mask in blocks if not mask & 1]
        blocks += rail + [(flipped(b, "ctx", ctx_size, 1), mask | 1) for b, mask in rail]
    return blocks


def stage_kernel(prompt_q, cand_q, prompt_kv, cand_kv, ends, head, *refs):
    q_out, cand_out, own_out, pay_out, ends_out, head_out, sems = refs
    steps = ends.shape[1]
    pairs = [
        (cand_q, cand_out),
        (ends, ends_out),
        (prompt_kv, own_out),
        (cand_kv, pay_out.at[0:2]),
        (prompt_q, q_out),
        (head, head_out),
    ]
    copies = [pltpu.make_async_copy(a, b, sems.at[i]) for i, (a, b) in enumerate(pairs)]
    for copy in copies:
        copy.start()
    copies[0].wait()
    copies[1].wait()
    rows = cand_out.shape[0]
    ends_column = column_of(ends_out[...])
    row_pos = lax.axis_index("ctx") * rows + lax.broadcasted_iota(jnp.int32, (steps, rows), 1)
    chosen = (row_pos == ends_column).astype(jnp.bfloat16)
    picked = jnp.dot(chosen, cand_out[...], preferred_element_type=jnp.float32)
    width = pay_out.shape[2]
    pieces = [picked[:, at : at + width] for at in range(0, picked.shape[1], width)]
    pay_out[2] = jnp.concatenate(pieces, axis=0).astype(jnp.bfloat16)
    for copy in copies[2:]:
        copy.wait()


def column_of(row):
    count = row.shape[1]
    down = lax.broadcasted_iota(jnp.int32, (count, count), 0)
    right = lax.broadcasted_iota(jnp.int32, (count, count), 1)
    return jnp.sum(jnp.where(down == right, row, 0), axis=1, keepdims=True)


def length_of(ends):
    return ends[:, ends.shape[1] - 1 :] + 1


def staged(prompt_q, cand_q, prompt_kv, cand_kv, ends, head):
    arrays = (prompt_q, cand_q, prompt_kv, cand_kv, ends, head)
    pay = jax.ShapeDtypeStruct((3,) + cand_kv.shape[1:], cand_kv.dtype)
    return pl.pallas_call(
        stage_kernel,
        out_shape=(like(prompt_q), like(cand_q), like(prompt_kv), pay, like(ends), like(head)),
        in_specs=[pl.BlockSpec(memory_space=pltpu.HBM)] * len(arrays),
        out_specs=tuple(vmem(6)),
        scratch_shapes=[pltpu.SemaphoreType.DMA((len(arrays),))],
        compiler_params=PARAMS,
        name="stage_operands",
    )(*(pltpu.with_memory_space_constraint(a, pltpu.HBM) for a in arrays))


def tiles(q_ref, head):
    rows = q_ref.shape[0]
    fan = max(1, ROW_TILE // rows)
    for start in range(head * GROUP, (head + 1) * GROUP, fan):
        heads = range(start, start + fan)
        queries = jnp.concatenate([q_ref[:, h * HEADDIM : (h + 1) * HEADDIM] for h in heads], axis=0)
        yield heads, slice(start * rows, (start + fan) * rows), queries


def stacked_rows(first_row, rows, count):
    return first_row + lax.rem(lax.broadcasted_iota(jnp.int32, (count, 1), 0), jnp.int32(rows))


def product(queries, key_rows):
    return lax.dot_general(
        queries, key_rows, (((1,), (1,)), ((), ())), preferred_element_type=jnp.float32
    )


def with_ones(value_rows):
    return jnp.concatenate([value_rows, jnp.ones_like(value_rows)], axis=1)


def head_rows(blocks, which, head):
    columns = slice(head * HEADDIM, (head + 1) * HEADDIM)
    return jnp.concatenate([ref[lead + (which,)][:, columns] for ref, lead in blocks], axis=0)


def key_positions(owners, rows):
    lane = lax.broadcasted_iota(jnp.int32, (1, len(owners) * rows), 1)
    positions = lane
    for index, owner in enumerate(owners):
        inside = (lane >= index * rows) & (lane < (index + 1) * rows)
        positions = jnp.where(inside, lane + (owner - index) * rows, positions)
    return positions


def spread(column, count):
    return jnp.concatenate([column] * (count // column.shape[1]), axis=1)


def absorb(queries, key_rows, widened, allowed, old):
    scores = product(queries, key_rows)
    if allowed is not None:
        scores = jnp.where(allowed, scores, NEG_FILL)
    count = scores.shape[1]
    peak = jnp.broadcast_to(jnp.max(scores, axis=1, keepdims=True), (scores.shape[0], HEADDIM))
    if old is not None:
        peak = jnp.maximum(peak, old[0])
    weights = jnp.exp2((scores - spread(peak, count)) * SCALE).astype(jnp.bfloat16)
    blended = jnp.dot(weights, widened, preferred_element_type=jnp.float32)
    if old is not None:
        blended += old[1] * spread(jnp.exp2((old[0] - peak) * SCALE), old[1].shape[1])
    return peak, blended


def prompt_place(cand_size):
    return lax.axis_index("ctx") * cand_size + lax.axis_index("cand")


def pairs_of(refs):
    return [(ref, (index,)) for ref in refs for index in range(ref.shape[0])]


def phase_kernel(sizes, arrays, masks, first, last, *refs):
    ctx_size, cand_size = sizes
    take = iter(refs)
    prompt_q, cand_q = next(take), next(take)
    block_refs = [next(take) for _ in arrays]
    pays = [next(take) for _ in masks]
    ends = next(take) if last else None
    old = None if first else [(next(take), next(take)) for _ in range(2)]
    outs = refs[-2:] if last else refs[-4:]
    rows = prompt_q.shape[0]
    cand_rows = cand_q.shape[0]
    owners = prompt_owners(ctx_size, cand_size)
    key_pos = key_positions([place for index in arrays for place in owners[index]], rows)
    blocks = pairs_of(block_refs)
    own = [(ref, ()) for ref in pays]
    ctx = lax.axis_index("ctx")
    own_pos = key_positions([ctx ^ mask for mask in masks], cand_rows) if masks else None
    alive = stacked_rows(ctx * cand_rows, cand_rows, cand_rows) < length_of(ends[...]) if last else None

    for head in range(block_refs[0].shape[3] // HEADDIM):
        key_rows = head_rows(blocks, 0, head)
        widened = with_ones(head_rows(blocks, 1, head))
        if masks:
            all_keys = jnp.concatenate([key_rows, head_rows(own, 0, head)], axis=0)
            all_widened = jnp.concatenate([widened, with_ones(head_rows(own, 1, head))], axis=0)
            free = jnp.full((1, key_rows.shape[0]), -1, jnp.int32)
            all_pos = jnp.concatenate([free, own_pos], axis=1)
        for kind, q_ref in enumerate((cand_q, prompt_q)):
            for heads, at, queries in tiles(q_ref, head):
                count = queries.shape[0]
                state = None if first else (old[kind][0][at], old[kind][1][at])
                if kind == 1:
                    first_row = prompt_place(cand_size) * rows
                    allowed = key_pos <= stacked_rows(first_row, rows, count)
                    state = absorb(queries, key_rows, widened, allowed, state)
                elif masks:
                    allowed = all_pos <= stacked_rows(ctx * cand_rows, cand_rows, count)
                    state = absorb(queries, all_keys, all_widened, allowed, state)
                else:
                    state = absorb(queries, key_rows, widened, None, state)
                if not last:
                    outs[2 * kind][at] = state[0]
                    outs[2 * kind + 1][at] = state[1]
                    continue
                sums = state[1][:, HEADDIM:]
                inverse = pl.reciprocal(sums, approx=True)
                result = state[1][:, :HEADDIM] * (inverse * (2.0 - sums * inverse))
                each = q_ref.shape[0]
                for index, h in enumerate(heads):
                    kept = result[index * each : (index + 1) * each]
                    if kind == 0:
                        kept = jnp.where(alive, kept, 0.0)
                    outs[kind][:, h * HEADDIM : (h + 1) * HEADDIM] = kept.astype(jnp.bfloat16)


def phase(sizes, arrays, q_rows, blocks, pays=(), state=None, ends=None, after=()):
    prompt_q, cand_q = q_rows
    first, last = state is None, ends is not None
    operands = [prompt_q, cand_q] + [blocks[index] for index in arrays]
    operands += [b for b, _ in pays]
    if last:
        operands.append(ends)
    if not first:
        operands += state
    heads = prompt_q.shape[1] // HEADDIM
    if last:
        shapes = [like(cand_q), like(prompt_q)]
    else:
        shapes = []
        for q in (cand_q, prompt_q):
            count = heads * q.shape[0]
            shapes.append(jax.ShapeDtypeStruct((count, HEADDIM), jnp.float32))
            shapes.append(jax.ShapeDtypeStruct((count, 2 * HEADDIM), jnp.float32))
    key_count = sum(blocks[i].shape[0] * blocks[i].shape[2] for i in arrays)
    scores = heads * (prompt_q.shape[0] + cand_q.shape[0]) * key_count
    masks = [mask for _, mask in pays]
    return pl.pallas_call(
        functools.partial(phase_kernel, sizes, arrays, masks, first, last),
        out_shape=tuple(shapes),
        in_specs=vmem(len(operands)) + [pl.BlockSpec(memory_space=pl.ANY)] * len(after),
        out_specs=tuple(vmem(len(shapes))),
        compiler_params=PARAMS,
        cost_estimate=pl.CostEstimate(
            flops=6 * scores * HEADDIM, bytes_accessed=scores, transcendentals=scores
        ),
        name="attend_" + "_".join(str(i) for i in arrays),
    )(*operands, *after)


def step_kernel(sizes, masks, ends_ref, head_ref, *refs):
    ctx_size, cand_size = sizes
    pays, blocks = refs[: len(masks)], refs[len(masks) : -2]
    logit_ref, kv_ref = refs[-2:]
    rows = blocks[0].shape[2]
    own_rows = pays[0].shape[1]
    free = rows * ctx_size * cand_size
    place = lax.axis_index("ctx")
    for ref, owners in zip(blocks, prompt_owners(ctx_size, cand_size)):
        for index, owner in enumerate(owners):
            at = pl.ds(pl.multiple_of(owner * rows, rows), rows)
            kv_ref[0, at, :] = ref[index, 0]
            kv_ref[1, at, :] = ref[index, 1]
    picked = jnp.zeros(pays[0].shape[1:], jnp.float32)
    for ref, mask in zip(pays, masks):
        at = pl.ds(pl.multiple_of(free + (place ^ mask) * own_rows, own_rows), own_rows)
        kv_ref[0, at, :] = ref[0]
        kv_ref[1, at, :] = ref[1]
        picked += ref[2].astype(jnp.float32)
    steps = ends_ref.shape[1]
    width = picked.shape[1]
    step_rows = [picked[at : at + steps] for at in range(0, steps * head_ref.shape[1] // width, steps)]

    ends = column_of(ends_ref[...])
    alive = ends < length_of(ends_ref[...])
    kinds = width // HEADDIM
    stacked = GROUP * steps
    parts = []
    for head in range(kinds):
        places = [divmod(h * HEADDIM, width) for h in range(head * GROUP, (head + 1) * GROUP)]
        part = jnp.concatenate([step_rows[a][:, b : b + HEADDIM] for a, b in places], axis=0)
        sides = [part if other == head else jnp.zeros_like(part) for other in range(kinds)]
        parts.append(jnp.concatenate(sides, axis=1))
    queries = jnp.concatenate(parts, axis=0).astype(jnp.bfloat16)
    own_pos = lax.broadcasted_iota(jnp.int32, (1, own_rows * len(masks)), 1)
    row_pos = jnp.concatenate([ends] * (GROUP * kinds), axis=0)
    scores = product(queries, kv_ref[0])
    bound = jnp.where(own_pos <= row_pos, scores[:, free:], NEG_FILL)
    scores = jnp.concatenate([scores[:, :free], bound], axis=1)
    peak = jnp.max(scores, axis=1, keepdims=True)
    weights = jnp.exp2((scores - peak) * SCALE).astype(jnp.bfloat16)
    value_rows = kv_ref[1]
    widened = jnp.concatenate([value_rows, jnp.ones_like(value_rows[:, :HEADDIM])], axis=1)
    blended = jnp.dot(weights, widened, preferred_element_type=jnp.float32)
    total = jnp.zeros((steps, HEADDIM), jnp.float32)
    for head in range(kinds):
        mixed = blended[head * stacked : (head + 1) * stacked]
        result = mixed[:, head * HEADDIM : (head + 1) * HEADDIM] / mixed[:, width:]
        for index in range(GROUP):
            kept = jnp.where(alive, result[index * steps : (index + 1) * steps], 0.0)
            kept = kept.astype(jnp.bfloat16).astype(jnp.float32)
            h = head * GROUP + index
            total += kept * head_ref[:, h * HEADDIM : (h + 1) * HEADDIM]
    logits = jnp.sum(total, axis=1, keepdims=True)
    down = lax.broadcasted_iota(jnp.int32, (steps, steps), 0)
    right = lax.broadcasted_iota(jnp.int32, (steps, steps), 1)
    logit_ref[...] = jnp.sum(jnp.where(down == right, logits, 0.0), axis=0, keepdims=True)


def step_shares(sizes, ends, head, pays, blocks):
    ctx_size, cand_size = sizes
    rows, width = blocks[0].shape[2:]
    count = rows * ctx_size * cand_size + pays[0][0].shape[1] * ctx_size
    scores = ends.shape[1] * head.shape[1] // HEADDIM * count
    return pl.pallas_call(
        functools.partial(step_kernel, sizes, [mask for _, mask in pays]),
        out_shape=jax.ShapeDtypeStruct(ends.shape, jnp.float32),
        in_specs=vmem(2 + len(pays) + len(blocks)),
        out_specs=vmem(1)[0],
        scratch_shapes=[pltpu.VMEM((2, count, width), blocks[0].dtype)],
        compiler_params=PARAMS,
        cost_estimate=pl.CostEstimate(
            flops=6 * scores * HEADDIM, bytes_accessed=scores, transcendentals=scores
        ),
        name="step_logits",
    )(ends, head, *(b for b, _ in pays), *blocks)


def per_device(ctx_size, cand_size, prompt_q, prompt_kv, cand_q, cand_kv, cand_lengths, step_ends, reward_head):
    sizes = ctx_size, cand_size
    size = ctx_size * cand_size
    prompt_rows, cand_rows, own, payload, ends, head = staged(
        prompt_q, cand_q[0], prompt_kv, cand_kv[:, 0], step_ends, reward_head[None]
    )
    q_rows = prompt_rows, cand_rows
    pays = gather_cand(payload, ctx_size)
    early, along, across, core = prompt_bits(ctx_size, cand_size)

    def across_cores(block):
        return flipped(block, PROMPT_AXES, size, core)

    def shared_out(block, even, odd):
        return lax.ppermute(
            block, PROMPT_AXES, [(i, i ^ (odd if i & core else even)) for i in range(size)]
        )

    held = own[None]
    sent = prompt_kv[None]
    for bit in early:
        held = packed(held, flipped(sent, PROMPT_AXES, size, bit))
        sent = held
    second = shared_out(held, along, across)
    third = shared_out(held, across, along)
    blocks = [held, second, third, None, across_cores(held), None, None, None]
    state = phase(sizes, [0, 4], q_rows, blocks)
    fourth = shared_out(packed(second, after=state[:1] + tuple(b for b, _ in pays[1:4])), across, along)
    blocks[3] = fourth
    blocks[5:7] = across_cores(second), across_cores(third)
    state = phase(sizes, [1, 2], q_rows, blocks, pays=pays, state=state)
    blocks[7] = across_cores(packed(fourth, after=state[:1]))
    state = phase(sizes, [5, 6], q_rows, blocks, state=state)
    step_logits = step_shares(sizes, ends, head, pays, blocks)
    cand_out, prompt_out = phase(sizes, [3, 7], q_rows, blocks, state=state, ends=ends)
    tp_size = lax.axis_size("tp")
    for bit in high_bits(tp_size, 1):
        step_logits = step_logits + flipped(step_logits, "tp", tp_size, bit)
    return (prompt_out, cand_out[None], step_logits)


def solution(mesh):
    placed = (
        P(("ctx", "cand"), "tp"),
        P(None, ("ctx", "cand"), "tp"),
        P("cand", "ctx", "tp"),
        P(None, "cand", "ctx", "tp"),
        P("cand"),
        P("cand", None),
        P("tp"),
    )
    return jax.shard_map(
        functools.partial(per_device, mesh.shape["ctx"], mesh.shape["cand"]),
        mesh=mesh,
        in_specs=placed,
        out_specs=(P(("ctx", "cand"), "tp"), P("cand", "ctx", "tp"), P("cand", None)),
        check_vma=False,
    )
```

```python
import functools
import math

import jax
import jax.numpy as jnp
from jax import lax
from jax.experimental import pallas as pl
from jax.experimental.pallas import tpu as pltpu
from jax.sharding import PartitionSpec as P

HEADDIM = 128
GROUP = 8
SUBLANES = 8
NEG_FILL = -1e30
SCALE = HEADDIM ** -0.5 * math.log2(math.e)
ROW_TILE = 512
VMEM_LIMIT = 28 * 1024 * 1024
PARAMS = pltpu.CompilerParams(vmem_limit_bytes=VMEM_LIMIT)
PROMPT_AXES = ("ctx", "cand")


def vmem(count):
    return [pl.BlockSpec(memory_space=pltpu.VMEM)] * count


def like(array):
    return jax.ShapeDtypeStruct(array.shape, array.dtype)


def high_bits(size, lowest):
    return [1 << b for b in reversed(range(size.bit_length() - 1)) if 1 << b >= lowest]


def flipped(block, axes, size, bit):
    return lax.ppermute(block, axes, [(i, i ^ bit) for i in range(size)])


def pack_kernel(count, *refs):
    sources, out_ref = refs[:count], refs[-1]
    start = 0
    for ref in sources:
        out_ref[start : start + ref.shape[0]] = ref[...]
        start += ref.shape[0]


def packed(*arrays, after=()):
    count = sum(a.shape[0] for a in arrays)
    return pl.pallas_call(
        functools.partial(pack_kernel, len(arrays)),
        out_shape=jax.ShapeDtypeStruct((count,) + arrays[0].shape[1:], arrays[0].dtype),
        in_specs=vmem(len(arrays)) + [pl.BlockSpec(memory_space=pl.ANY)] * len(after),
        out_specs=vmem(1)[0],
        compiler_params=PARAMS,
        name="pack_blocks",
    )(*arrays, *after)


def prompt_bits(ctx_size, cand_size):
    core, along, across = cand_size, 1, 2 * cand_size
    early = high_bits(cand_size, 2) + [bit * cand_size for bit in high_bits(ctx_size, 4)]
    return early, along, across, core


def prompt_owners(ctx_size, cand_size):
    early, along, across, core = prompt_bits(ctx_size, cand_size)
    place = lax.axis_index("ctx") * cand_size + lax.axis_index("cand")
    odd = lax.rem(lax.axis_index("ctx"), 2)
    near = along + odd * (across - along)
    far = along + across - near
    masks = [0]
    for bit in early:
        masks += [mask ^ bit for mask in masks]
    shifts = [0, near, far, along + across, core, core + far, core + near, core + along + across]
    return [[place ^ mask ^ shift for mask in masks] for shift in shifts]


def gather_cand(own, ctx_size):
    blocks = [(own, 0), (flipped(own, "ctx", ctx_size, 1), 1)]
    for bit in reversed(high_bits(ctx_size, 2)):
        rail = [(flipped(b, "ctx", ctx_size, bit), mask | bit) for b, mask in blocks if not mask & 1]
        blocks += rail + [(flipped(b, "ctx", ctx_size, 1), mask | 1) for b, mask in rail]
    return blocks


def stage_kernel(prompt_q, cand_q, prompt_kv, cand_kv, ends, head, *refs):
    q_out, cand_out, own_out, pay_out, ends_out, head_out, sems = refs
    steps = ends.shape[1]
    pairs = [
        (cand_q, cand_out),
        (ends, ends_out),
        (prompt_kv, own_out),
        (cand_kv, pay_out.at[0:2]),
        (prompt_q, q_out),
        (head, head_out),
    ]
    copies = [pltpu.make_async_copy(a, b, sems.at[i]) for i, (a, b) in enumerate(pairs)]
    for copy in copies:
        copy.start()
    copies[0].wait()
    copies[1].wait()
    rows = cand_out.shape[0]
    ends_column = column_of(ends_out[...])
    row_pos = lax.axis_index("ctx") * rows + lax.broadcasted_iota(jnp.int32, (steps, rows), 1)
    chosen = (row_pos == ends_column).astype(jnp.bfloat16)
    picked = jnp.dot(chosen, cand_out[...], preferred_element_type=jnp.float32)
    width = pay_out.shape[2]
    pieces = [picked[:, at : at + width] for at in range(0, picked.shape[1], width)]
    pay_out[2] = jnp.concatenate(pieces, axis=0).astype(jnp.bfloat16)
    for copy in copies[2:]:
        copy.wait()


def column_of(row):
    count = row.shape[1]
    down = lax.broadcasted_iota(jnp.int32, (count, count), 0)
    right = lax.broadcasted_iota(jnp.int32, (count, count), 1)
    return jnp.sum(jnp.where(down == right, row, 0), axis=1, keepdims=True)


def length_of(ends):
    return ends[:, ends.shape[1] - 1 :] + 1


def staged(prompt_q, cand_q, prompt_kv, cand_kv, ends, head):
    arrays = (prompt_q, cand_q, prompt_kv, cand_kv, ends, head)
    pay = jax.ShapeDtypeStruct((3,) + cand_kv.shape[1:], cand_kv.dtype)
    return pl.pallas_call(
        stage_kernel,
        out_shape=(like(prompt_q), like(cand_q), like(prompt_kv), pay, like(ends), like(head)),
        in_specs=[pl.BlockSpec(memory_space=pltpu.HBM)] * len(arrays),
        out_specs=tuple(vmem(6)),
        scratch_shapes=[pltpu.SemaphoreType.DMA((len(arrays),))],
        compiler_params=PARAMS,
        name="stage_operands",
    )(*(pltpu.with_memory_space_constraint(a, pltpu.HBM) for a in arrays))


def tiles(q_ref, head):
    rows = q_ref.shape[0]
    fan = max(1, ROW_TILE // rows)
    for start in range(head * GROUP, (head + 1) * GROUP, fan):
        heads = range(start, start + fan)
        queries = jnp.concatenate([q_ref[:, h * HEADDIM : (h + 1) * HEADDIM] for h in heads], axis=0)
        yield heads, slice(start * rows, (start + fan) * rows), queries


def stacked_rows(first_row, rows, count):
    return first_row + lax.rem(lax.broadcasted_iota(jnp.int32, (count, 1), 0), jnp.int32(rows))


def product(queries, key_rows):
    return lax.dot_general(
        queries, key_rows, (((1,), (1,)), ((), ())), preferred_element_type=jnp.float32
    )


def with_ones(value_rows):
    return jnp.concatenate([value_rows, jnp.ones_like(value_rows)], axis=1)


def head_rows(blocks, which, head):
    columns = slice(head * HEADDIM, (head + 1) * HEADDIM)
    return jnp.concatenate([ref[lead + (which,)][:, columns] for ref, lead in blocks], axis=0)


def key_positions(owners, rows):
    lane = lax.broadcasted_iota(jnp.int32, (1, len(owners) * rows), 1)
    positions = lane
    for index, owner in enumerate(owners):
        inside = (lane >= index * rows) & (lane < (index + 1) * rows)
        positions = jnp.where(inside, lane + (owner - index) * rows, positions)
    return positions


def spread(column, count):
    return jnp.concatenate([column] * (count // column.shape[1]), axis=1)


def absorb(queries, key_rows, widened, allowed, old):
    scores = product(queries, key_rows)
    if allowed is not None:
        scores = jnp.where(allowed, scores, NEG_FILL)
    count = scores.shape[1]
    peak = jnp.broadcast_to(jnp.max(scores, axis=1, keepdims=True), (scores.shape[0], HEADDIM))
    if old is not None:
        peak = jnp.maximum(peak, old[0])
    weights = jnp.exp2((scores - spread(peak, count)) * SCALE).astype(jnp.bfloat16)
    blended = jnp.dot(weights, widened, preferred_element_type=jnp.float32)
    if old is not None:
        blended += old[1] * spread(jnp.exp2((old[0] - peak) * SCALE), old[1].shape[1])
    return peak, blended


def prompt_place(cand_size):
    return lax.axis_index("ctx") * cand_size + lax.axis_index("cand")


def pairs_of(refs):
    return [(ref, (index,)) for ref in refs for index in range(ref.shape[0])]


def phase_kernel(sizes, arrays, masks, first, last, *refs):
    ctx_size, cand_size = sizes
    take = iter(refs)
    prompt_q, cand_q = next(take), next(take)
    block_refs = [next(take) for _ in arrays]
    pays = [next(take) for _ in masks]
    ends = next(take) if last else None
    old = None if first else [(next(take), next(take)) for _ in range(2)]
    outs = refs[-2:] if last else refs[-4:]
    rows = prompt_q.shape[0]
    cand_rows = cand_q.shape[0]
    owners = prompt_owners(ctx_size, cand_size)
    key_pos = key_positions([place for index in arrays for place in owners[index]], rows)
    blocks = pairs_of(block_refs)
    own = [(ref, ()) for ref in pays]
    ctx = lax.axis_index("ctx")
    own_pos = key_positions([ctx ^ mask for mask in masks], cand_rows) if masks else None
    alive = stacked_rows(ctx * cand_rows, cand_rows, cand_rows) < length_of(ends[...]) if last else None

    for head in range(block_refs[0].shape[3] // HEADDIM):
        key_rows = head_rows(blocks, 0, head)
        widened = with_ones(head_rows(blocks, 1, head))
        if masks:
            all_keys = jnp.concatenate([key_rows, head_rows(own, 0, head)], axis=0)
            all_widened = jnp.concatenate([widened, with_ones(head_rows(own, 1, head))], axis=0)
            free = jnp.full((1, key_rows.shape[0]), -1, jnp.int32)
            all_pos = jnp.concatenate([free, own_pos], axis=1)
        for kind, q_ref in enumerate((cand_q, prompt_q)):
            for heads, at, queries in tiles(q_ref, head):
                count = queries.shape[0]
                state = None if first else (old[kind][0][at], old[kind][1][at])
                if kind == 1:
                    first_row = prompt_place(cand_size) * rows
                    allowed = key_pos <= stacked_rows(first_row, rows, count)
                    state = absorb(queries, key_rows, widened, allowed, state)
                elif masks:
                    allowed = all_pos <= stacked_rows(ctx * cand_rows, cand_rows, count)
                    state = absorb(queries, all_keys, all_widened, allowed, state)
                else:
                    state = absorb(queries, key_rows, widened, None, state)
                if not last:
                    outs[2 * kind][at] = state[0]
                    outs[2 * kind + 1][at] = state[1]
                    continue
                result = state[1][:, :HEADDIM] / state[1][:, HEADDIM:]
                each = q_ref.shape[0]
                for index, h in enumerate(heads):
                    kept = result[index * each : (index + 1) * each]
                    if kind == 0:
                        kept = jnp.where(alive, kept, 0.0)
                    outs[kind][:, h * HEADDIM : (h + 1) * HEADDIM] = kept.astype(jnp.bfloat16)


def phase(sizes, arrays, q_rows, blocks, pays=(), state=None, ends=None, after=()):
    prompt_q, cand_q = q_rows
    first, last = state is None, ends is not None
    operands = [prompt_q, cand_q] + [blocks[index] for index in arrays]
    operands += [b for b, _ in pays]
    if last:
        operands.append(ends)
    if not first:
        operands += state
    heads = prompt_q.shape[1] // HEADDIM
    if last:
        shapes = [like(cand_q), like(prompt_q)]
    else:
        shapes = []
        for q in (cand_q, prompt_q):
            count = heads * q.shape[0]
            shapes.append(jax.ShapeDtypeStruct((count, HEADDIM), jnp.float32))
            shapes.append(jax.ShapeDtypeStruct((count, 2 * HEADDIM), jnp.float32))
    key_count = sum(blocks[i].shape[0] * blocks[i].shape[2] for i in arrays)
    scores = heads * (prompt_q.shape[0] + cand_q.shape[0]) * key_count
    masks = [mask for _, mask in pays]
    return pl.pallas_call(
        functools.partial(phase_kernel, sizes, arrays, masks, first, last),
        out_shape=tuple(shapes),
        in_specs=vmem(len(operands)) + [pl.BlockSpec(memory_space=pl.ANY)] * len(after),
        out_specs=tuple(vmem(len(shapes))),
        compiler_params=PARAMS,
        cost_estimate=pl.CostEstimate(
            flops=6 * scores * HEADDIM, bytes_accessed=scores, transcendentals=scores
        ),
        name="attend_" + "_".join(str(i) for i in arrays),
    )(*operands, *after)


def step_kernel(sizes, masks, ends_ref, head_ref, *refs):
    ctx_size, cand_size = sizes
    pays, blocks = refs[: len(masks)], refs[len(masks) : -2]
    logit_ref, kv_ref = refs[-2:]
    rows = blocks[0].shape[2]
    own_rows = pays[0].shape[1]
    free = rows * ctx_size * cand_size
    place = lax.axis_index("ctx")
    for ref, owners in zip(blocks, prompt_owners(ctx_size, cand_size)):
        for index, owner in enumerate(owners):
            at = pl.ds(pl.multiple_of(owner * rows, rows), rows)
            kv_ref[0, at, :] = ref[index, 0]
            kv_ref[1, at, :] = ref[index, 1]
    picked = jnp.zeros(pays[0].shape[1:], jnp.float32)
    for ref, mask in zip(pays, masks):
        at = pl.ds(pl.multiple_of(free + (place ^ mask) * own_rows, own_rows), own_rows)
        kv_ref[0, at, :] = ref[0]
        kv_ref[1, at, :] = ref[1]
        picked += ref[2].astype(jnp.float32)
    steps = ends_ref.shape[1]
    width = picked.shape[1]
    step_rows = [picked[at : at + steps] for at in range(0, steps * head_ref.shape[1] // width, steps)]

    ends = column_of(ends_ref[...])
    alive = ends < length_of(ends_ref[...])
    kinds = width // HEADDIM
    stacked = GROUP * steps
    parts = []
    for head in range(kinds):
        places = [divmod(h * HEADDIM, width) for h in range(head * GROUP, (head + 1) * GROUP)]
        part = jnp.concatenate([step_rows[a][:, b : b + HEADDIM] for a, b in places], axis=0)
        sides = [part if other == head else jnp.zeros_like(part) for other in range(kinds)]
        parts.append(jnp.concatenate(sides, axis=1))
    queries = jnp.concatenate(parts, axis=0).astype(jnp.bfloat16)
    own_pos = lax.broadcasted_iota(jnp.int32, (1, own_rows * len(masks)), 1)
    row_pos = jnp.concatenate([ends] * (GROUP * kinds), axis=0)
    scores = product(queries, kv_ref[0])
    bound = jnp.where(own_pos <= row_pos, scores[:, free:], NEG_FILL)
    scores = jnp.concatenate([scores[:, :free], bound], axis=1)
    peak = jnp.max(scores, axis=1, keepdims=True)
    weights = jnp.exp2((scores - peak) * SCALE).astype(jnp.bfloat16)
    value_rows = kv_ref[1]
    widened = jnp.concatenate([value_rows, jnp.ones_like(value_rows[:, :HEADDIM])], axis=1)
    blended = jnp.dot(weights, widened, preferred_element_type=jnp.float32)
    total = jnp.zeros((steps, HEADDIM), jnp.float32)
    for head in range(kinds):
        mixed = blended[head * stacked : (head + 1) * stacked]
        result = mixed[:, head * HEADDIM : (head + 1) * HEADDIM] / mixed[:, width:]
        for index in range(GROUP):
            kept = jnp.where(alive, result[index * steps : (index + 1) * steps], 0.0)
            kept = kept.astype(jnp.bfloat16).astype(jnp.float32)
            h = head * GROUP + index
            total += kept * head_ref[:, h * HEADDIM : (h + 1) * HEADDIM]
    logits = jnp.sum(total, axis=1, keepdims=True)
    down = lax.broadcasted_iota(jnp.int32, (steps, steps), 0)
    right = lax.broadcasted_iota(jnp.int32, (steps, steps), 1)
    logit_ref[...] = jnp.sum(jnp.where(down == right, logits, 0.0), axis=0, keepdims=True)


def step_shares(sizes, ends, head, pays, blocks):
    ctx_size, cand_size = sizes
    rows, width = blocks[0].shape[2:]
    count = rows * ctx_size * cand_size + pays[0][0].shape[1] * ctx_size
    scores = ends.shape[1] * head.shape[1] // HEADDIM * count
    return pl.pallas_call(
        functools.partial(step_kernel, sizes, [mask for _, mask in pays]),
        out_shape=jax.ShapeDtypeStruct(ends.shape, jnp.float32),
        in_specs=vmem(2 + len(pays) + len(blocks)),
        out_specs=vmem(1)[0],
        scratch_shapes=[pltpu.VMEM((2, count, width), blocks[0].dtype)],
        compiler_params=PARAMS,
        cost_estimate=pl.CostEstimate(
            flops=6 * scores * HEADDIM, bytes_accessed=scores, transcendentals=scores
        ),
        name="step_logits",
    )(ends, head, *(b for b, _ in pays), *blocks)


def per_device(ctx_size, cand_size, prompt_q, prompt_kv, cand_q, cand_kv, cand_lengths, step_ends, reward_head):
    sizes = ctx_size, cand_size
    size = ctx_size * cand_size
    prompt_rows, cand_rows, own, payload, ends, head = staged(
        prompt_q, cand_q[0], prompt_kv, cand_kv[:, 0], step_ends, reward_head[None]
    )
    q_rows = prompt_rows, cand_rows
    pays = gather_cand(payload, ctx_size)
    early, along, across, core = prompt_bits(ctx_size, cand_size)

    def across_cores(block):
        return flipped(block, PROMPT_AXES, size, core)

    def shared_out(block, even, odd):
        return lax.ppermute(
            block, PROMPT_AXES, [(i, i ^ (odd if i & core else even)) for i in range(size)]
        )

    held = own[None]
    sent = prompt_kv[None]
    for bit in early:
        held = packed(held, flipped(sent, PROMPT_AXES, size, bit))
        sent = held
    second = shared_out(held, along, across)
    third = shared_out(held, across, along)
    blocks = [held, second, third, None, across_cores(held), None, None, None]
    state = phase(sizes, [0, 4], q_rows, blocks)
    fourth = shared_out(packed(second, after=state[:1] + tuple(b for b, _ in pays[1:4])), across, along)
    blocks[3] = fourth
    blocks[5:7] = across_cores(second), across_cores(third)
    state = phase(sizes, [1, 2], q_rows, blocks, pays=pays, state=state)
    blocks[7] = across_cores(packed(fourth, after=state[:1]))
    state = phase(sizes, [5, 6], q_rows, blocks, state=state)
    step_logits = step_shares(sizes, ends, head, pays, blocks)
    cand_out, prompt_out = phase(sizes, [3, 7], q_rows, blocks, state=state, ends=ends)
    tp_size = lax.axis_size("tp")
    for bit in high_bits(tp_size, 1):
        step_logits = step_logits + flipped(step_logits, "tp", tp_size, bit)
    return (prompt_out, cand_out[None], step_logits)


def solution(mesh):
    placed = (
        P(("ctx", "cand"), "tp"),
        P(None, ("ctx", "cand"), "tp"),
        P("cand", "ctx", "tp"),
        P(None, "cand", "ctx", "tp"),
        P("cand"),
        P("cand", None),
        P("tp"),
    )
    return jax.shard_map(
        functools.partial(per_device, mesh.shape["ctx"], mesh.shape["cand"]),
        mesh=mesh,
        in_specs=placed,
        out_specs=(P(("ctx", "cand"), "tp"), P("cand", "ctx", "tp"), P("cand", None)),
        check_vma=False,
    )
```
